32 devices in a mesh: gx: 8 (over y, x, core), gy: 4 (over z).
Axes of the slice: x: 2, y: 2, z: 4, core: 2. Of those that a mesh axis runs over, the one named last changes fastest.
Arguments:
- hidden_states: bfloat16 [4, 256, 2048], P('gy', 'gx'), may hold values from -500 to 500
- norm_gain: float32 [2048], replicated, may hold values from 0.1 to 1.9
- norm_bias: float32 [2048], replicated, may hold values from -3 to 3
- query_weight: bfloat16 [2048, 2048], P('gy', 'gx'), may hold values from -0.125 to 0.125
- keyvalue_weight: bfloat16 [2048, 256], P('gy', 'gx'), may hold values from -0.125 to 0.125
- out_weight: bfloat16 [2048, 2048], P('gx', 'gy'), may hold values from -0.75 to 0.75
- key_cache: bfloat16 [4, 2304, 128], P('gy', 'gx'), may hold values from -400 to 400
- value_cache: bfloat16 [4, 2304, 128], P('gy', 'gx'), may hold values from -6 to 6
- cache_length: int32 [4], P('gy'), may hold values from 0 to 2048, as said below
Outputs:
- attention_out: bfloat16 [4, 256, 2048], P('gy', 'gx')
- new_key_cache: bfloat16 [4, 2304, 128], P('gy', 'gx')
- new_value_cache: bfloat16 [4, 2304, 128], P('gy', 'gx')
The draws below stay inside these ranges and needn't reach their ends.
Inputs may be any that keep to these rules, and one draw needn't show every extreme that they name: Request r holds cache_length[r] earlier tokens; its new tokens take positions cache_length[r] to cache_length[r] + 255. Some request holds exactly 2048.
All inputs are finite; a program needn't handle non-finite values.
Results may differ from the reference program's by a relative error of at most 0.012.
The reference program's roundings to bfloat16 on the way count: a program that leaves them out, or rounds other values in their place, can miss the bound.
Values may be sent and summed in bfloat16 or wider, within the bound.
A program may use at most 192 MiB of HBM per device.

```python
import math
import jax
import jax.numpy as jnp
from jax import lax

D = 2048
HEADS = 16
HEAD_DIM = 128
NEW_TOK = 256
CACHE_MAX = 2048
REQUESTS = 4
SEQ_CAP = 2304
PAGE = 288


def draw_hidden_states(key, part):
    key_rows, key_cols, key_base = jax.random.split(key, 3)
    full_shape = (REQUESTS, NEW_TOK, D)
    row_scale = jnp.exp(jax.random.uniform(key_rows, (REQUESTS, NEW_TOK, 1), jnp.float32, 0.0, math.log(10.0)))
    col_scale = jnp.exp(jax.random.uniform(key_cols, (1, 1, D), jnp.float32, 0.0, math.log(10.0)))
    entries = jnp.clip(jax.random.normal(key_base, full_shape, jnp.float32), -5.0, 5.0)
    return (entries * row_scale * col_scale).astype(jnp.bfloat16)


def draw_key_cache(key, part):
    key_base = jax.random.fold_in(key, 0)
    full_shape = (REQUESTS, SEQ_CAP, HEAD_DIM)
    entries = 2.0 * jnp.clip(jax.random.normal(key_base, full_shape, jnp.float32), -5.0, 5.0)
    return entries.astype(jnp.bfloat16)


def draw_cache_length(key, part):
    key_len, key_pick = jax.random.split(key, 2)
    lengths = jax.random.randint(key_len, (REQUESTS,), 0, CACHE_MAX + 1, dtype=jnp.int32)
    chosen = jax.random.randint(key_pick, (), 0, REQUESTS, dtype=jnp.int32)
    return jnp.where(jnp.arange(REQUESTS, dtype=jnp.int32) == chosen, CACHE_MAX, lengths).astype(jnp.int32)


def levels(key, shape, cuts, least, high):
    def one(axis_at, parts):
        steps = jax.random.uniform(jax.random.fold_in(jax.random.fold_in(key, 6), axis_at), (parts,), jnp.float32, least / len(cuts), high / len(cuts))
        return jnp.repeat(jnp.exp(steps), shape[axis_at] // parts).reshape((-1,) + (1,) * (len(shape) - axis_at - 1))

    factor_of = one(*cuts[0])
    for cut in cuts[1:]:
        factor_of = factor_of * one(*cut)
    return factor_of


def bell_draw(stream_key, extent, deviation, most, cuts=(), held_as=jnp.bfloat16):
    values = deviation * jax.random.normal(stream_key, extent, jnp.float32)
    if cuts:
        values = values * levels(stream_key, extent, cuts, -0.22, 0.18)
    return jnp.clip(values, -most, most).astype(held_as)


def setup_inputs(seed: int = 0) -> dict:
    splits = jax.random.split(jax.random.key(seed), 10)
    return {
        "hidden_states": draw_hidden_states(jax.random.fold_in(splits[9], 71), 0),
        "norm_gain": jnp.clip(1.0 + 0.18 * jax.random.normal(splits[1], (D,), jnp.float32), 0.1, 1.9),
        "norm_bias": bell_draw(splits[2], (D,), 0.5, 3.0, (), jnp.float32),
        "query_weight": bell_draw(splits[3], (D, HEADS * HEAD_DIM), D ** -0.5, 0.125, ((0, 4), (1, 8))),
        "keyvalue_weight": bell_draw(splits[4], (D, 2 * HEAD_DIM), D ** -0.5, 0.125, ((0, 4), (1, 8))),
        "out_weight": bell_draw(splits[5], (HEADS * HEAD_DIM, D), (HEADS * HEAD_DIM // 32) ** -0.5, 0.75, ((0, 8), (1, 4))),
        "key_cache": draw_key_cache(jax.random.fold_in(splits[9], 71), 0),
        "value_cache": bell_draw(splits[7], (REQUESTS, SEQ_CAP, HEAD_DIM), 1.0, 6.0, ((0, 4), (1, 8))),
        "cache_length": draw_cache_length(jax.random.fold_in(splits[9], 71), 0),
    }


NEGATIVE = -1e+30

def normalize(hidden_states, norm_gain, norm_bias):
    values = hidden_states.astype(jnp.float32)
    average = lax.optimization_barrier(jnp.mean(values, axis=-1, keepdims=True))
    centred = values - average
    spread = lax.optimization_barrier(jnp.mean(centred * centred, axis=-1, keepdims=True))
    return (centred * lax.rsqrt(spread + 1e-05) * norm_gain + norm_bias).astype(jnp.bfloat16)

def page_terms(query_rows, query_pos, key_rows, value_rows, first_pos, page_size):
    row_count = query_rows.shape[0]
    head_dim = key_rows.shape[1]
    page_count = key_rows.shape[0] // page_size
    scores = jnp.dot(query_rows, key_rows.T, preferred_element_type=jnp.float32)
    scores = (scores * head_dim ** (-0.5)).reshape(row_count, page_count, page_size)
    key_pos = first_pos + jnp.arange(page_count * page_size, dtype=jnp.int32).reshape(page_count, page_size)
    allowed = key_pos[None, :, :] <= query_pos[:, None, None]
    maxima = lax.optimization_barrier(jnp.max(jnp.where(allowed, scores, NEGATIVE), axis=2))
    weights = jnp.where(allowed, jnp.exp(scores - maxima[:, :, None]), 0.0)
    totals = lax.optimization_barrier(jnp.sum(weights, axis=2))
    rounded = lax.optimization_barrier(weights.astype(jnp.bfloat16))
    weighted = jnp.einsum('rnp,npd->rnd', rounded.astype(jnp.float32), value_rows.reshape(page_count, page_size, head_dim).astype(jnp.float32))
    return (maxima, totals, weighted)

def reduce_pages(maxima, totals, weighted):
    largest = lax.optimization_barrier(jnp.max(maxima, axis=1))
    factor = jnp.exp(maxima - largest[:, None])
    return (largest, lax.optimization_barrier(jnp.sum(totals * factor, axis=1)), lax.optimization_barrier(jnp.sum(weighted * factor[:, :, None], axis=1)))

def pick_rows(rows_keyvalue, indices):
    return jnp.take(rows_keyvalue, indices, axis=0)

def reference(hidden_states, norm_gain, norm_bias, query_weight, keyvalue_weight, out_weight, key_cache, value_cache, cache_length):
    normed = normalize(hidden_states, norm_gain, norm_bias).reshape(REQUESTS * NEW_TOK, D)
    queries = jnp.dot(normed, query_weight, preferred_element_type=jnp.float32).astype(jnp.bfloat16)
    queries = queries.reshape(REQUESTS, NEW_TOK, HEADS * HEAD_DIM)
    keyvalue = jnp.dot(normed, keyvalue_weight, preferred_element_type=jnp.float32).astype(jnp.bfloat16)
    keyvalue = keyvalue.reshape(REQUESTS, NEW_TOK, 2 * HEAD_DIM)
    offsets = jnp.arange(SEQ_CAP, dtype=jnp.int32)[None, :] - cache_length.astype(jnp.int32)[:, None]
    inside = (offsets >= 0) & (offsets < NEW_TOK)
    picked = jax.vmap(pick_rows)(keyvalue, jnp.clip(offsets, 0, NEW_TOK - 1).astype(jnp.int32))
    new_key_cache = jnp.where(inside[:, :, None], picked[:, :, :HEAD_DIM], key_cache)
    new_value_cache = jnp.where(inside[:, :, None], picked[:, :, HEAD_DIM:], value_cache)
    row_total = NEW_TOK * HEADS
    row_block = math.gcd(row_total, 512)

    def one_request(packed):
        query_all, key_rows, value_rows, length = packed
        rows_all = query_all.reshape(row_total // row_block, row_block, HEAD_DIM)
        row_pos = (length + jnp.arange(row_total, dtype=jnp.int32) // HEADS).reshape(row_total // row_block, row_block)

        def one_block(block_args):
            maxima, totals, weighted = page_terms(block_args[0], block_args[1], key_rows, value_rows, jnp.int32(0), PAGE)
            largest, weight_sum, summed = reduce_pages(maxima, totals, weighted)
            return summed / weight_sum[:, None]
        result = lax.map(one_block, (rows_all, row_pos))
        return result.reshape(NEW_TOK, HEADS * HEAD_DIM).astype(jnp.bfloat16)
    attended = lax.map(one_request, (queries, new_key_cache, new_value_cache, cache_length.astype(jnp.int32)))
    attention_out = jnp.dot(attended.reshape(REQUESTS * NEW_TOK, HEADS * HEAD_DIM), out_weight, preferred_element_type=jnp.float32).astype(jnp.bfloat16)
    return (attention_out.reshape(REQUESTS, NEW_TOK, D), new_key_cache, new_value_cache)
```

```python
import functools
import math

import jax
import jax.numpy as jnp
from jax import lax
from jax.experimental import pallas as pl
from jax.experimental.pallas import tpu as pltpu
from jax.sharding import PartitionSpec as P

HEADS = 16


NEGATIVE = -1e30


def normalize(hidden_states, norm_gain, norm_bias):
    values = hidden_states.astype(jnp.float32)
    average = jnp.mean(values, axis=-1, keepdims=True)
    centred = values - average
    spread = jnp.mean(centred * centred, axis=-1, keepdims=True)
    return (centred * lax.rsqrt(spread + 1e-05) * norm_gain + norm_bias).astype(jnp.bfloat16)


def page_terms(query_rows, query_pos, key_rows, value_rows, page_size):
    row_count = query_rows.shape[0]
    head_dim = key_rows.shape[1]
    page_count = key_rows.shape[0] // page_size
    scores = lax.dot_general(
        query_rows, key_rows, (((1,), (1,)), ((), ())), preferred_element_type=jnp.float32
    )
    scores = (scores * head_dim ** (-0.5)).reshape(row_count, page_count, page_size)
    key_pos = jnp.arange(page_count * page_size, dtype=jnp.int32).reshape(page_count, page_size)
    allowed = key_pos[None, :, :] <= query_pos[:, None, None]
    maxima = jnp.max(jnp.where(allowed, scores, NEGATIVE), axis=2)
    weights = jnp.where(allowed, jnp.exp(scores - maxima[:, :, None]), 0.0)
    totals = jnp.sum(weights, axis=2)
    weighted = jnp.einsum(
        "rnp,npd->rnd",
        weights.astype(jnp.bfloat16),
        value_rows.reshape(page_count, page_size, head_dim),
        preferred_element_type=jnp.float32,
    )
    return (maxima, totals, weighted)


def reduce_pages(maxima, totals, weighted):
    largest = jnp.max(maxima, axis=1)
    factor = jnp.exp(maxima - largest[:, None])
    return (
        largest,
        jnp.sum(totals * factor, axis=1),
        jnp.sum(weighted * factor[:, :, None], axis=1),
    )


def join_pages(first, second):
    larger = jnp.maximum(first[0], second[0])
    second_factor = jnp.exp(second[0] - larger)
    return (larger, second[1] * second_factor, second[2] * second_factor[:, None])


def body(
    hidden_states,
    norm_gain,
    norm_bias,
    query_weight,
    keyvalue_weight,
    out_weight,
    key_cache,
    value_cache,
    cache_length,
):
    own_tokens = hidden_states.shape[1]
    groups = lax.axis_size("gx")
    column_index = lax.axis_index("gx")
    span_len = own_tokens * groups
    page_size = key_cache.shape[1]
    head_dim = key_cache.shape[2]
    head_count = HEADS
    head_width = head_count * head_dim
    normed = normalize(hidden_states[0], norm_gain, norm_bias)
    full_rows = lax.all_gather(normed, "gx", axis=0, tiled=True)
    pieces = (
        lax.all_gather(query_weight, "gy", axis=0, tiled=True),
        lax.all_gather(keyvalue_weight, "gy", axis=0, tiled=True),
    )
    query_part = jnp.dot(full_rows, pieces[0], preferred_element_type=jnp.float32)
    keyvalue_part = jnp.dot(full_rows, pieces[1], preferred_element_type=jnp.float32)
    query_local = query_part.astype(jnp.bfloat16)
    keyvalue_local = keyvalue_part.astype(jnp.bfloat16)
    queries, new_keyvalue = (
        lax.all_gather(query_local, "gx", axis=1, tiled=True),
        lax.all_gather(keyvalue_local, "gx", axis=1, tiled=True),
    )
    length = cache_length[0]
    page_base = column_index * page_size
    offsets = page_base + jnp.arange(page_size, dtype=jnp.int32) - length
    inside = (offsets >= 0) & (offsets < span_len)
    picked = jnp.take(new_keyvalue, jnp.clip(offsets, 0, span_len - 1), axis=0)
    key_page = jnp.where(inside[:, None], picked[:, :head_dim], key_cache[0])
    value_page = jnp.where(inside[:, None], picked[:, head_dim:], value_cache[0])
    own_rows = lax.dynamic_slice_in_dim(queries, column_index * own_tokens, own_tokens, 0)
    own_rows = own_rows.reshape(own_tokens * head_count, head_dim)
    own_pos = (
        length
        + column_index * own_tokens
        + jnp.arange(own_tokens * head_count, dtype=jnp.int32) // head_count
    )
    own_total = own_tokens * head_count
    empty = (
        jnp.full((own_total,), NEGATIVE, jnp.float32),
        jnp.zeros((own_total,), jnp.float32),
        jnp.zeros((own_total, head_dim), jnp.float32),
    )
    pieces = (
        lax.all_gather(key_page, "gx", axis=0, tiled=True),
        lax.all_gather(value_page, "gx", axis=0, tiled=True),
    )
    maxima, totals, weighted = page_terms(own_rows, own_pos, pieces[0], pieces[1], page_size)
    maxima, totals, weighted = join_pages(empty, reduce_pages(maxima, totals, weighted))
    own_out = (weighted / totals[:, None]).reshape(own_tokens, head_width).astype(jnp.bfloat16)
    attended = lax.all_to_all(own_out, "gx", split_axis=1, concat_axis=0, tiled=True)
    out_full = lax.all_gather(out_weight, "gy", axis=1, tiled=True)
    hidden_part = lax.psum_scatter(
        jnp.dot(attended, out_full, preferred_element_type=jnp.float32),
        "gx",
        scatter_dimension=0,
        tiled=True,
    )
    return (hidden_part.astype(jnp.bfloat16)[None], key_page[None], value_page[None])


MESH = pl.DeviceIdType.MESH
CHIPS = 4
FLIPS = 3


def fused_kernel(
    planes,
    hidden_ref,
    gain_ref,
    bias_ref,
    wq_ref,
    wkv_ref,
    wo_ref,
    key_ref,
    value_ref,
    length_ref,
    out_ref,
    new_key_ref,
    new_value_ref,
    normed,
    wq_all,
    wkv_all,
    wo_all,
    keys,
    values,
    new_kv,
    query_rows,
    attended,
    partial,
    sibling_out,
    sibling_in,
    chip_out,
    chip_in,
    own_sum,
    load_sem,
    z_send,
    z_recv,
    rows_send,
    rows_recv,
    kv_send,
    kv_recv,
    sib_send,
    sib_recv,
    chip_send,
    chip_recv,
):
    me = lax.axis_index("gx")
    z = lax.axis_index("gy")
    core = me % 2
    chip = me // 2
    cx = chip % 2
    cy = chip // 2
    sibling = chip * 2 + 1 - core
    other_chips = (cy * 2 + 1 - cx, (1 - cy) * 2 + cx, (1 - cy) * 2 + 1 - cx)
    peers = [other * 2 + core for other in other_chips]
    far = [other * 2 + 1 - core for other in other_chips]
    everyone = [sibling] + peers + far
    has_up = z < planes - 1
    has_down = z > 0

    barrier = pltpu.get_barrier_semaphore()
    for peer in everyone:
        pl.semaphore_signal(barrier, inc=1, device_id={"gx": peer}, device_id_type=MESH)

    @pl.when(has_up)
    def _():
        pl.semaphore_signal(barrier, inc=1, device_id={"gy": z + 1}, device_id_type=MESH)

    @pl.when(has_down)
    def _():
        pl.semaphore_signal(barrier, inc=1, device_id={"gy": z - 1}, device_id_type=MESH)

    loads = [
        pltpu.make_async_copy(wq_ref, wq_all.at[z], load_sem.at[0]),
        pltpu.make_async_copy(wo_ref, wo_all.at[z], load_sem.at[1]),
        pltpu.make_async_copy(key_ref, keys.at[me], load_sem.at[2]),
        pltpu.make_async_copy(value_ref, values.at[me], load_sem.at[3]),
    ]
    for load in loads:
        load.start()

    rows = hidden_ref[...].astype(jnp.float32)
    average = jnp.mean(rows, axis=-1, keepdims=True)
    centred = rows - average
    spread = jnp.mean(centred * centred, axis=-1, keepdims=True)
    normed[me] = (
        centred * lax.rsqrt(spread + 1e-05) * gain_ref[...] + bias_ref[...]
    ).astype(jnp.bfloat16)
    wkv_all[z] = wkv_ref[...].astype(jnp.float32).T.astype(jnp.bfloat16)

    neighbours = has_up.astype(jnp.int32) + has_down.astype(jnp.int32)
    pl.semaphore_wait(barrier, len(everyone) + neighbours)

    def z_copy(kind, buffer, step, direction):
        shard = z - direction * step
        return pltpu.make_async_remote_copy(
            src_ref=buffer.at[shard],
            dst_ref=buffer.at[shard],
            send_sem=z_send.at[kind, step, (direction + 1) // 2],
            recv_sem=z_recv.at[kind, shard],
            device_id={"gy": z + direction},
            device_id_type=MESH,
        )

    def z_cond(step, direction):
        if direction > 0:
            return has_up & (z - step >= 0)
        return has_down & (z + step < planes)

    def z_start(kind, buffer, step):
        for direction in (1, -1):

            @pl.when(z_cond(step, direction))
            def _(direction=direction):
                z_copy(kind, buffer, step, direction).start()

    def z_wait_send(kind, buffer, step):
        for direction in (1, -1):

            @pl.when(z_cond(step, direction))
            def _(direction=direction):
                z_copy(kind, buffer, step, direction).wait_send()

    def z_wait_recv(kind, buffer, step):
        for direction in (1, -1):
            shard = z - direction * (step + 1)

            @pl.when((shard >= 0) & (shard < planes))
            def _(shard=shard):
                pltpu.make_async_copy(
                    buffer.at[shard], buffer.at[shard], z_recv.at[kind, shard]
                ).wait()

    gathered = (normed, keys, values)

    def row_copy(kind, block, target, slot):
        return pltpu.make_async_remote_copy(
            src_ref=gathered[kind].at[block],
            dst_ref=gathered[kind].at[block],
            send_sem=rows_send.at[kind, slot],
            recv_sem=rows_recv.at[kind, block],
            device_id={"gx": target},
            device_id_type=MESH,
        )

    def rows_start(kind):
        for slot, target in enumerate(peers + [sibling]):
            row_copy(kind, me, target, slot).start()

    def rows_wait(kind, block):
        pltpu.make_async_copy(
            gathered[kind].at[block], gathered[kind].at[block], rows_recv.at[kind, block]
        ).wait()

    def rows_forward(kind):
        for flip in range(FLIPS):
            rows_wait(kind, peers[flip])
            row_copy(kind, peers[flip], sibling, 4 + flip).start()

    def rows_finish(kind):
        for block in [sibling] + far:
            rows_wait(kind, block)

    z_start(0, wkv_all, 0)
    loads[0].wait()
    z_start(1, wq_all, 0)
    rows_start(0)
    loads[2].wait()
    rows_start(1)
    loads[3].wait()
    rows_start(2)
    loads[1].wait()

    z_wait_recv(0, wkv_all, 0)
    z_start(0, wkv_all, 1)
    z_wait_recv(0, wkv_all, 1)
    z_start(0, wkv_all, 2)
    rows_forward(0)
    z_wait_recv(1, wq_all, 0)
    z_start(1, wq_all, 1)
    rows_finish(0)
    z_wait_recv(0, wkv_all, 2)

    tokens = normed[...].reshape(-1, normed.shape[2])
    token_count = tokens.shape[0]
    depth = wq_all.shape[1]
    kv_width = wkv_all.shape[1]
    kv_part = jnp.zeros((kv_width, token_count), jnp.float32)
    for part in range(planes):
        kv_part += lax.dot_general(
            wkv_all[part],
            tokens[:, part * depth : (part + 1) * depth],
            (((1,), (1,)), ((), ())),
            preferred_element_type=jnp.float32,
        )
    new_kv[me] = kv_part.astype(jnp.bfloat16)

    def kv_copy(block, target, slot):
        return pltpu.make_async_remote_copy(
            src_ref=new_kv.at[block],
            dst_ref=new_kv.at[block],
            send_sem=kv_send.at[slot],
            recv_sem=kv_recv.at[block],
            device_id={"gx": target},
            device_id_type=MESH,
        )

    for slot, target in enumerate(everyone):
        kv_copy(me, target, slot).start()

    rows_forward(1)
    rows_forward(2)
    z_wait_recv(1, wq_all, 1)
    z_start(1, wq_all, 2)
    z_start(2, wo_all, 0)

    for block in everyone:
        pltpu.make_async_copy(new_kv.at[block], new_kv.at[block], kv_recv.at[block]).wait()

    length = length_ref[0]
    page = key_ref.shape[0]
    head_dim = key_ref.shape[1]
    kv_cols = new_kv[...].reshape(2 * head_dim, token_count)
    offsets = (
        lax.broadcasted_iota(jnp.int32, (page, token_count), 0) + me * page - length
    )
    chosen = offsets == lax.broadcasted_iota(jnp.int32, (page, token_count), 1)
    picked = lax.dot_general(
        jnp.where(chosen, 1.0, 0.0).astype(jnp.bfloat16),
        kv_cols,
        (((1,), (1,)), ((), ())),
        preferred_element_type=jnp.float32,
    )
    row_offset = lax.broadcasted_iota(jnp.int32, (page, head_dim), 0) + me * page - length
    inside = (row_offset >= 0) & (row_offset < token_count)
    new_key_ref[...] = jnp.where(
        inside, picked[:, :head_dim], keys[me].astype(jnp.float32)
    ).astype(jnp.bfloat16)
    new_value_ref[...] = jnp.where(
        inside, picked[:, head_dim:], values[me].astype(jnp.float32)
    ).astype(jnp.bfloat16)

    rows_finish(1)
    rows_finish(2)
    z_wait_recv(1, wq_all, 2)

    heads = wq_all.shape[2] // head_dim
    query = jnp.zeros((token_count, heads * head_dim), jnp.float32)
    for part in range(planes):
        query += jnp.dot(
            normed[:, :, part * depth : (part + 1) * depth].reshape(token_count, depth),
            wq_all[part],
            preferred_element_type=jnp.float32,
        )
    query = query.astype(jnp.bfloat16)
    for head in range(heads):
        query_rows[head * token_count : (head + 1) * token_count, :] = query[
            :, head * head_dim : (head + 1) * head_dim
        ]

    cached = keys.shape[0] * page - token_count
    block_rows = 128
    scale = head_dim ** (-0.5) * math.log2(math.e)

    def attend(start):
        first = pl.multiple_of(start * block_rows, block_rows)
        q = query_rows[pl.ds(first, block_rows), :]
        old_keys = keys[...].reshape(-1, head_dim)[:cached]
        old_values = values[...].reshape(-1, head_dim)[:cached]
        fresh = new_kv[...].reshape(2 * head_dim, token_count)
        old_pos = lax.broadcasted_iota(jnp.int32, (block_rows, cached), 1)
        old = lax.dot_general(
            q, old_keys, (((1,), (1,)), ((), ())), preferred_element_type=jnp.float32
        )
        old = jnp.where(old_pos < length, old * scale, NEGATIVE)
        row = lax.broadcasted_iota(jnp.int32, (block_rows, token_count), 0) + first % token_count
        col = lax.broadcasted_iota(jnp.int32, (block_rows, token_count), 1)
        new = jnp.dot(q, fresh[:head_dim], preferred_element_type=jnp.float32)
        new = jnp.where(col <= row, new * scale, NEGATIVE)
        top = jnp.maximum(
            jnp.max(old, axis=1, keepdims=True), jnp.max(new, axis=1, keepdims=True)
        )
        old = jnp.exp2(old - top)
        new = jnp.exp2(new - top)
        total = jnp.sum(old, axis=1, keepdims=True) + jnp.sum(new, axis=1, keepdims=True)
        summed = jnp.dot(
            old.astype(jnp.bfloat16), old_values, preferred_element_type=jnp.float32
        ) + lax.dot_general(
            new.astype(jnp.bfloat16),
            fresh[head_dim:],
            (((1,), (1,)), ((), ())),
            preferred_element_type=jnp.float32,
        )
        attended[pl.ds(first, block_rows), :] = (summed / total).astype(jnp.bfloat16)

    pl.loop(0, heads * token_count // block_rows)(attend)

    own_rows = hidden_ref.shape[0]
    width = wo_all.shape[2]
    result_rows = jnp.concatenate(
        [attended[head * token_count : (head + 1) * token_count, :] for head in range(heads)],
        axis=1,
    )

    def sib_copy(n):
        return pltpu.make_async_remote_copy(
            src_ref=sibling_out.at[n],
            dst_ref=sibling_in.at[n],
            send_sem=sib_send.at[n],
            recv_sem=sib_recv.at[n],
            device_id={"gx": sibling},
            device_id_type=MESH,
        )

    def chip_copy(n, flip):
        return pltpu.make_async_remote_copy(
            src_ref=chip_out.at[n, flip],
            dst_ref=chip_in.at[n, flip],
            send_sem=chip_send.at[n, flip],
            recv_sem=chip_recv.at[n, flip],
            device_id={"gx": peers[flip]},
            device_id_type=MESH,
        )

    def project(n, shard):
        partial[n] = jnp.dot(
            result_rows, wo_all[shard], preferred_element_type=jnp.float32
        ).reshape(2 * CHIPS, own_rows, width)
        for k in range(CHIPS):
            sibling_out[n, k] = partial[n, 2 * k + 1 - core].astype(jnp.bfloat16)
        sib_copy(n).start()

    def spread_sums(n):
        sib_copy(n).wait_recv()
        for flip in range(FLIPS):
            other = other_chips[flip]
            chip_out[n, flip] = (
                partial[n, 2 * other + core] + sibling_in[n, other].astype(jnp.float32)
            ).astype(jnp.bfloat16)
            chip_copy(n, flip).start()
        own_sum[n] = partial[n, me] + sibling_in[n, chip].astype(jnp.float32)

    low = z < planes // 2
    order = [z, jnp.where(low, z + 1, z - 1)]
    order.append(jnp.where(low, (z + planes - 1) % planes, (z + 1) % planes))
    order[2] = jnp.where((z == 0) | (z == planes - 1), jnp.where(low, 2, planes - 3), order[2])
    order.append(jnp.where(low, planes - 1, 0))

    project(0, order[0])
    z_wait_recv(2, wo_all, 0)
    z_start(2, wo_all, 1)
    project(1, order[1])
    spread_sums(0)
    z_wait_recv(2, wo_all, 1)
    z_start(2, wo_all, 2)
    project(2, order[2])
    spread_sums(1)
    z_wait_recv(2, wo_all, 2)
    project(3, order[3])
    spread_sums(2)
    spread_sums(3)
    for n in range(planes):
        total = own_sum[n]
        for flip in range(FLIPS):
            chip_copy(n, flip).wait_recv()
            total += chip_in[n, flip].astype(jnp.float32)
        column = pl.multiple_of(order[n] * width, width)
        out_ref[:, pl.ds(column, width)] = total.astype(jnp.bfloat16)

    for kind, buffer in enumerate((wkv_all, wq_all, wo_all)):
        for step in range(planes - 1):
            z_wait_send(kind, buffer, step)
    for kind in range(3):
        for slot, target in enumerate(peers + [sibling]):
            row_copy(kind, me, target, slot).wait_send()
        for flip in range(FLIPS):
            row_copy(kind, peers[flip], sibling, 4 + flip).wait_send()
    for slot, target in enumerate(everyone):
        kv_copy(me, target, slot).wait_send()
    for n in range(planes):
        sib_copy(n).wait_send()
        for flip in range(FLIPS):
            chip_copy(n, flip).wait_send()


def fused(
    groups,
    planes,
    hidden_states,
    norm_gain,
    norm_bias,
    query_weight,
    keyvalue_weight,
    out_weight,
    key_cache,
    value_cache,
    cache_length,
):
    own_rows, model = hidden_states.shape[1:]
    page, head_dim = key_cache.shape[1:]
    span = own_rows * groups
    depth, columns = query_weight.shape
    kv_width = keyvalue_weight.shape[1]
    out_rows, width = out_weight.shape
    heads = columns // head_dim
    bf16, f32 = jnp.bfloat16, jnp.float32
    vmem = pl.BlockSpec(memory_space=pltpu.VMEM)
    anywhere = pl.BlockSpec(memory_space=pl.ANY)
    dma = pltpu.SemaphoreType.DMA
    out, new_key, new_value = pl.pallas_call(
        functools.partial(fused_kernel, planes),
        out_shape=(
            jax.ShapeDtypeStruct((own_rows, model), bf16),
            jax.ShapeDtypeStruct((page, head_dim), bf16),
            jax.ShapeDtypeStruct((page, head_dim), bf16),
        ),
        in_specs=[
            vmem,
            vmem,
            vmem,
            anywhere,
            vmem,
            anywhere,
            anywhere,
            anywhere,
            pl.BlockSpec(memory_space=pltpu.SMEM),
        ],
        out_specs=(vmem, vmem, vmem),
        scratch_shapes=[
            pltpu.VMEM((groups, own_rows, model), bf16),
            pltpu.VMEM((planes, depth, columns), bf16),
            pltpu.VMEM((planes, kv_width, depth), bf16),
            pltpu.VMEM((planes, out_rows, width), bf16),
            pltpu.VMEM((groups, page, head_dim), bf16),
            pltpu.VMEM((groups, page, head_dim), bf16),
            pltpu.VMEM((groups, kv_width, span), bf16),
            pltpu.VMEM((heads * span, head_dim), bf16),
            pltpu.VMEM((heads * span, head_dim), bf16),
            pltpu.VMEM((planes, 2 * CHIPS, own_rows, width), f32),
            pltpu.VMEM((planes, CHIPS, own_rows, width), bf16),
            pltpu.VMEM((planes, CHIPS, own_rows, width), bf16),
            pltpu.VMEM((planes, FLIPS, own_rows, width), bf16),
            pltpu.VMEM((planes, FLIPS, own_rows, width), bf16),
            pltpu.VMEM((planes, own_rows, width), f32),
            dma((4,)),
            dma((3, planes - 1, 2)),
            dma((3, planes)),
            dma((3, 4 + FLIPS)),
            dma((3, groups)),
            dma((groups - 1,)),
            dma((groups,)),
            dma((planes,)),
            dma((planes,)),
            dma((planes, FLIPS)),
            dma((planes, FLIPS)),
        ],
        compiler_params=pltpu.CompilerParams(
            collective_id=0, has_side_effects=True, vmem_limit_bytes=48 * 1024 * 1024
        ),
        cost_estimate=pl.CostEstimate(
            flops=10**9, bytes_accessed=2 * 10**6, transcendentals=10**6
        ),
        name="attention_layer",
    )(
        hidden_states[0],
        norm_gain[None],
        norm_bias[None],
        query_weight,
        keyvalue_weight,
        out_weight,
        key_cache[0],
        value_cache[0],
        cache_length,
    )
    return out[None], new_key[None], new_value[None]


def device_program(mesh, *args):
    groups, planes = mesh.shape["gx"], mesh.shape["gy"]
    if groups == 2 * CHIPS and planes == 4:
        return fused(groups, planes, *args)
    return body(*args)


def solution(mesh):
    return jax.shard_map(
        functools.partial(device_program, mesh),
        mesh=mesh,
        in_specs=(
            P("gy", "gx", None),
            P(),
            P(),
            P("gy", "gx"),
            P("gy", "gx"),
            P("gx", "gy"),
            P("gy", "gx", None),
            P("gy", "gx", None),
            P("gy"),
        ),
        out_specs=(P("gy", "gx", None), P("gy", "gx", None), P("gy", "gx", None)),
        check_vma=False,
    )
```

```python
import functools
import math

import jax
import jax.numpy as jnp
from jax import lax
from jax.experimental import pallas as pl
from jax.experimental.pallas import tpu as pltpu
from jax.sharding import PartitionSpec as P

HEADS = 16


NEGATIVE = -1e30


def normalize(hidden_states, norm_gain, norm_bias):
    values = hidden_states.astype(jnp.float32)
    average = jnp.mean(values, axis=-1, keepdims=True)
    centred = values - average
    spread = jnp.mean(centred * centred, axis=-1, keepdims=True)
    return (centred * lax.rsqrt(spread + 1e-05) * norm_gain + norm_bias).astype(jnp.bfloat16)


def page_terms(query_rows, query_pos, key_rows, value_rows, page_size):
    row_count = query_rows.shape[0]
    head_dim = key_rows.shape[1]
    page_count = key_rows.shape[0] // page_size
    scores = lax.dot_general(
        query_rows, key_rows, (((1,), (1,)), ((), ())), preferred_element_type=jnp.float32
    )
    scores = (scores * head_dim ** (-0.5)).reshape(row_count, page_count, page_size)
    key_pos = jnp.arange(page_count * page_size, dtype=jnp.int32).reshape(page_count, page_size)
    allowed = key_pos[None, :, :] <= query_pos[:, None, None]
    maxima = jnp.max(jnp.where(allowed, scores, NEGATIVE), axis=2)
    weights = jnp.where(allowed, jnp.exp(scores - maxima[:, :, None]), 0.0)
    totals = jnp.sum(weights, axis=2)
    weighted = jnp.einsum(
        "rnp,npd->rnd",
        weights.astype(jnp.bfloat16),
        value_rows.reshape(page_count, page_size, head_dim),
        preferred_element_type=jnp.float32,
    )
    return (maxima, totals, weighted)


def reduce_pages(maxima, totals, weighted):
    largest = jnp.max(maxima, axis=1)
    factor = jnp.exp(maxima - largest[:, None])
    return (
        largest,
        jnp.sum(totals * factor, axis=1),
        jnp.sum(weighted * factor[:, :, None], axis=1),
    )


def join_pages(first, second):
    larger = jnp.maximum(first[0], second[0])
    second_factor = jnp.exp(second[0] - larger)
    return (larger, second[1] * second_factor, second[2] * second_factor[:, None])


def body(
    hidden_states,
    norm_gain,
    norm_bias,
    query_weight,
    keyvalue_weight,
    out_weight,
    key_cache,
    value_cache,
    cache_length,
):
    own_tokens = hidden_states.shape[1]
    groups = lax.axis_size("gx")
    column_index = lax.axis_index("gx")
    span_len = own_tokens * groups
    page_size = key_cache.shape[1]
    head_dim = key_cache.shape[2]
    head_count = HEADS
    head_width = head_count * head_dim
    normed = normalize(hidden_states[0], norm_gain, norm_bias)
    full_rows = lax.all_gather(normed, "gx", axis=0, tiled=True)
    pieces = (
        lax.all_gather(query_weight, "gy", axis=0, tiled=True),
        lax.all_gather(keyvalue_weight, "gy", axis=0, tiled=True),
    )
    query_part = jnp.dot(full_rows, pieces[0], preferred_element_type=jnp.float32)
    keyvalue_part = jnp.dot(full_rows, pieces[1], preferred_element_type=jnp.float32)
    query_local = query_part.astype(jnp.bfloat16)
    keyvalue_local = keyvalue_part.astype(jnp.bfloat16)
    queries, new_keyvalue = (
        lax.all_gather(query_local, "gx", axis=1, tiled=True),
        lax.all_gather(keyvalue_local, "gx", axis=1, tiled=True),
    )
    length = cache_length[0]
    page_base = column_index * page_size
    offsets = page_base + jnp.arange(page_size, dtype=jnp.int32) - length
    inside = (offsets >= 0) & (offsets < span_len)
    picked = jnp.take(new_keyvalue, jnp.clip(offsets, 0, span_len - 1), axis=0)
    key_page = jnp.where(inside[:, None], picked[:, :head_dim], key_cache[0])
    value_page = jnp.where(inside[:, None], picked[:, head_dim:], value_cache[0])
    own_rows = lax.dynamic_slice_in_dim(queries, column_index * own_tokens, own_tokens, 0)
    own_rows = own_rows.reshape(own_tokens * head_count, head_dim)
    own_pos = (
        length
        + column_index * own_tokens
        + jnp.arange(own_tokens * head_count, dtype=jnp.int32) // head_count
    )
    own_total = own_tokens * head_count
    empty = (
        jnp.full((own_total,), NEGATIVE, jnp.float32),
        jnp.zeros((own_total,), jnp.float32),
        jnp.zeros((own_total, head_dim), jnp.float32),
    )
    pieces = (
        lax.all_gather(key_page, "gx", axis=0, tiled=True),
        lax.all_gather(value_page, "gx", axis=0, tiled=True),
    )
    maxima, totals, weighted = page_terms(own_rows, own_pos, pieces[0], pieces[1], page_size)
    maxima, totals, weighted = join_pages(empty, reduce_pages(maxima, totals, weighted))
    own_out = (weighted / totals[:, None]).reshape(own_tokens, head_width).astype(jnp.bfloat16)
    attended = lax.all_to_all(own_out, "gx", split_axis=1, concat_axis=0, tiled=True)
    out_full = lax.all_gather(out_weight, "gy", axis=1, tiled=True)
    hidden_part = lax.psum_scatter(
        jnp.dot(attended, out_full, preferred_element_type=jnp.float32),
        "gx",
        scatter_dimension=0,
        tiled=True,
    )
    return (hidden_part.astype(jnp.bfloat16)[None], key_page[None], value_page[None])


MESH = pl.DeviceIdType.MESH
CHIPS = 4
FLIPS = 3


def fused_kernel(
    planes,
    hidden_ref,
    gain_ref,
    bias_ref,
    wq_ref,
    wkv_ref,
    wo_ref,
    key_ref,
    value_ref,
    length_ref,
    out_ref,
    new_key_ref,
    new_value_ref,
    hidden_in,
    gain_in,
    bias_in,
    normed,
    wq_all,
    wkv_all,
    wo_all,
    keys,
    values,
    new_kv,
    query_rows,
    attended,
    partial,
    sibling_out,
    sibling_in,
    chip_out,
    chip_in,
    own_sum,
    load_sem,
    z_send,
    z_recv,
    rows_send,
    rows_recv,
    kv_send,
    kv_recv,
    sib_send,
    sib_recv,
    chip_send,
    chip_recv,
):
    me = lax.axis_index("gx")
    z = lax.axis_index("gy")
    core = me % 2
    chip = me // 2
    cx = chip % 2
    cy = chip // 2
    sibling = chip * 2 + 1 - core
    other_chips = (cy * 2 + 1 - cx, (1 - cy) * 2 + cx, (1 - cy) * 2 + 1 - cx)
    peers = [other * 2 + core for other in other_chips]
    far = [other * 2 + 1 - core for other in other_chips]
    everyone = [sibling] + peers + far
    has_up = z < planes - 1
    has_down = z > 0

    barrier = pltpu.get_barrier_semaphore()
    for peer in everyone:
        pl.semaphore_signal(barrier, inc=1, device_id={"gx": peer}, device_id_type=MESH)

    @pl.when(has_up)
    def _():
        pl.semaphore_signal(barrier, inc=1, device_id={"gy": z + 1}, device_id_type=MESH)

    @pl.when(has_down)
    def _():
        pl.semaphore_signal(barrier, inc=1, device_id={"gy": z - 1}, device_id_type=MESH)

    half_depth = wq_all.shape[2]
    half_width = wo_all.shape[3]
    half_rows = [wq_ref.at[pl.ds(half * half_depth, half_depth)] for half in range(2)]
    half_cols = [wo_ref.at[:, pl.ds(half * half_width, half_width)] for half in range(2)]
    sources = [wkv_ref] + half_rows + half_cols
    buffers = [wkv_all, wq_all.at[0], wq_all.at[1], wo_all.at[0], wo_all.at[1]]
    loads = [
        pltpu.make_async_copy(source, target, load_sem.at[slot])
        for slot, (source, target) in enumerate(
            [
                (hidden_ref, hidden_in),
                (gain_ref, gain_in),
                (bias_ref, bias_in),
                (key_ref, keys.at[me]),
                (value_ref, values.at[me]),
            ]
            + [(source, buffer.at[z]) for source, buffer in zip(sources, buffers)]
        )
    ]
    for load in loads:
        load.start()

    neighbours = has_up.astype(jnp.int32) + has_down.astype(jnp.int32)
    pl.semaphore_wait(barrier, len(everyone) + neighbours)

    def z_copy(kind, step, direction):
        shard = z - direction * step
        buffer = buffers[kind]
        return pltpu.make_async_remote_copy(
            src_ref=sources[kind] if step == 0 else buffer.at[shard],
            dst_ref=buffer.at[shard],
            send_sem=z_send.at[kind, step, (direction + 1) // 2],
            recv_sem=z_recv.at[kind, shard],
            device_id={"gy": z + direction},
            device_id_type=MESH,
        )

    def z_cond(step, direction):
        if direction > 0:
            return has_up & (z - step >= 0)
        return has_down & (z + step < planes)

    def z_arrived(kind, shard):
        buffer = buffers[kind]
        pltpu.make_async_copy(buffer.at[shard], buffer.at[shard], z_recv.at[kind, shard]).wait()

    def z_forward(kind, step):
        for direction in (1, -1):

            @pl.when(z_cond(step, direction))
            def _(direction=direction):
                if step > 0:
                    z_arrived(kind, z - direction * step)
                z_copy(kind, step, direction).start()

    def z_wait_send(kind, step):
        for direction in (1, -1):

            @pl.when(z_cond(step, direction))
            def _(direction=direction):
                z_copy(kind, step, direction).wait_send()

    def z_last(kind, step):
        @pl.when((z == planes - 1) & (z - 1 - step >= 0))
        def _():
            z_arrived(kind, z - 1 - step)

        @pl.when((z == 0) & (z + 1 + step < planes))
        def _():
            z_arrived(kind, z + 1 + step)

    def out_start(step):
        for direction in (1, -1):
            last = z if direction > 0 else planes - 1 - z

            @pl.when(z_cond(0, direction) & (last == step))
            def _(direction=direction):
                z_copy(3, 0, direction).start()
                z_copy(4, 0, direction).start()

    gathered = (normed, keys, values)

    def row_copy(kind, block, target, slot):
        return pltpu.make_async_remote_copy(
            src_ref=gathered[kind].at[block],
            dst_ref=gathered[kind].at[block],
            send_sem=rows_send.at[kind, slot],
            recv_sem=rows_recv.at[kind, block],
            device_id={"gx": target},
            device_id_type=MESH,
        )

    def rows_start(kind):
        for slot, target in enumerate(peers + [sibling]):
            row_copy(kind, me, target, slot).start()

    def rows_wait(kind, block):
        pltpu.make_async_copy(
            gathered[kind].at[block], gathered[kind].at[block], rows_recv.at[kind, block]
        ).wait()

    def rows_forward(kind):
        for flip in range(FLIPS):
            rows_wait(kind, peers[flip])
            row_copy(kind, peers[flip], sibling, 4 + flip).start()

    def rows_finish(kind):
        for block in [sibling] + far:
            rows_wait(kind, block)

    for kind in range(3):
        z_forward(kind, 0)
    out_start(0)

    for slot in range(3):
        loads[slot].wait()
    rows = hidden_in[...].astype(jnp.float32)
    average = jnp.mean(rows, axis=-1, keepdims=True)
    centred = rows - average
    spread = jnp.mean(centred * centred, axis=-1, keepdims=True)
    normed[me] = (
        centred * lax.rsqrt(spread + 1e-05) * gain_in[...] + bias_in[...]
    ).astype(jnp.bfloat16)
    rows_start(0)
    for kind in (1, 2):
        loads[kind + 2].wait()
        rows_start(kind)

    z_forward(0, 1)
    z_forward(0, 2)
    z_forward(1, 1)
    rows_forward(0)
    z_forward(2, 1)
    out_start(1)
    rows_finish(0)
    loads[5].wait()
    for step in range(planes - 1):
        z_last(0, step)

    tokens = normed[...].reshape(-1, normed.shape[2])
    token_count = tokens.shape[0]
    depth = 2 * half_depth
    kv_width = wkv_all.shape[1]
    kv_part = jnp.zeros((kv_width, token_count), jnp.float32)
    for part in range(planes):
        kv_part += lax.dot_general(
            wkv_all[part],
            tokens[:, part * depth : (part + 1) * depth],
            (((1,), (1,)), ((), ())),
            preferred_element_type=jnp.float32,
        )
    new_kv[me] = kv_part.astype(jnp.bfloat16)

    def kv_copy(block, target, slot):
        return pltpu.make_async_remote_copy(
            src_ref=new_kv.at[block],
            dst_ref=new_kv.at[block],
            send_sem=kv_send.at[slot],
            recv_sem=kv_recv.at[block],
            device_id={"gx": target},
            device_id_type=MESH,
        )

    for slot, target in enumerate(everyone):
        kv_copy(me, target, slot).start()

    rows_forward(1)
    z_forward(1, 2)
    rows_forward(2)
    z_forward(2, 2)
    out_start(2)

    for block in everyone:
        pltpu.make_async_copy(new_kv.at[block], new_kv.at[block], kv_recv.at[block]).wait()

    length = length_ref[0]
    page = key_ref.shape[0]
    head_dim = key_ref.shape[1]
    kv_cols = new_kv[...].reshape(2 * head_dim, token_count)
    offsets = (
        lax.broadcasted_iota(jnp.int32, (page, token_count), 0) + me * page - length
    )
    chosen = offsets == lax.broadcasted_iota(jnp.int32, (page, token_count), 1)
    picked = lax.dot_general(
        jnp.where(chosen, 1.0, 0.0).astype(jnp.bfloat16),
        kv_cols,
        (((1,), (1,)), ((), ())),
        preferred_element_type=jnp.float32,
    )
    row_offset = lax.broadcasted_iota(jnp.int32, (page, head_dim), 0) + me * page - length
    inside = (row_offset >= 0) & (row_offset < token_count)
    new_key_ref[...] = jnp.where(
        inside, picked[:, :head_dim], keys[me].astype(jnp.float32)
    ).astype(jnp.bfloat16)
    new_value_ref[...] = jnp.where(
        inside, picked[:, head_dim:], values[me].astype(jnp.float32)
    ).astype(jnp.bfloat16)

    rows_finish(1)
    rows_finish(2)
    for half in range(2):
        loads[6 + half].wait()
        for step in range(planes - 1):
            z_last(1 + half, step)

    heads = wq_all.shape[3] // head_dim
    query = jnp.zeros((token_count, heads * head_dim), jnp.float32)
    for part in range(2 * planes):
        query += jnp.dot(
            normed[:, :, part * half_depth : (part + 1) * half_depth].reshape(
                token_count, half_depth
            ),
            wq_all[part % 2, part // 2],
            preferred_element_type=jnp.float32,
        )
    query = query.astype(jnp.bfloat16)
    for head in range(heads):
        query_rows[head * token_count : (head + 1) * token_count, :] = query[
            :, head * head_dim : (head + 1) * head_dim
        ]

    cached = keys.shape[0] * page - token_count
    block_rows = 128
    scale = head_dim ** (-0.5) * math.log2(math.e)

    def attend(start):
        first = pl.multiple_of(start * block_rows, block_rows)
        q = query_rows[pl.ds(first, block_rows), :]
        old_keys = keys[...].reshape(-1, head_dim)[:cached]
        old_values = values[...].reshape(-1, head_dim)[:cached]
        fresh = new_kv[...].reshape(2 * head_dim, token_count)
        old_pos = lax.broadcasted_iota(jnp.int32, (block_rows, cached), 1)
        old = lax.dot_general(
            q, old_keys, (((1,), (1,)), ((), ())), preferred_element_type=jnp.float32
        )
        old = jnp.where(old_pos < length, old * scale, NEGATIVE)
        row = lax.broadcasted_iota(jnp.int32, (block_rows, token_count), 0) + first % token_count
        col = lax.broadcasted_iota(jnp.int32, (block_rows, token_count), 1)
        new = jnp.dot(q, fresh[:head_dim], preferred_element_type=jnp.float32)
        new = jnp.where(col <= row, new * scale, NEGATIVE)
        top = jnp.maximum(
            jnp.max(old, axis=1, keepdims=True), jnp.max(new, axis=1, keepdims=True)
        )
        old = jnp.exp2(old - top)
        new = jnp.exp2(new - top)
        total = jnp.sum(old, axis=1, keepdims=True) + jnp.sum(new, axis=1, keepdims=True)
        summed = jnp.dot(
            old.astype(jnp.bfloat16), old_values, preferred_element_type=jnp.float32
        ) + lax.dot_general(
            new.astype(jnp.bfloat16),
            fresh[head_dim:],
            (((1,), (1,)), ((), ())),
            preferred_element_type=jnp.float32,
        )
        attended[pl.ds(first, block_rows), :] = (summed / total).astype(jnp.bfloat16)

    blocks = heads * token_count // block_rows
    pl.loop(0, blocks // 2)(attend)
    z_forward(3, 1)
    z_forward(4, 1)
    pl.loop(blocks // 2, blocks)(attend)

    own_rows = hidden_ref.shape[0]
    result_rows = jnp.concatenate(
        [attended[head * token_count : (head + 1) * token_count, :] for head in range(heads)],
        axis=1,
    )

    def sib_copy(n):
        return pltpu.make_async_remote_copy(
            src_ref=sibling_out.at[n],
            dst_ref=sibling_in.at[n],
            send_sem=sib_send.at[n],
            recv_sem=sib_recv.at[n],
            device_id={"gx": sibling},
            device_id_type=MESH,
        )

    def chip_copy(n, flip):
        return pltpu.make_async_remote_copy(
            src_ref=chip_out.at[n, flip],
            dst_ref=chip_in.at[n, flip],
            send_sem=chip_send.at[n, flip],
            recv_sem=chip_recv.at[n, flip],
            device_id={"gx": peers[flip]},
            device_id_type=MESH,
        )

    def project(n):
        partial[n] = jnp.dot(
            result_rows, wo_all[n % 2, order[n // 2]], preferred_element_type=jnp.float32
        ).reshape(2 * CHIPS, own_rows, half_width)
        for k in range(CHIPS):
            sibling_out[n, k] = partial[n, 2 * k + 1 - core].astype(jnp.bfloat16)
        sib_copy(n).start()

    def spread_sums(n):
        sib_copy(n).wait_recv()
        for flip in range(FLIPS):
            other = other_chips[flip]
            chip_out[n, flip] = (
                partial[n, 2 * other + core] + sibling_in[n, other].astype(jnp.float32)
            ).astype(jnp.bfloat16)
            chip_copy(n, flip).start()
        own_sum[n] = partial[n, me] + sibling_in[n, chip].astype(jnp.float32)

    low = z < planes // 2
    order = [z, jnp.where(low, z + 1, z - 1)]
    order.append(jnp.where(low, (z + planes - 1) % planes, (z + 1) % planes))
    order[2] = jnp.where((z == 0) | (z == planes - 1), jnp.where(low, 2, planes - 3), order[2])
    order.append(jnp.where(low, planes - 1, 0))

    slices = 2 * planes
    for n in range(slices):
        step = n // 2 - 1
        if n < 2:
            loads[8 + n].wait()
        else:
            z_last(3 + n % 2, step)
        if n >= 2 and step + 1 == 1:
            z_forward(3 + n % 2, 2)
        project(n)
        if n > 0:
            spread_sums(n - 1)
    spread_sums(slices - 1)
    for n in range(slices):
        total = own_sum[n]
        for flip in range(FLIPS):
            chip_copy(n, flip).wait_recv()
            total += chip_in[n, flip].astype(jnp.float32)
        column = pl.multiple_of(order[n // 2] * 2 * half_width + n % 2 * half_width, half_width)
        out_ref[:, pl.ds(column, half_width)] = total.astype(jnp.bfloat16)

    for kind in range(5):
        for step in range(planes - 1):
            z_wait_send(kind, step)
    for kind in range(3):
        for slot, target in enumerate(peers + [sibling]):
            row_copy(kind, me, target, slot).wait_send()
        for flip in range(FLIPS):
            row_copy(kind, peers[flip], sibling, 4 + flip).wait_send()
    for slot, target in enumerate(everyone):
        kv_copy(me, target, slot).wait_send()
    for n in range(slices):
        sib_copy(n).wait_send()
        for flip in range(FLIPS):
            chip_copy(n, flip).wait_send()


def fused(
    groups,
    planes,
    hidden_states,
    norm_gain,
    norm_bias,
    query_weight,
    keyvalue_weight,
    out_weight,
    key_cache,
    value_cache,
    cache_length,
):
    own_rows, model = hidden_states.shape[1:]
    page, head_dim = key_cache.shape[1:]
    span = own_rows * groups
    depth, columns = query_weight.shape
    kv_width = keyvalue_weight.shape[1]
    out_rows, width = out_weight.shape
    heads = columns // head_dim
    bf16, f32 = jnp.bfloat16, jnp.float32
    vmem = pl.BlockSpec(memory_space=pltpu.VMEM)
    hbm = pl.BlockSpec(memory_space=pltpu.HBM)
    dma = pltpu.SemaphoreType.DMA
    out, new_key, new_value = pl.pallas_call(
        functools.partial(fused_kernel, planes),
        out_shape=(
            jax.ShapeDtypeStruct((own_rows, model), bf16),
            jax.ShapeDtypeStruct((page, head_dim), bf16),
            jax.ShapeDtypeStruct((page, head_dim), bf16),
        ),
        in_specs=[hbm] * 8 + [pl.BlockSpec(memory_space=pltpu.SMEM)],
        out_specs=(vmem, vmem, vmem),
        scratch_shapes=[
            pltpu.VMEM((own_rows, model), bf16),
            pltpu.VMEM((1, model), f32),
            pltpu.VMEM((1, model), f32),
            pltpu.VMEM((groups, own_rows, model), bf16),
            pltpu.VMEM((2, planes, depth // 2, columns), bf16),
            pltpu.VMEM((planes, kv_width, depth), bf16),
            pltpu.VMEM((2, planes, out_rows, width // 2), bf16),
            pltpu.VMEM((groups, page, head_dim), bf16),
            pltpu.VMEM((groups, page, head_dim), bf16),
            pltpu.VMEM((groups, kv_width, span), bf16),
            pltpu.VMEM((heads * span, head_dim), bf16),
            pltpu.VMEM((heads * span, head_dim), bf16),
            pltpu.VMEM((2 * planes, 2 * CHIPS, own_rows, width // 2), f32),
            pltpu.VMEM((2 * planes, CHIPS, own_rows, width // 2), bf16),
            pltpu.VMEM((2 * planes, CHIPS, own_rows, width // 2), bf16),
            pltpu.VMEM((2 * planes, FLIPS, own_rows, width // 2), bf16),
            pltpu.VMEM((2 * planes, FLIPS, own_rows, width // 2), bf16),
            pltpu.VMEM((2 * planes, own_rows, width // 2), f32),
            dma((10,)),
            dma((5, planes - 1, 2)),
            dma((5, planes)),
            dma((3, 4 + FLIPS)),
            dma((3, groups)),
            dma((groups - 1,)),
            dma((groups,)),
            dma((2 * planes,)),
            dma((2 * planes,)),
            dma((2 * planes, FLIPS)),
            dma((2 * planes, FLIPS)),
        ],
        compiler_params=pltpu.CompilerParams(
            collective_id=0, has_side_effects=True, vmem_limit_bytes=64 * 1024 * 1024
        ),
        cost_estimate=pl.CostEstimate(
            flops=10**9, bytes_accessed=2 * 10**6, transcendentals=10**6
        ),
        name="attention_layer",
    )(
        hidden_states[0],
        norm_gain[None],
        norm_bias[None],
        query_weight,
        keyvalue_weight.T,
        out_weight,
        key_cache[0],
        value_cache[0],
        cache_length,
    )
    return out[None], new_key[None], new_value[None]


def device_program(mesh, *args):
    groups, planes = mesh.shape["gx"], mesh.shape["gy"]
    if groups == 2 * CHIPS and planes == 4:
        return fused(groups, planes, *args)
    return body(*args)


def solution(mesh):
    return jax.shard_map(
        functools.partial(device_program, mesh),
        mesh=mesh,
        in_specs=(
            P("gy", "gx", None),
            P(),
            P(),
            P("gy", "gx"),
            P("gy", "gx"),
            P("gx", "gy"),
            P("gy", "gx", None),
            P("gy", "gx", None),
            P("gy"),
        ),
        out_specs=(P("gy", "gx", None), P("gy", "gx", None), P("gy", "gx", None)),
        check_vma=False,
    )
```

```python
import functools
import math

import jax
import jax.numpy as jnp
from jax import lax
from jax.experimental import pallas as pl
from jax.experimental.pallas import tpu as pltpu
from jax.sharding import PartitionSpec as P

HEADS = 16


NEGATIVE = -1e30


def normalize(hidden_states, norm_gain, norm_bias):
    values = hidden_states.astype(jnp.float32)
    average = jnp.mean(values, axis=-1, keepdims=True)
    centred = values - average
    spread = jnp.mean(centred * centred, axis=-1, keepdims=True)
    return (centred * lax.rsqrt(spread + 1e-05) * norm_gain + norm_bias).astype(jnp.bfloat16)


def page_terms(query_rows, query_pos, key_rows, value_rows, page_size):
    row_count = query_rows.shape[0]
    head_dim = key_rows.shape[1]
    page_count = key_rows.shape[0] // page_size
    scores = lax.dot_general(
        query_rows, key_rows, (((1,), (1,)), ((), ())), preferred_element_type=jnp.float32
    )
    scores = (scores * head_dim ** (-0.5)).reshape(row_count, page_count, page_size)
    key_pos = jnp.arange(page_count * page_size, dtype=jnp.int32).reshape(page_count, page_size)
    allowed = key_pos[None, :, :] <= query_pos[:, None, None]
    maxima = jnp.max(jnp.where(allowed, scores, NEGATIVE), axis=2)
    weights = jnp.where(allowed, jnp.exp(scores - maxima[:, :, None]), 0.0)
    totals = jnp.sum(weights, axis=2)
    weighted = jnp.einsum(
        "rnp,npd->rnd",
        weights.astype(jnp.bfloat16),
        value_rows.reshape(page_count, page_size, head_dim),
        preferred_element_type=jnp.float32,
    )
    return (maxima, totals, weighted)


def reduce_pages(maxima, totals, weighted):
    largest = jnp.max(maxima, axis=1)
    factor = jnp.exp(maxima - largest[:, None])
    return (
        largest,
        jnp.sum(totals * factor, axis=1),
        jnp.sum(weighted * factor[:, :, None], axis=1),
    )


def join_pages(first, second):
    larger = jnp.maximum(first[0], second[0])
    second_factor = jnp.exp(second[0] - larger)
    return (larger, second[1] * second_factor, second[2] * second_factor[:, None])


def body(
    hidden_states,
    norm_gain,
    norm_bias,
    query_weight,
    keyvalue_weight,
    out_weight,
    key_cache,
    value_cache,
    cache_length,
):
    own_tokens = hidden_states.shape[1]
    groups = lax.axis_size("gx")
    column_index = lax.axis_index("gx")
    span_len = own_tokens * groups
    page_size = key_cache.shape[1]
    head_dim = key_cache.shape[2]
    head_count = HEADS
    head_width = head_count * head_dim
    normed = normalize(hidden_states[0], norm_gain, norm_bias)
    full_rows = lax.all_gather(normed, "gx", axis=0, tiled=True)
    pieces = (
        lax.all_gather(query_weight, "gy", axis=0, tiled=True),
        lax.all_gather(keyvalue_weight, "gy", axis=0, tiled=True),
    )
    query_part = jnp.dot(full_rows, pieces[0], preferred_element_type=jnp.float32)
    keyvalue_part = jnp.dot(full_rows, pieces[1], preferred_element_type=jnp.float32)
    query_local = query_part.astype(jnp.bfloat16)
    keyvalue_local = keyvalue_part.astype(jnp.bfloat16)
    queries, new_keyvalue = (
        lax.all_gather(query_local, "gx", axis=1, tiled=True),
        lax.all_gather(keyvalue_local, "gx", axis=1, tiled=True),
    )
    length = cache_length[0]
    page_base = column_index * page_size
    offsets = page_base + jnp.arange(page_size, dtype=jnp.int32) - length
    inside = (offsets >= 0) & (offsets < span_len)
    picked = jnp.take(new_keyvalue, jnp.clip(offsets, 0, span_len - 1), axis=0)
    key_page = jnp.where(inside[:, None], picked[:, :head_dim], key_cache[0])
    value_page = jnp.where(inside[:, None], picked[:, head_dim:], value_cache[0])
    own_rows = lax.dynamic_slice_in_dim(queries, column_index * own_tokens, own_tokens, 0)
    own_rows = own_rows.reshape(own_tokens * head_count, head_dim)
    own_pos = (
        length
        + column_index * own_tokens
        + jnp.arange(own_tokens * head_count, dtype=jnp.int32) // head_count
    )
    own_total = own_tokens * head_count
    empty = (
        jnp.full((own_total,), NEGATIVE, jnp.float32),
        jnp.zeros((own_total,), jnp.float32),
        jnp.zeros((own_total, head_dim), jnp.float32),
    )
    pieces = (
        lax.all_gather(key_page, "gx", axis=0, tiled=True),
        lax.all_gather(value_page, "gx", axis=0, tiled=True),
    )
    maxima, totals, weighted = page_terms(own_rows, own_pos, pieces[0], pieces[1], page_size)
    maxima, totals, weighted = join_pages(empty, reduce_pages(maxima, totals, weighted))
    own_out = (weighted / totals[:, None]).reshape(own_tokens, head_width).astype(jnp.bfloat16)
    attended = lax.all_to_all(own_out, "gx", split_axis=1, concat_axis=0, tiled=True)
    out_full = lax.all_gather(out_weight, "gy", axis=1, tiled=True)
    hidden_part = lax.psum_scatter(
        jnp.dot(attended, out_full, preferred_element_type=jnp.float32),
        "gx",
        scatter_dimension=0,
        tiled=True,
    )
    return (hidden_part.astype(jnp.bfloat16)[None], key_page[None], value_page[None])


MESH = pl.DeviceIdType.MESH
CHIPS = 4
FLIPS = 3


def fused_kernel(
    planes,
    hidden_ref,
    gain_ref,
    bias_ref,
    wq_ref,
    wkv_ref,
    wo_ref,
    key_ref,
    value_ref,
    length_ref,
    out_ref,
    new_key_ref,
    new_value_ref,
    hidden_in,
    gain_in,
    bias_in,
    normed,
    wq_all,
    wkv_all,
    wo_own,
    keys,
    values,
    new_kv,
    query_rows,
    attended,
    partial,
    sibling_out,
    sibling_in,
    chip_out,
    chip_in,
    own_sum,
    pieces,
    load_sem,
    z_send,
    z_recv,
    rows_send,
    rows_recv,
    kv_send,
    kv_recv,
    sib_send,
    sib_recv,
    chip_send,
    chip_recv,
    home_send,
    home_recv,
):
    me = lax.axis_index("gx")
    z = lax.axis_index("gy")
    core = me % 2
    chip = me // 2
    cx = chip % 2
    cy = chip // 2
    sibling = chip * 2 + 1 - core
    other_chips = (cy * 2 + 1 - cx, (1 - cy) * 2 + cx, (1 - cy) * 2 + 1 - cx)
    peers = [other * 2 + core for other in other_chips]
    far = [other * 2 + 1 - core for other in other_chips]
    everyone = [sibling] + peers + far
    has_up = z < planes - 1
    has_down = z > 0

    barrier = pltpu.get_barrier_semaphore()
    for peer in everyone:
        pl.semaphore_signal(barrier, inc=1, device_id={"gx": peer}, device_id_type=MESH)

    other_planes = [lax.rem(z + k, planes) for k in range(1, planes)]
    for plane in other_planes:
        pl.semaphore_signal(barrier, inc=1, device_id={"gy": plane}, device_id_type=MESH)

    half_depth = wq_all.shape[2]
    half_rows = [wq_ref.at[pl.ds(half * half_depth, half_depth)] for half in range(2)]
    sources = [wkv_ref] + half_rows
    buffers = [wkv_all, wq_all.at[0], wq_all.at[1], attended.at[0], attended.at[1]]
    loads = [
        pltpu.make_async_copy(source, target, load_sem.at[slot])
        for slot, (source, target) in enumerate(
            [
                (hidden_ref, hidden_in),
                (gain_ref, gain_in),
                (bias_ref, bias_in),
                (key_ref, keys.at[me]),
                (value_ref, values.at[me]),
            ]
            + [(source, buffer.at[z]) for source, buffer in zip(sources, buffers)]
            + [(wo_ref, wo_own)]
        )
    ]
    for load in loads:
        load.start()

    pl.semaphore_wait(barrier, len(everyone) + planes - 1)

    def z_copy(kind, step, direction, own=False):
        shard = z - direction * step
        buffer = buffers[kind]
        return pltpu.make_async_remote_copy(
            src_ref=sources[kind] if own and kind < len(sources) else buffer.at[shard],
            dst_ref=buffer.at[shard],
            send_sem=z_send.at[kind, step, (direction + 1) // 2],
            recv_sem=z_recv.at[kind, shard],
            device_id={"gy": z + direction},
            device_id_type=MESH,
        )

    def z_cond(step, direction):
        if direction > 0:
            return has_up & (z - step >= 0)
        return has_down & (z + step < planes)

    def z_arrived(kind, shard):
        buffer = buffers[kind]
        pltpu.make_async_copy(buffer.at[shard], buffer.at[shard], z_recv.at[kind, shard]).wait()

    def z_forward(kind, step):
        for direction in (1, -1):

            @pl.when(z_cond(step, direction))
            def _(direction=direction):
                if step > 0:
                    z_arrived(kind, z - direction * step)
                z_copy(kind, step, direction, step == 0).start()

    def z_wait_send(kind, step):
        for direction in (1, -1):

            @pl.when(z_cond(step, direction))
            def _(direction=direction):
                z_copy(kind, step, direction, step == 0).wait_send()

    def z_last(kind, step):
        @pl.when((z == planes - 1) & (z - 1 - step >= 0))
        def _():
            z_arrived(kind, z - 1 - step)

        @pl.when((z == 0) & (z + 1 + step < planes))
        def _():
            z_arrived(kind, z + 1 + step)

    def z_take(kind, shard):
        z_arrived(kind, shard)

        @pl.when((shard < z) & has_up)
        def _():
            z_copy(kind, z - shard, 1).start()

        @pl.when((shard > z) & has_down)
        def _():
            z_copy(kind, shard - z, -1).start()

    gathered = (normed, keys, values)

    def row_copy(kind, block, target, slot):
        return pltpu.make_async_remote_copy(
            src_ref=gathered[kind].at[block],
            dst_ref=gathered[kind].at[block],
            send_sem=rows_send.at[kind, slot],
            recv_sem=rows_recv.at[kind, block],
            device_id={"gx": target},
            device_id_type=MESH,
        )

    def rows_start(kind):
        for slot, target in enumerate(peers + [sibling]):
            row_copy(kind, me, target, slot).start()

    def rows_wait(kind, block):
        pltpu.make_async_copy(
            gathered[kind].at[block], gathered[kind].at[block], rows_recv.at[kind, block]
        ).wait()

    def rows_forward(kind):
        for flip in range(FLIPS):
            rows_wait(kind, peers[flip])
            row_copy(kind, peers[flip], sibling, 4 + flip).start()

    def rows_finish(kind):
        for block in [sibling] + far:
            rows_wait(kind, block)

    for kind in range(3):
        z_forward(kind, 0)

    for slot in range(3):
        loads[slot].wait()
    rows = hidden_in[...].astype(jnp.float32)
    average = jnp.mean(rows, axis=-1, keepdims=True)
    centred = rows - average
    spread = jnp.mean(centred * centred, axis=-1, keepdims=True)
    normed[me] = (
        centred * lax.rsqrt(spread + 1e-05) * gain_in[...] + bias_in[...]
    ).astype(jnp.bfloat16)
    rows_start(0)
    for kind in (1, 2):
        loads[kind + 2].wait()
        rows_start(kind)

    z_forward(0, 1)
    z_forward(0, 2)
    z_forward(1, 1)
    rows_forward(0)
    z_forward(2, 1)
    rows_finish(0)
    loads[5].wait()
    for step in range(planes - 1):
        z_last(0, step)

    tokens = normed[...].reshape(-1, normed.shape[2])
    token_count = tokens.shape[0]
    depth = 2 * half_depth
    kv_width = wkv_all.shape[1]
    kv_part = jnp.zeros((kv_width, token_count), jnp.float32)
    for part in range(planes):
        kv_part += lax.dot_general(
            wkv_all[part],
            tokens[:, part * depth : (part + 1) * depth],
            (((1,), (1,)), ((), ())),
            preferred_element_type=jnp.float32,
        )
    new_kv[me] = kv_part.astype(jnp.bfloat16)

    def kv_copy(block, target, slot):
        return pltpu.make_async_remote_copy(
            src_ref=new_kv.at[block],
            dst_ref=new_kv.at[block],
            send_sem=kv_send.at[slot],
            recv_sem=kv_recv.at[block],
            device_id={"gx": target},
            device_id_type=MESH,
        )

    for slot, target in enumerate(everyone):
        kv_copy(me, target, slot).start()

    rows_forward(1)
    z_forward(1, 2)
    rows_forward(2)
    z_forward(2, 2)

    for block in everyone:
        pltpu.make_async_copy(new_kv.at[block], new_kv.at[block], kv_recv.at[block]).wait()

    length = length_ref[0]
    page = key_ref.shape[0]
    head_dim = key_ref.shape[1]
    kv_cols = new_kv[...].reshape(2 * head_dim, token_count)
    offsets = (
        lax.broadcasted_iota(jnp.int32, (page, token_count), 0) + me * page - length
    )
    chosen = offsets == lax.broadcasted_iota(jnp.int32, (page, token_count), 1)
    picked = lax.dot_general(
        jnp.where(chosen, 1.0, 0.0).astype(jnp.bfloat16),
        kv_cols,
        (((1,), (1,)), ((), ())),
        preferred_element_type=jnp.float32,
    )
    row_offset = lax.broadcasted_iota(jnp.int32, (page, head_dim), 0) + me * page - length
    inside = (row_offset >= 0) & (row_offset < token_count)
    new_key_ref[...] = jnp.where(
        inside, picked[:, :head_dim], keys[me].astype(jnp.float32)
    ).astype(jnp.bfloat16)
    new_value_ref[...] = jnp.where(
        inside, picked[:, head_dim:], values[me].astype(jnp.float32)
    ).astype(jnp.bfloat16)

    rows_finish(1)
    rows_finish(2)
    for half in range(2):
        loads[6 + half].wait()
        for step in range(planes - 1):
            z_last(1 + half, step)

    heads = wq_all.shape[3] // head_dim
    query = jnp.zeros((token_count, heads * head_dim), jnp.float32)
    for part in range(2 * planes):
        query += jnp.dot(
            normed[:, :, part * half_depth : (part + 1) * half_depth].reshape(
                token_count, half_depth
            ),
            wq_all[part % 2, part // 2],
            preferred_element_type=jnp.float32,
        )
    query = query.astype(jnp.bfloat16)
    own_rows = hidden_ref.shape[0]
    half_own = own_rows // 2
    half_rows = token_count // 2
    query = query.reshape(2 * CHIPS, own_rows, heads * head_dim)
    for half in range(2):
        rows_of_half = query[:, half * half_own : (half + 1) * half_own].reshape(half_rows, -1)
        for head in range(heads):
            query_rows[half * heads + head] = rows_of_half[
                :, head * head_dim : (head + 1) * head_dim
            ]

    cached = keys.shape[0] * page - token_count
    block_rows = half_rows
    scale = head_dim ** (-0.5) * math.log2(math.e)

    def attend(half, head):
        q = query_rows[half * heads + head]
        old_keys = keys[...].reshape(-1, head_dim)[:cached]
        old_values = values[...].reshape(-1, head_dim)[:cached]
        fresh = new_kv[...].reshape(2 * head_dim, token_count)
        old_pos = lax.broadcasted_iota(jnp.int32, (block_rows, cached), 1)
        old = lax.dot_general(
            q, old_keys, (((1,), (1,)), ((), ())), preferred_element_type=jnp.float32
        )
        old = jnp.where(old_pos < length, old * scale, NEGATIVE)
        row = lax.broadcasted_iota(jnp.int32, (block_rows, token_count), 0)
        row = row // half_own * own_rows + half * half_own + row % half_own
        col = lax.broadcasted_iota(jnp.int32, (block_rows, token_count), 1)
        new = jnp.dot(q, fresh[:head_dim], preferred_element_type=jnp.float32)
        new = jnp.where(col <= row, new * scale, NEGATIVE)
        top = jnp.maximum(
            jnp.max(old, axis=1, keepdims=True), jnp.max(new, axis=1, keepdims=True)
        )
        old = jnp.exp2(old - top)
        new = jnp.exp2(new - top)
        total = jnp.sum(old, axis=1, keepdims=True) + jnp.sum(new, axis=1, keepdims=True)
        summed = jnp.dot(
            old.astype(jnp.bfloat16), old_values, preferred_element_type=jnp.float32
        ) + lax.dot_general(
            new.astype(jnp.bfloat16),
            fresh[head_dim:],
            (((1,), (1,)), ((), ())),
            preferred_element_type=jnp.float32,
        )
        return (summed / total).astype(jnp.bfloat16)

    for half in range(2):
        attended[half, z] = jnp.concatenate(
            [attend(half, head) for head in range(heads)], axis=1
        )
        z_forward(3 + half, 0)

    width = wo_own.shape[1]

    def sib_copy(n):
        return pltpu.make_async_remote_copy(
            src_ref=sibling_out.at[n],
            dst_ref=sibling_in.at[n],
            send_sem=sib_send.at[n],
            recv_sem=sib_recv.at[n],
            device_id={"gx": sibling},
            device_id_type=MESH,
        )

    def chip_copy(n, flip):
        return pltpu.make_async_remote_copy(
            src_ref=chip_out.at[n, flip],
            dst_ref=chip_in.at[n, flip],
            send_sem=chip_send.at[n, flip],
            recv_sem=chip_recv.at[n, flip],
            device_id={"gx": peers[flip]},
            device_id_type=MESH,
        )

    def project(n):
        partial[n] = jnp.dot(
            attended[n % 2, order[n // 2]], wo_own[...], preferred_element_type=jnp.float32
        ).reshape(2 * CHIPS, half_own, width)
        for k in range(CHIPS):
            sibling_out[n, k] = partial[n, 2 * k + 1 - core].astype(jnp.bfloat16)
        sib_copy(n).start()

    def spread_sums(n):
        sib_copy(n).wait_recv()
        for flip in range(FLIPS):
            other = other_chips[flip]
            chip_out[n, flip] = (
                partial[n, 2 * other + core] + sibling_in[n, other].astype(jnp.float32)
            ).astype(jnp.bfloat16)
            chip_copy(n, flip).start()
        own_sum[n] = partial[n, me] + sibling_in[n, chip].astype(jnp.float32)

    low = z < planes // 2
    order = [z, jnp.where(low, z + 1, z - 1)]
    order.append(jnp.where(low, (z + planes - 1) % planes, (z + 1) % planes))
    order[2] = jnp.where((z == 0) | (z == planes - 1), jnp.where(low, 2, planes - 3), order[2])
    order.append(jnp.where(low, planes - 1, 0))

    def home_copy(n, plane):
        return pltpu.make_async_remote_copy(
            src_ref=pieces.at[n],
            dst_ref=out_ref.at[
                pl.ds(n % 2 * half_own, half_own), pl.ds(pl.multiple_of(z * width, width), width)
            ],
            send_sem=home_send.at[n],
            recv_sem=home_recv.at[n % 2, z],
            device_id={"gy": plane},
            device_id_type=MESH,
        )

    def finish(n):
        total = own_sum[n]
        for flip in range(FLIPS):
            chip_copy(n, flip).wait_recv()
            total += chip_in[n, flip].astype(jnp.float32)
        piece = total.astype(jnp.bfloat16)
        if n < 2:
            column = pl.multiple_of(z * width, width)
            out_ref[n * half_own : (n + 1) * half_own, pl.ds(column, width)] = piece
        else:
            pieces[n] = piece
            home_copy(n, order[n // 2]).start()

    slices = 2 * planes
    loads[8].wait()
    for pos in range(planes):
        pair = (2 * pos, 2 * pos + 1)
        for n in pair:
            if pos > 0:
                z_take(3 + n % 2, order[pos])
            project(n)
        if pos > 0:
            for n in pair:
                finish(n - 2)
        for n in pair:
            spread_sums(n)
    finish(slices - 2)
    finish(slices - 1)
    for plane in other_planes:
        for half in range(2):
            landed = out_ref.at[
                pl.ds(half * half_own, half_own),
                pl.ds(pl.multiple_of(plane * width, width), width),
            ]
            pltpu.make_async_copy(landed, landed, home_recv.at[half, plane]).wait()

    for n in range(2, slices):
        home_copy(n, order[n // 2]).wait_send()
    for kind in range(5):
        for step in range(planes - 1):
            z_wait_send(kind, step)
    for kind in range(3):
        for slot, target in enumerate(peers + [sibling]):
            row_copy(kind, me, target, slot).wait_send()
        for flip in range(FLIPS):
            row_copy(kind, peers[flip], sibling, 4 + flip).wait_send()
    for slot, target in enumerate(everyone):
        kv_copy(me, target, slot).wait_send()
    for n in range(slices):
        sib_copy(n).wait_send()
        for flip in range(FLIPS):
            chip_copy(n, flip).wait_send()


def hand_over(out_ref, key_ref, value_ref, out_to, key_to, value_to, sem):
    copies = [
        pltpu.make_async_copy(source, target.at[0], sem.at[slot])
        for slot, (source, target) in enumerate(
            [(out_ref, out_to), (key_ref, key_to), (value_ref, value_to)]
        )
    ]
    for copy in copies:
        copy.start()
    for copy in copies:
        copy.wait()


def fused(
    groups,
    planes,
    hidden_states,
    norm_gain,
    norm_bias,
    query_weight,
    keyvalue_weight,
    out_weight,
    key_cache,
    value_cache,
    cache_length,
):
    own_rows, model = hidden_states.shape[1:]
    page, head_dim = key_cache.shape[1:]
    span = own_rows * groups
    depth, columns = query_weight.shape
    kv_width = keyvalue_weight.shape[1]
    out_rows, width = out_weight.shape
    heads = columns // head_dim
    bf16, f32 = jnp.bfloat16, jnp.float32
    vmem = pl.BlockSpec(memory_space=pltpu.VMEM)
    hbm = pl.BlockSpec(memory_space=pltpu.HBM)
    dma = pltpu.SemaphoreType.DMA
    out, new_key, new_value = pl.pallas_call(
        functools.partial(fused_kernel, planes),
        out_shape=(
            jax.ShapeDtypeStruct((own_rows, model), bf16),
            jax.ShapeDtypeStruct((page, head_dim), bf16),
            jax.ShapeDtypeStruct((page, head_dim), bf16),
        ),
        in_specs=[hbm] * 8 + [pl.BlockSpec(memory_space=pltpu.SMEM)],
        out_specs=(vmem, vmem, vmem),
        scratch_shapes=[
            pltpu.VMEM((own_rows, model), bf16),
            pltpu.VMEM((1, model), f32),
            pltpu.VMEM((1, model), f32),
            pltpu.VMEM((groups, own_rows, model), bf16),
            pltpu.VMEM((2, planes, depth // 2, columns), bf16),
            pltpu.VMEM((planes, kv_width, depth), bf16),
            pltpu.VMEM((out_rows, width), bf16),
            pltpu.VMEM((groups, page, head_dim), bf16),
            pltpu.VMEM((groups, page, head_dim), bf16),
            pltpu.VMEM((groups, kv_width, span), bf16),
            pltpu.VMEM((2 * heads, span // 2, head_dim), bf16),
            pltpu.VMEM((2, planes, span // 2, heads * head_dim), bf16),
            pltpu.VMEM((2 * planes, 2 * CHIPS, own_rows // 2, width), f32),
            pltpu.VMEM((2 * planes, CHIPS, own_rows // 2, width), bf16),
            pltpu.VMEM((2 * planes, CHIPS, own_rows // 2, width), bf16),
            pltpu.VMEM((2 * planes, FLIPS, own_rows // 2, width), bf16),
            pltpu.VMEM((2 * planes, FLIPS, own_rows // 2, width), bf16),
            pltpu.VMEM((2 * planes, own_rows // 2, width), f32),
            pltpu.VMEM((2 * planes, own_rows // 2, width), bf16),
            dma((9,)),
            dma((5, planes - 1, 2)),
            dma((5, planes)),
            dma((3, 4 + FLIPS)),
            dma((3, groups)),
            dma((groups - 1,)),
            dma((groups,)),
            dma((2 * planes,)),
            dma((2 * planes,)),
            dma((2 * planes, FLIPS)),
            dma((2 * planes, FLIPS)),
            dma((2 * planes,)),
            dma((2, planes)),
        ],
        compiler_params=pltpu.CompilerParams(
            collective_id=0, has_side_effects=True, vmem_limit_bytes=64 * 1024 * 1024
        ),
        cost_estimate=pl.CostEstimate(
            flops=10**9, bytes_accessed=2 * 10**6, transcendentals=10**6
        ),
        name="attention_layer",
    )(
        hidden_states[0],
        norm_gain[None],
        norm_bias[None],
        query_weight,
        keyvalue_weight.T,
        out_weight,
        key_cache[0],
        value_cache[0],
        cache_length,
    )
    results = pl.pallas_call(
        hand_over,
        out_shape=tuple(
            jax.ShapeDtypeStruct((1,) + result.shape, bf16) for result in (out, new_key, new_value)
        ),
        in_specs=[hbm] * 3,
        out_specs=(hbm,) * 3,
        scratch_shapes=[dma((3,))],
        compiler_params=pltpu.CompilerParams(vmem_limit_bytes=64 * 1024 * 1024),
        name="hand_over",
    )(out, new_key, new_value)
    return tuple(results)


def device_program(mesh, *args):
    groups, planes = mesh.shape["gx"], mesh.shape["gy"]
    if groups == 2 * CHIPS and planes == 4:
        return fused(groups, planes, *args)
    return body(*args)


def solution(mesh):
    return jax.shard_map(
        functools.partial(device_program, mesh),
        mesh=mesh,
        in_specs=(
            P("gy", "gx", None),
            P(),
            P(),
            P("gy", "gx"),
            P("gy", "gx"),
            P("gx", "gy"),
            P("gy", "gx", None),
            P("gy", "gx", None),
            P("gy"),
        ),
        out_specs=(P("gy", "gx", None), P("gy", "gx", None), P("gy", "gx", None)),
        check_vma=False,
    )
```

```python
import functools
import math

import jax
import jax.numpy as jnp
from jax import lax
from jax.experimental import pallas as pl
from jax.experimental.pallas import tpu as pltpu
from jax.sharding import PartitionSpec as P

HEADS = 16


NEGATIVE = -1e30


def normalize(hidden_states, norm_gain, norm_bias):
    values = hidden_states.astype(jnp.float32)
    average = jnp.mean(values, axis=-1, keepdims=True)
    centred = values - average
    spread = jnp.mean(centred * centred, axis=-1, keepdims=True)
    return (centred * lax.rsqrt(spread + 1e-05) * norm_gain + norm_bias).astype(jnp.bfloat16)


def page_terms(query_rows, query_pos, key_rows, value_rows, page_size):
    row_count = query_rows.shape[0]
    head_dim = key_rows.shape[1]
    page_count = key_rows.shape[0] // page_size
    scores = lax.dot_general(
        query_rows, key_rows, (((1,), (1,)), ((), ())), preferred_element_type=jnp.float32
    )
    scores = (scores * head_dim ** (-0.5)).reshape(row_count, page_count, page_size)
    key_pos = jnp.arange(page_count * page_size, dtype=jnp.int32).reshape(page_count, page_size)
    allowed = key_pos[None, :, :] <= query_pos[:, None, None]
    maxima = jnp.max(jnp.where(allowed, scores, NEGATIVE), axis=2)
    weights = jnp.where(allowed, jnp.exp(scores - maxima[:, :, None]), 0.0)
    totals = jnp.sum(weights, axis=2)
    weighted = jnp.einsum(
        "rnp,npd->rnd",
        weights.astype(jnp.bfloat16),
        value_rows.reshape(page_count, page_size, head_dim),
        preferred_element_type=jnp.float32,
    )
    return (maxima, totals, weighted)


def reduce_pages(maxima, totals, weighted):
    largest = jnp.max(maxima, axis=1)
    factor = jnp.exp(maxima - largest[:, None])
    return (
        largest,
        jnp.sum(totals * factor, axis=1),
        jnp.sum(weighted * factor[:, :, None], axis=1),
    )


def join_pages(first, second):
    larger = jnp.maximum(first[0], second[0])
    second_factor = jnp.exp(second[0] - larger)
    return (larger, second[1] * second_factor, second[2] * second_factor[:, None])


def body(
    hidden_states,
    norm_gain,
    norm_bias,
    query_weight,
    keyvalue_weight,
    out_weight,
    key_cache,
    value_cache,
    cache_length,
):
    own_tokens = hidden_states.shape[1]
    groups = lax.axis_size("gx")
    column_index = lax.axis_index("gx")
    span_len = own_tokens * groups
    page_size = key_cache.shape[1]
    head_dim = key_cache.shape[2]
    head_count = HEADS
    head_width = head_count * head_dim
    normed = normalize(hidden_states[0], norm_gain, norm_bias)
    full_rows = lax.all_gather(normed, "gx", axis=0, tiled=True)
    pieces = (
        lax.all_gather(query_weight, "gy", axis=0, tiled=True),
        lax.all_gather(keyvalue_weight, "gy", axis=0, tiled=True),
    )
    query_part = jnp.dot(full_rows, pieces[0], preferred_element_type=jnp.float32)
    keyvalue_part = jnp.dot(full_rows, pieces[1], preferred_element_type=jnp.float32)
    query_local = query_part.astype(jnp.bfloat16)
    keyvalue_local = keyvalue_part.astype(jnp.bfloat16)
    queries, new_keyvalue = (
        lax.all_gather(query_local, "gx", axis=1, tiled=True),
        lax.all_gather(keyvalue_local, "gx", axis=1, tiled=True),
    )
    length = cache_length[0]
    page_base = column_index * page_size
    offsets = page_base + jnp.arange(page_size, dtype=jnp.int32) - length
    inside = (offsets >= 0) & (offsets < span_len)
    picked = jnp.take(new_keyvalue, jnp.clip(offsets, 0, span_len - 1), axis=0)
    key_page = jnp.where(inside[:, None], picked[:, :head_dim], key_cache[0])
    value_page = jnp.where(inside[:, None], picked[:, head_dim:], value_cache[0])
    own_rows = lax.dynamic_slice_in_dim(queries, column_index * own_tokens, own_tokens, 0)
    own_rows = own_rows.reshape(own_tokens * head_count, head_dim)
    own_pos = (
        length
        + column_index * own_tokens
        + jnp.arange(own_tokens * head_count, dtype=jnp.int32) // head_count
    )
    own_total = own_tokens * head_count
    empty = (
        jnp.full((own_total,), NEGATIVE, jnp.float32),
        jnp.zeros((own_total,), jnp.float32),
        jnp.zeros((own_total, head_dim), jnp.float32),
    )
    pieces = (
        lax.all_gather(key_page, "gx", axis=0, tiled=True),
        lax.all_gather(value_page, "gx", axis=0, tiled=True),
    )
    maxima, totals, weighted = page_terms(own_rows, own_pos, pieces[0], pieces[1], page_size)
    maxima, totals, weighted = join_pages(empty, reduce_pages(maxima, totals, weighted))
    own_out = (weighted / totals[:, None]).reshape(own_tokens, head_width).astype(jnp.bfloat16)
    attended = lax.all_to_all(own_out, "gx", split_axis=1, concat_axis=0, tiled=True)
    out_full = lax.all_gather(out_weight, "gy", axis=1, tiled=True)
    hidden_part = lax.psum_scatter(
        jnp.dot(attended, out_full, preferred_element_type=jnp.float32),
        "gx",
        scatter_dimension=0,
        tiled=True,
    )
    return (hidden_part.astype(jnp.bfloat16)[None], key_page[None], value_page[None])


MESH = pl.DeviceIdType.MESH
CHIPS = 4
FLIPS = 3


def fused_kernel(
    planes,
    hidden_ref,
    gain_ref,
    bias_ref,
    wq_ref,
    wkv_ref,
    wo_ref,
    key_ref,
    value_ref,
    length_ref,
    out_ref,
    new_key_ref,
    new_value_ref,
    hidden_in,
    gain_in,
    bias_in,
    normed,
    wq_all,
    wkv_all,
    wo_own,
    keys,
    values,
    new_kv,
    attended,
    partial,
    sibling_out,
    sibling_in,
    chip_out,
    chip_in,
    own_sum,
    pieces,
    load_sem,
    z_send,
    z_recv,
    rows_send,
    rows_recv,
    kv_send,
    kv_recv,
    sib_send,
    sib_recv,
    chip_send,
    chip_recv,
    home_send,
    home_recv,
):
    me = lax.axis_index("gx")
    z = lax.axis_index("gy")
    core = me % 2
    chip = me // 2
    cx = chip % 2
    cy = chip // 2
    sibling = chip * 2 + 1 - core
    other_chips = (cy * 2 + 1 - cx, (1 - cy) * 2 + cx, (1 - cy) * 2 + 1 - cx)
    peers = [other * 2 + core for other in other_chips]
    far = [other * 2 + 1 - core for other in other_chips]
    everyone = [sibling] + peers + far
    has_up = z < planes - 1
    has_down = z > 0

    barrier = pltpu.get_barrier_semaphore()
    for peer in everyone:
        pl.semaphore_signal(barrier, inc=1, device_id={"gx": peer}, device_id_type=MESH)

    other_planes = [lax.rem(z + k, planes) for k in range(1, planes)]
    for plane in other_planes:
        pl.semaphore_signal(barrier, inc=1, device_id={"gy": plane}, device_id_type=MESH)

    head_dim = key_ref.shape[1]
    head_columns = [wq_ref.at[:, pl.ds(head * head_dim, head_dim)] for head in range(2)]
    sources = [wkv_ref] + head_columns
    buffers = [wkv_all, wq_all.at[0], wq_all.at[1], attended.at[0], attended.at[1]]
    loads = [
        pltpu.make_async_copy(source, target, load_sem.at[slot])
        for slot, (source, target) in enumerate(
            [
                (hidden_ref, hidden_in),
                (gain_ref, gain_in),
                (bias_ref, bias_in),
                (key_ref, keys.at[me]),
                (value_ref, values.at[me]),
            ]
            + [(source, buffer.at[z]) for source, buffer in zip(sources, buffers)]
            + [(wo_ref, wo_own)]
        )
    ]
    for load in loads:
        load.start()

    pl.semaphore_wait(barrier, len(everyone) + planes - 1)

    def z_copy(kind, step, direction, own=False):
        shard = z - direction * step
        buffer = buffers[kind]
        return pltpu.make_async_remote_copy(
            src_ref=sources[kind] if own and kind < len(sources) else buffer.at[shard],
            dst_ref=buffer.at[shard],
            send_sem=z_send.at[kind, step, (direction + 1) // 2],
            recv_sem=z_recv.at[kind, shard],
            device_id={"gy": z + direction},
            device_id_type=MESH,
        )

    def z_cond(step, direction):
        if direction > 0:
            return has_up & (z - step >= 0)
        return has_down & (z + step < planes)

    def z_arrived(kind, shard):
        buffer = buffers[kind]
        pltpu.make_async_copy(buffer.at[shard], buffer.at[shard], z_recv.at[kind, shard]).wait()

    def z_forward(kind, step):
        for direction in (1, -1):

            @pl.when(z_cond(step, direction))
            def _(direction=direction):
                if step > 0:
                    z_arrived(kind, z - direction * step)
                z_copy(kind, step, direction, step == 0).start()

    def z_wait_send(kind, step):
        for direction in (1, -1):

            @pl.when(z_cond(step, direction))
            def _(direction=direction):
                z_copy(kind, step, direction, step == 0).wait_send()

    def z_last(kind, step):
        @pl.when((z == planes - 1) & (z - 1 - step >= 0))
        def _():
            z_arrived(kind, z - 1 - step)

        @pl.when((z == 0) & (z + 1 + step < planes))
        def _():
            z_arrived(kind, z + 1 + step)

    def second_start(step):
        for direction in (1, -1):
            last = z if direction > 0 else planes - 1 - z

            @pl.when(z_cond(0, direction) & (last == step))
            def _(direction=direction):
                z_copy(2, 0, direction, True).start()

    def z_take(kind, shard):
        z_arrived(kind, shard)

        @pl.when((shard < z) & has_up)
        def _():
            z_copy(kind, z - shard, 1).start()

        @pl.when((shard > z) & has_down)
        def _():
            z_copy(kind, shard - z, -1).start()

    gathered = (normed, keys, values)

    def row_copy(kind, block, target, slot):
        return pltpu.make_async_remote_copy(
            src_ref=gathered[kind].at[block],
            dst_ref=gathered[kind].at[block],
            send_sem=rows_send.at[kind, slot],
            recv_sem=rows_recv.at[kind, block],
            device_id={"gx": target},
            device_id_type=MESH,
        )

    def rows_start(kind):
        for slot, target in enumerate(peers + [sibling]):
            row_copy(kind, me, target, slot).start()

    def rows_wait(kind, block):
        pltpu.make_async_copy(
            gathered[kind].at[block], gathered[kind].at[block], rows_recv.at[kind, block]
        ).wait()

    def rows_forward(kind):
        for flip in range(FLIPS):
            rows_wait(kind, peers[flip])
            row_copy(kind, peers[flip], sibling, 4 + flip).start()

    def rows_finish(kind):
        for block in [sibling] + far:
            rows_wait(kind, block)

    for kind in range(2):
        z_forward(kind, 0)
    second_start(0)

    for slot in range(3):
        loads[slot].wait()
    rows = hidden_in[...].astype(jnp.float32)
    average = jnp.mean(rows, axis=-1, keepdims=True)
    centred = rows - average
    spread = jnp.mean(centred * centred, axis=-1, keepdims=True)
    normed[me] = (
        centred * lax.rsqrt(spread + 1e-05) * gain_in[...] + bias_in[...]
    ).astype(jnp.bfloat16)
    rows_start(0)
    for kind in (1, 2):
        loads[kind + 2].wait()
        rows_start(kind)

    z_forward(0, 1)
    z_forward(0, 2)
    z_forward(1, 1)
    second_start(1)
    rows_forward(0)
    z_forward(1, 2)
    second_start(2)
    rows_finish(0)
    loads[5].wait()
    for step in range(planes - 1):
        z_last(0, step)

    tokens = normed[...].reshape(-1, normed.shape[2])
    token_count = tokens.shape[0]
    depth = wq_all.shape[2]
    kv_width = wkv_all.shape[1]
    kv_part = jnp.zeros((kv_width, token_count), jnp.float32)
    for part in range(planes):
        kv_part += lax.dot_general(
            wkv_all[part],
            tokens[:, part * depth : (part + 1) * depth],
            (((1,), (1,)), ((), ())),
            preferred_element_type=jnp.float32,
        )
    new_kv[me] = kv_part.astype(jnp.bfloat16)

    def kv_copy(block, target, slot):
        return pltpu.make_async_remote_copy(
            src_ref=new_kv.at[block],
            dst_ref=new_kv.at[block],
            send_sem=kv_send.at[slot],
            recv_sem=kv_recv.at[block],
            device_id={"gx": target},
            device_id_type=MESH,
        )

    for slot, target in enumerate(everyone):
        kv_copy(me, target, slot).start()

    rows_forward(1)
    rows_forward(2)
    z_forward(2, 1)

    for block in everyone:
        pltpu.make_async_copy(new_kv.at[block], new_kv.at[block], kv_recv.at[block]).wait()

    length = length_ref[0]
    page = key_ref.shape[0]
    kv_cols = new_kv[...].reshape(2 * head_dim, token_count)
    offsets = (
        lax.broadcasted_iota(jnp.int32, (page, token_count), 0) + me * page - length
    )
    chosen = offsets == lax.broadcasted_iota(jnp.int32, (page, token_count), 1)
    picked = lax.dot_general(
        jnp.where(chosen, 1.0, 0.0).astype(jnp.bfloat16),
        kv_cols,
        (((1,), (1,)), ((), ())),
        preferred_element_type=jnp.float32,
    )
    row_offset = lax.broadcasted_iota(jnp.int32, (page, head_dim), 0) + me * page - length
    inside = (row_offset >= 0) & (row_offset < token_count)
    new_key_ref[...] = jnp.where(
        inside, picked[:, :head_dim], keys[me].astype(jnp.float32)
    ).astype(jnp.bfloat16)
    new_value_ref[...] = jnp.where(
        inside, picked[:, head_dim:], values[me].astype(jnp.float32)
    ).astype(jnp.bfloat16)

    rows_finish(1)
    rows_finish(2)
    def queries(head):
        loads[6 + head].wait()
        for step in range(planes - 1):
            z_last(1 + head, step)
        query = jnp.zeros((token_count, head_dim), jnp.float32)
        for part in range(planes):
            query += jnp.dot(
                normed[:, :, part * depth : (part + 1) * depth].reshape(token_count, depth),
                wq_all[head, part],
                preferred_element_type=jnp.float32,
            )
        return query.astype(jnp.bfloat16)

    cached = keys.shape[0] * page - token_count
    block_rows = token_count
    scale = head_dim ** (-0.5) * math.log2(math.e)

    def attend(q):
        old_keys = keys[...].reshape(-1, head_dim)[:cached]
        old_values = values[...].reshape(-1, head_dim)[:cached]
        fresh = new_kv[...].reshape(2 * head_dim, token_count)
        old_pos = lax.broadcasted_iota(jnp.int32, (1, cached), 1)
        hidden = jnp.where(old_pos < length, 0.0, NEGATIVE)
        old = lax.dot_general(
            q, old_keys, (((1,), (1,)), ((), ())), preferred_element_type=jnp.float32
        )
        old = old * scale + hidden
        row = lax.broadcasted_iota(jnp.int32, (block_rows, token_count), 0)
        col = lax.broadcasted_iota(jnp.int32, (block_rows, token_count), 1)
        new = jnp.dot(q, fresh[:head_dim], preferred_element_type=jnp.float32)
        new = jnp.where(col <= row, new * scale, NEGATIVE)
        top = jnp.maximum(
            jnp.max(old, axis=1, keepdims=True), jnp.max(new, axis=1, keepdims=True)
        )
        old = jnp.exp2(old - top)
        new = jnp.exp2(new - top)
        total = jnp.sum(old, axis=1, keepdims=True) + jnp.sum(new, axis=1, keepdims=True)
        summed = jnp.dot(
            old.astype(jnp.bfloat16), old_values, preferred_element_type=jnp.float32
        ) + lax.dot_general(
            new.astype(jnp.bfloat16),
            fresh[head_dim:],
            (((1,), (1,)), ((), ())),
            preferred_element_type=jnp.float32,
        )
        return (summed / total).astype(jnp.bfloat16)

    for head in range(2):
        attended[head, z] = attend(queries(head))
        z_forward(3 + head, 0)
        if head == 0:
            z_forward(2, 2)

    own_rows = hidden_ref.shape[0]
    width = wo_own.shape[1]

    def sib_copy(n):
        return pltpu.make_async_remote_copy(
            src_ref=sibling_out.at[n],
            dst_ref=sibling_in.at[n],
            send_sem=sib_send.at[n],
            recv_sem=sib_recv.at[n],
            device_id={"gx": sibling},
            device_id_type=MESH,
        )

    def chip_copy(n, flip):
        return pltpu.make_async_remote_copy(
            src_ref=chip_out.at[n, flip],
            dst_ref=chip_in.at[n, flip],
            send_sem=chip_send.at[n, flip],
            recv_sem=chip_recv.at[n, flip],
            device_id={"gx": peers[flip]},
            device_id_type=MESH,
        )

    def head_product(n, head):
        return jnp.dot(
            attended[head, order[n]],
            wo_own[head * head_dim : (head + 1) * head_dim, :],
            preferred_element_type=jnp.float32,
        ).reshape(2 * CHIPS, own_rows, width)

    def project(n):
        partial[n] += head_product(n, 1)
        for k in range(CHIPS):
            sibling_out[n, k] = partial[n, 2 * k + 1 - core].astype(jnp.bfloat16)
        sib_copy(n).start()

    def spread_sums(n):
        sib_copy(n).wait_recv()
        for flip in range(FLIPS):
            other = other_chips[flip]
            chip_out[n, flip] = (
                partial[n, 2 * other + core] + sibling_in[n, other].astype(jnp.float32)
            ).astype(jnp.bfloat16)
            chip_copy(n, flip).start()
        own_sum[n] = partial[n, me] + sibling_in[n, chip].astype(jnp.float32)

    low = z < planes // 2
    order = [z, jnp.where(low, z + 1, z - 1)]
    order.append(jnp.where(low, (z + planes - 1) % planes, (z + 1) % planes))
    order[2] = jnp.where((z == 0) | (z == planes - 1), jnp.where(low, 2, planes - 3), order[2])
    order.append(jnp.where(low, planes - 1, 0))

    def home_copy(n, plane):
        return pltpu.make_async_remote_copy(
            src_ref=pieces.at[n],
            dst_ref=out_ref.at[:, pl.ds(pl.multiple_of(z * width, width), width)],
            send_sem=home_send.at[n],
            recv_sem=home_recv.at[z],
            device_id={"gy": plane},
            device_id_type=MESH,
        )

    def finish(n):
        total = own_sum[n]
        for flip in range(FLIPS):
            chip_copy(n, flip).wait_recv()
            total += chip_in[n, flip].astype(jnp.float32)
        piece = total.astype(jnp.bfloat16)
        if n == 0:
            out_ref[:, pl.ds(pl.multiple_of(z * width, width), width)] = piece
        else:
            pieces[n] = piece
            home_copy(n, order[n]).start()

    loads[8].wait()
    for n in range(planes):
        if n > 0:
            z_take(3, order[n])
        partial[n] = head_product(n, 0)
    for n in range(planes):
        if n > 0:
            z_take(4, order[n])
        project(n)
        if n > 0:
            finish(n - 1)
        spread_sums(n)
    finish(planes - 1)
    for plane in other_planes:
        landed = out_ref.at[:, pl.ds(pl.multiple_of(plane * width, width), width)]
        pltpu.make_async_copy(landed, landed, home_recv.at[plane]).wait()

    for n in range(1, planes):
        home_copy(n, order[n]).wait_send()
    for kind in range(5):
        for step in range(planes - 1):
            z_wait_send(kind, step)
    for kind in range(3):
        for slot, target in enumerate(peers + [sibling]):
            row_copy(kind, me, target, slot).wait_send()
        for flip in range(FLIPS):
            row_copy(kind, peers[flip], sibling, 4 + flip).wait_send()
    for slot, target in enumerate(everyone):
        kv_copy(me, target, slot).wait_send()
    for n in range(planes):
        sib_copy(n).wait_send()
        for flip in range(FLIPS):
            chip_copy(n, flip).wait_send()


def hand_over(out_ref, key_ref, value_ref, out_to, key_to, value_to):
    out_to[0] = out_ref[...]
    key_to[0] = key_ref[...]
    value_to[0] = value_ref[...]


def fused(
    groups,
    planes,
    hidden_states,
    norm_gain,
    norm_bias,
    query_weight,
    keyvalue_weight,
    out_weight,
    key_cache,
    value_cache,
    cache_length,
):
    own_rows, model = hidden_states.shape[1:]
    page, head_dim = key_cache.shape[1:]
    span = own_rows * groups
    depth, columns = query_weight.shape
    kv_width = keyvalue_weight.shape[1]
    out_rows, width = out_weight.shape
    heads = columns // head_dim
    bf16, f32 = jnp.bfloat16, jnp.float32
    vmem = pl.BlockSpec(memory_space=pltpu.VMEM)
    hbm = pl.BlockSpec(memory_space=pltpu.HBM)
    dma = pltpu.SemaphoreType.DMA
    out, new_key, new_value = pl.pallas_call(
        functools.partial(fused_kernel, planes),
        out_shape=(
            jax.ShapeDtypeStruct((own_rows, model), bf16),
            jax.ShapeDtypeStruct((page, head_dim), bf16),
            jax.ShapeDtypeStruct((page, head_dim), bf16),
        ),
        in_specs=[hbm] * 8 + [pl.BlockSpec(memory_space=pltpu.SMEM)],
        out_specs=(vmem, vmem, vmem),
        scratch_shapes=[
            pltpu.VMEM((own_rows, model), bf16),
            pltpu.VMEM((1, model), f32),
            pltpu.VMEM((1, model), f32),
            pltpu.VMEM((groups, own_rows, model), bf16),
            pltpu.VMEM((heads, planes, depth, head_dim), bf16),
            pltpu.VMEM((planes, kv_width, depth), bf16),
            pltpu.VMEM((out_rows, width), bf16),
            pltpu.VMEM((groups, page, head_dim), bf16),
            pltpu.VMEM((groups, page, head_dim), bf16),
            pltpu.VMEM((groups, kv_width, span), bf16),
            pltpu.VMEM((heads, planes, span, head_dim), bf16),
            pltpu.VMEM((planes, 2 * CHIPS, own_rows, width), f32),
            pltpu.VMEM((planes, CHIPS, own_rows, width), bf16),
            pltpu.VMEM((planes, CHIPS, own_rows, width), bf16),
            pltpu.VMEM((planes, FLIPS, own_rows, width), bf16),
            pltpu.VMEM((planes, FLIPS, own_rows, width), bf16),
            pltpu.VMEM((planes, own_rows, width), f32),
            pltpu.VMEM((planes, own_rows, width), bf16),
            dma((9,)),
            dma((5, planes - 1, 2)),
            dma((5, planes)),
            dma((3, 4 + FLIPS)),
            dma((3, groups)),
            dma((groups - 1,)),
            dma((groups,)),
            dma((planes,)),
            dma((planes,)),
            dma((planes, FLIPS)),
            dma((planes, FLIPS)),
            dma((planes,)),
            dma((planes,)),
        ],
        compiler_params=pltpu.CompilerParams(
            collective_id=0, has_side_effects=True, vmem_limit_bytes=64 * 1024 * 1024
        ),
        cost_estimate=pl.CostEstimate(
            flops=10**9, bytes_accessed=2 * 10**6, transcendentals=10**6
        ),
        name="attention_layer",
    )(
        hidden_states[0],
        norm_gain[None],
        norm_bias[None],
        query_weight,
        keyvalue_weight.T,
        out_weight,
        key_cache[0],
        value_cache[0],
        cache_length,
    )
    results = pl.pallas_call(
        hand_over,
        out_shape=tuple(
            jax.ShapeDtypeStruct((1,) + result.shape, bf16) for result in (out, new_key, new_value)
        ),
        in_specs=[vmem] * 3,
        out_specs=(vmem,) * 3,
        compiler_params=pltpu.CompilerParams(vmem_limit_bytes=64 * 1024 * 1024),
        name="hand_over",
    )(out, new_key, new_value)
    return tuple(results)


def device_program(mesh, *args):
    groups, planes = mesh.shape["gx"], mesh.shape["gy"]
    if groups == 2 * CHIPS and planes == 4:
        return fused(groups, planes, *args)
    return body(*args)


def solution(mesh):
    return jax.shard_map(
        functools.partial(device_program, mesh),
        mesh=mesh,
        in_specs=(
            P("gy", "gx", None),
            P(),
            P(),
            P("gy", "gx"),
            P("gy", "gx"),
            P("gx", "gy"),
            P("gy", "gx", None),
            P("gy", "gx", None),
            P("gy"),
        ),
        out_specs=(P("gy", "gx", None), P("gy", "gx", None), P("gy", "gx", None)),
        check_vma=False,
    )
```

```python
import functools
import math

import jax
import jax.numpy as jnp
from jax import lax
from jax.experimental import pallas as pl
from jax.experimental.pallas import tpu as pltpu
from jax.sharding import PartitionSpec as P

HEADS = 16


NEGATIVE = -1e30


def normalize(hidden_states, norm_gain, norm_bias):
    values = hidden_states.astype(jnp.float32)
    average = jnp.mean(values, axis=-1, keepdims=True)
    centred = values - average
    spread = jnp.mean(centred * centred, axis=-1, keepdims=True)
    return (centred * lax.rsqrt(spread + 1e-05) * norm_gain + norm_bias).astype(jnp.bfloat16)


def page_terms(query_rows, query_pos, key_rows, value_rows, page_size):
    row_count = query_rows.shape[0]
    head_dim = key_rows.shape[1]
    page_count = key_rows.shape[0] // page_size
    scores = lax.dot_general(
        query_rows, key_rows, (((1,), (1,)), ((), ())), preferred_element_type=jnp.float32
    )
    scores = (scores * head_dim ** (-0.5)).reshape(row_count, page_count, page_size)
    key_pos = jnp.arange(page_count * page_size, dtype=jnp.int32).reshape(page_count, page_size)
    allowed = key_pos[None, :, :] <= query_pos[:, None, None]
    maxima = jnp.max(jnp.where(allowed, scores, NEGATIVE), axis=2)
    weights = jnp.where(allowed, jnp.exp(scores - maxima[:, :, None]), 0.0)
    totals = jnp.sum(weights, axis=2)
    weighted = jnp.einsum(
        "rnp,npd->rnd",
        weights.astype(jnp.bfloat16),
        value_rows.reshape(page_count, page_size, head_dim),
        preferred_element_type=jnp.float32,
    )
    return (maxima, totals, weighted)


def reduce_pages(maxima, totals, weighted):
    largest = jnp.max(maxima, axis=1)
    factor = jnp.exp(maxima - largest[:, None])
    return (
        largest,
        jnp.sum(totals * factor, axis=1),
        jnp.sum(weighted * factor[:, :, None], axis=1),
    )


def join_pages(first, second):
    larger = jnp.maximum(first[0], second[0])
    second_factor = jnp.exp(second[0] - larger)
    return (larger, second[1] * second_factor, second[2] * second_factor[:, None])


def body(
    hidden_states,
    norm_gain,
    norm_bias,
    query_weight,
    keyvalue_weight,
    out_weight,
    key_cache,
    value_cache,
    cache_length,
):
    own_tokens = hidden_states.shape[1]
    groups = lax.axis_size("gx")
    column_index = lax.axis_index("gx")
    span_len = own_tokens * groups
    page_size = key_cache.shape[1]
    head_dim = key_cache.shape[2]
    head_count = HEADS
    head_width = head_count * head_dim
    normed = normalize(hidden_states[0], norm_gain, norm_bias)
    full_rows = lax.all_gather(normed, "gx", axis=0, tiled=True)
    pieces = (
        lax.all_gather(query_weight, "gy", axis=0, tiled=True),
        lax.all_gather(keyvalue_weight, "gy", axis=0, tiled=True),
    )
    query_part = jnp.dot(full_rows, pieces[0], preferred_element_type=jnp.float32)
    keyvalue_part = jnp.dot(full_rows, pieces[1], preferred_element_type=jnp.float32)
    query_local = query_part.astype(jnp.bfloat16)
    keyvalue_local = keyvalue_part.astype(jnp.bfloat16)
    queries, new_keyvalue = (
        lax.all_gather(query_local, "gx", axis=1, tiled=True),
        lax.all_gather(keyvalue_local, "gx", axis=1, tiled=True),
    )
    length = cache_length[0]
    page_base = column_index * page_size
    offsets = page_base + jnp.arange(page_size, dtype=jnp.int32) - length
    inside = (offsets >= 0) & (offsets < span_len)
    picked = jnp.take(new_keyvalue, jnp.clip(offsets, 0, span_len - 1), axis=0)
    key_page = jnp.where(inside[:, None], picked[:, :head_dim], key_cache[0])
    value_page = jnp.where(inside[:, None], picked[:, head_dim:], value_cache[0])
    own_rows = lax.dynamic_slice_in_dim(queries, column_index * own_tokens, own_tokens, 0)
    own_rows = own_rows.reshape(own_tokens * head_count, head_dim)
    own_pos = (
        length
        + column_index * own_tokens
        + jnp.arange(own_tokens * head_count, dtype=jnp.int32) // head_count
    )
    own_total = own_tokens * head_count
    empty = (
        jnp.full((own_total,), NEGATIVE, jnp.float32),
        jnp.zeros((own_total,), jnp.float32),
        jnp.zeros((own_total, head_dim), jnp.float32),
    )
    pieces = (
        lax.all_gather(key_page, "gx", axis=0, tiled=True),
        lax.all_gather(value_page, "gx", axis=0, tiled=True),
    )
    maxima, totals, weighted = page_terms(own_rows, own_pos, pieces[0], pieces[1], page_size)
    maxima, totals, weighted = join_pages(empty, reduce_pages(maxima, totals, weighted))
    own_out = (weighted / totals[:, None]).reshape(own_tokens, head_width).astype(jnp.bfloat16)
    attended = lax.all_to_all(own_out, "gx", split_axis=1, concat_axis=0, tiled=True)
    out_full = lax.all_gather(out_weight, "gy", axis=1, tiled=True)
    hidden_part = lax.psum_scatter(
        jnp.dot(attended, out_full, preferred_element_type=jnp.float32),
        "gx",
        scatter_dimension=0,
        tiled=True,
    )
    return (hidden_part.astype(jnp.bfloat16)[None], key_page[None], value_page[None])


MESH = pl.DeviceIdType.MESH
CHIPS = 4
FLIPS = 3


def fused_kernel(
    planes,
    hidden_ref,
    gain_ref,
    bias_ref,
    wq_ref,
    wkv_ref,
    wo_ref,
    key_ref,
    value_ref,
    length_ref,
    out_ref,
    new_key_ref,
    new_value_ref,
    hidden_in,
    gain_in,
    bias_in,
    normed,
    wq_all,
    wkv_all,
    wo_own,
    keys,
    values,
    new_kv,
    attended,
    keys_turned,
    hidden_row,
    scores,
    partial,
    sibling_out,
    sibling_in,
    chip_out,
    chip_in,
    own_sum,
    pieces,
    load_sem,
    z_send,
    z_recv,
    rows_send,
    rows_recv,
    kv_send,
    kv_recv,
    sib_send,
    sib_recv,
    chip_send,
    chip_recv,
    home_send,
    home_recv,
):
    me = lax.axis_index("gx")
    z = lax.axis_index("gy")
    core = me % 2
    chip = me // 2
    cx = chip % 2
    cy = chip // 2
    sibling = chip * 2 + 1 - core
    other_chips = (cy * 2 + 1 - cx, (1 - cy) * 2 + cx, (1 - cy) * 2 + 1 - cx)
    peers = [other * 2 + core for other in other_chips]
    far = [other * 2 + 1 - core for other in other_chips]
    everyone = [sibling] + peers + far
    has_up = z < planes - 1
    has_down = z > 0

    barrier = pltpu.get_barrier_semaphore()
    for peer in everyone:
        pl.semaphore_signal(barrier, inc=1, device_id={"gx": peer}, device_id_type=MESH)

    other_planes = [lax.rem(z + k, planes) for k in range(1, planes)]
    for plane in other_planes:
        pl.semaphore_signal(barrier, inc=1, device_id={"gy": plane}, device_id_type=MESH)

    head_dim = key_ref.shape[1]
    head_columns = [wq_ref.at[:, pl.ds(head * head_dim, head_dim)] for head in range(2)]
    sources = [wkv_ref] + head_columns
    buffers = [wkv_all, wq_all.at[0], wq_all.at[1], attended.at[0], attended.at[1]]
    loads = [
        pltpu.make_async_copy(source, target, load_sem.at[slot])
        for slot, (source, target) in enumerate(
            [
                (hidden_ref, hidden_in),
                (gain_ref, gain_in),
                (bias_ref, bias_in),
                (key_ref, keys.at[me]),
                (value_ref, values.at[me]),
            ]
            + [(source, buffer.at[z]) for source, buffer in zip(sources, buffers)]
            + [(wo_ref, wo_own)]
        )
    ]
    for load in loads:
        load.start()

    pl.semaphore_wait(barrier, len(everyone) + planes - 1)

    def z_copy(kind, step, direction, own=False):
        shard = z - direction * step
        buffer = buffers[kind]
        return pltpu.make_async_remote_copy(
            src_ref=sources[kind] if own and kind < len(sources) else buffer.at[shard],
            dst_ref=buffer.at[shard],
            send_sem=z_send.at[kind, step, (direction + 1) // 2],
            recv_sem=z_recv.at[kind, shard],
            device_id={"gy": z + direction},
            device_id_type=MESH,
        )

    def z_cond(step, direction):
        if direction > 0:
            return has_up & (z - step >= 0)
        return has_down & (z + step < planes)

    def z_arrived(kind, shard):
        buffer = buffers[kind]
        pltpu.make_async_copy(buffer.at[shard], buffer.at[shard], z_recv.at[kind, shard]).wait()

    def z_forward(kind, step):
        for direction in (1, -1):

            @pl.when(z_cond(step, direction))
            def _(direction=direction):
                if step > 0:
                    z_arrived(kind, z - direction * step)
                z_copy(kind, step, direction, step == 0).start()

    def z_wait_send(kind, step):
        for direction in (1, -1):

            @pl.when(z_cond(step, direction))
            def _(direction=direction):
                z_copy(kind, step, direction, step == 0).wait_send()

    def z_last(kind, step):
        @pl.when((z == planes - 1) & (z - 1 - step >= 0))
        def _():
            z_arrived(kind, z - 1 - step)

        @pl.when((z == 0) & (z + 1 + step < planes))
        def _():
            z_arrived(kind, z + 1 + step)

    def second_start(step):
        for direction in (1, -1):
            last = z if direction > 0 else planes - 1 - z

            @pl.when(z_cond(0, direction) & (last == step))
            def _(direction=direction):
                z_copy(2, 0, direction, True).start()

    def z_take(kind, shard):
        z_arrived(kind, shard)

        @pl.when((shard < z) & has_up)
        def _():
            z_copy(kind, z - shard, 1).start()

        @pl.when((shard > z) & has_down)
        def _():
            z_copy(kind, shard - z, -1).start()

    gathered = (normed, keys, values)

    def row_copy(kind, block, target, slot):
        return pltpu.make_async_remote_copy(
            src_ref=gathered[kind].at[block],
            dst_ref=gathered[kind].at[block],
            send_sem=rows_send.at[kind, slot],
            recv_sem=rows_recv.at[kind, block],
            device_id={"gx": target},
            device_id_type=MESH,
        )

    def rows_start(kind):
        for slot, target in enumerate(peers + [sibling]):
            row_copy(kind, me, target, slot).start()

    def rows_wait(kind, block):
        pltpu.make_async_copy(
            gathered[kind].at[block], gathered[kind].at[block], rows_recv.at[kind, block]
        ).wait()

    def rows_forward(kind):
        for flip in range(FLIPS):
            rows_wait(kind, peers[flip])
            row_copy(kind, peers[flip], sibling, 4 + flip).start()

    def rows_finish(kind):
        for block in [sibling] + far:
            rows_wait(kind, block)

    for kind in range(2):
        z_forward(kind, 0)
    second_start(0)

    for slot in range(3):
        loads[slot].wait()
    rows = hidden_in[...].astype(jnp.float32)
    average = jnp.mean(rows, axis=-1, keepdims=True)
    centred = rows - average
    spread = jnp.mean(centred * centred, axis=-1, keepdims=True)
    normed[me] = (
        centred * lax.rsqrt(spread + 1e-05) * gain_in[...] + bias_in[...]
    ).astype(jnp.bfloat16)
    rows_start(0)
    for kind in (1, 2):
        loads[kind + 2].wait()
        rows_start(kind)

    z_forward(0, 1)
    z_forward(0, 2)
    z_forward(1, 1)
    second_start(1)
    rows_forward(0)
    z_forward(1, 2)
    second_start(2)
    rows_finish(0)
    loads[5].wait()
    for step in range(planes - 1):
        z_last(0, step)

    tokens = normed[...].reshape(-1, normed.shape[2])
    token_count = tokens.shape[0]
    depth = wq_all.shape[2]
    kv_width = wkv_all.shape[1]
    kv_part = jnp.zeros((kv_width, token_count), jnp.float32)
    for part in range(planes):
        kv_part += lax.dot_general(
            wkv_all[part],
            tokens[:, part * depth : (part + 1) * depth],
            (((1,), (1,)), ((), ())),
            preferred_element_type=jnp.float32,
        )
    new_kv[me] = kv_part.astype(jnp.bfloat16)

    def kv_copy(block, target, slot):
        return pltpu.make_async_remote_copy(
            src_ref=new_kv.at[block],
            dst_ref=new_kv.at[block],
            send_sem=kv_send.at[slot],
            recv_sem=kv_recv.at[block],
            device_id={"gx": target},
            device_id_type=MESH,
        )

    for slot, target in enumerate(everyone):
        kv_copy(me, target, slot).start()

    rows_forward(1)
    rows_forward(2)
    z_forward(2, 1)

    for block in everyone:
        pltpu.make_async_copy(new_kv.at[block], new_kv.at[block], kv_recv.at[block]).wait()

    length = length_ref[0]
    page = key_ref.shape[0]
    kv_cols = new_kv[...].reshape(2 * head_dim, token_count)
    offsets = (
        lax.broadcasted_iota(jnp.int32, (page, token_count), 0) + me * page - length
    )
    chosen = offsets == lax.broadcasted_iota(jnp.int32, (page, token_count), 1)
    picked = lax.dot_general(
        jnp.where(chosen, 1.0, 0.0).astype(jnp.bfloat16),
        kv_cols,
        (((1,), (1,)), ((), ())),
        preferred_element_type=jnp.float32,
    )
    row_offset = lax.broadcasted_iota(jnp.int32, (page, head_dim), 0) + me * page - length
    inside = (row_offset >= 0) & (row_offset < token_count)
    new_key_ref[...] = jnp.where(
        inside, picked[:, :head_dim], keys[me].astype(jnp.float32)
    ).astype(jnp.bfloat16)
    new_value_ref[...] = jnp.where(
        inside, picked[:, head_dim:], values[me].astype(jnp.float32)
    ).astype(jnp.bfloat16)

    rows_finish(1)
    rows_finish(2)
    def queries(head):
        loads[6 + head].wait()
        for step in range(planes - 1):
            z_last(1 + head, step)
        query = jnp.zeros((token_count, head_dim), jnp.float32)
        for part in range(planes):
            query += jnp.dot(
                normed[:, :, part * depth : (part + 1) * depth].reshape(token_count, depth),
                wq_all[head, part],
                preferred_element_type=jnp.float32,
            )
        return query.astype(jnp.bfloat16)

    cached = keys.shape[0] * page - token_count
    chunk = token_count
    chunks = cached // chunk
    scale = head_dim ** (-0.5) * math.log2(math.e)
    lanes = 128
    keys_turned[...] = (
        keys[...].reshape(-1, head_dim)[:cached].astype(jnp.float32).T.astype(jnp.bfloat16)
    )
    old_pos = lax.broadcasted_iota(jnp.int32, hidden_row.shape, 1)
    hidden_row[...] = jnp.where(old_pos < length, 0.0, NEGATIVE)

    def attend(q):
        running = None
        for c in range(chunks + 1):
            if c < chunks:
                part = jnp.dot(
                    q,
                    keys_turned[:, c * chunk : (c + 1) * chunk],
                    preferred_element_type=jnp.float32,
                )
                part = part * scale + hidden_row[:1, c * chunk : (c + 1) * chunk]
            else:
                part = jnp.dot(
                    q,
                    new_kv[...].reshape(2 * head_dim, token_count)[:head_dim],
                    preferred_element_type=jnp.float32,
                )
                row = lax.broadcasted_iota(jnp.int32, part.shape, 0) % token_count
                col = lax.broadcasted_iota(jnp.int32, part.shape, 1)
                part = jnp.where(col <= row, part * scale, NEGATIVE)
            scores[c] = part
            for first in range(0, chunk, lanes):
                piece = part[:, first : first + lanes]
                running = piece if running is None else jnp.maximum(running, piece)
        top = jnp.max(running, axis=1, keepdims=True)
        total = jnp.zeros((q.shape[0], lanes), jnp.float32)
        summed = jnp.zeros((q.shape[0], head_dim), jnp.float32)
        for c in range(chunks + 1):
            probs = jnp.exp2(scores[c] - top)
            for first in range(0, chunk, lanes):
                total += probs[:, first : first + lanes]
            if c < chunks:
                summed += jnp.dot(
                    probs.astype(jnp.bfloat16),
                    values[...].reshape(-1, head_dim)[c * chunk : (c + 1) * chunk],
                    preferred_element_type=jnp.float32,
                )
            else:
                summed += lax.dot_general(
                    probs.astype(jnp.bfloat16),
                    new_kv[...].reshape(2 * head_dim, token_count)[head_dim:],
                    (((1,), (1,)), ((), ())),
                    preferred_element_type=jnp.float32,
                )
        return (summed / jnp.sum(total, axis=1, keepdims=True)).astype(jnp.bfloat16)

    for head in range(2):
        attended[head, z] = attend(queries(head))
        z_forward(3 + head, 0)
        if head == 0:
            z_forward(2, 2)

    own_rows = hidden_ref.shape[0]
    width = wo_own.shape[1]

    def sib_copy(n):
        return pltpu.make_async_remote_copy(
            src_ref=sibling_out.at[n],
            dst_ref=sibling_in.at[n],
            send_sem=sib_send.at[n],
            recv_sem=sib_recv.at[n],
            device_id={"gx": sibling},
            device_id_type=MESH,
        )

    def chip_copy(n, flip):
        return pltpu.make_async_remote_copy(
            src_ref=chip_out.at[n, flip],
            dst_ref=chip_in.at[n, flip],
            send_sem=chip_send.at[n, flip],
            recv_sem=chip_recv.at[n, flip],
            device_id={"gx": peers[flip]},
            device_id_type=MESH,
        )

    def head_product(n, head):
        return jnp.dot(
            attended[head, order[n]],
            wo_own[head * head_dim : (head + 1) * head_dim, :],
            preferred_element_type=jnp.float32,
        ).reshape(2 * CHIPS, own_rows, width)

    def project(n):
        partial[n] += head_product(n, 1)
        for k in range(CHIPS):
            sibling_out[n, k] = partial[n, 2 * k + 1 - core].astype(jnp.bfloat16)
        sib_copy(n).start()

    def spread_sums(n):
        sib_copy(n).wait_recv()
        for flip in range(FLIPS):
            other = other_chips[flip]
            chip_out[n, flip] = (
                partial[n, 2 * other + core] + sibling_in[n, other].astype(jnp.float32)
            ).astype(jnp.bfloat16)
            chip_copy(n, flip).start()
        own_sum[n] = partial[n, me] + sibling_in[n, chip].astype(jnp.float32)

    low = z < planes // 2
    order = [z, jnp.where(low, z + 1, z - 1)]
    order.append(jnp.where(low, (z + planes - 1) % planes, (z + 1) % planes))
    order[2] = jnp.where((z == 0) | (z == planes - 1), jnp.where(low, 2, planes - 3), order[2])
    order.append(jnp.where(low, planes - 1, 0))

    def home_copy(n, plane):
        return pltpu.make_async_remote_copy(
            src_ref=pieces.at[n],
            dst_ref=out_ref.at[:, pl.ds(pl.multiple_of(z * width, width), width)],
            send_sem=home_send.at[n],
            recv_sem=home_recv.at[z],
            device_id={"gy": plane},
            device_id_type=MESH,
        )

    def finish(n):
        total = own_sum[n]
        for flip in range(FLIPS):
            chip_copy(n, flip).wait_recv()
            total += chip_in[n, flip].astype(jnp.float32)
        piece = total.astype(jnp.bfloat16)
        if n == 0:
            out_ref[:, pl.ds(pl.multiple_of(z * width, width), width)] = piece
        else:
            pieces[n] = piece
            home_copy(n, order[n]).start()

    loads[8].wait()
    for n in range(planes):
        if n > 0:
            z_take(3, order[n])
        partial[n] = head_product(n, 0)
    for n in range(planes):
        if n > 0:
            z_take(4, order[n])
        project(n)
        if n > 0:
            finish(n - 1)
        spread_sums(n)
    finish(planes - 1)
    for plane in other_planes:
        landed = out_ref.at[:, pl.ds(pl.multiple_of(plane * width, width), width)]
        pltpu.make_async_copy(landed, landed, home_recv.at[plane]).wait()

    for n in range(1, planes):
        home_copy(n, order[n]).wait_send()
    for kind in range(5):
        for step in range(planes - 1):
            z_wait_send(kind, step)
    for kind in range(3):
        for slot, target in enumerate(peers + [sibling]):
            row_copy(kind, me, target, slot).wait_send()
        for flip in range(FLIPS):
            row_copy(kind, peers[flip], sibling, 4 + flip).wait_send()
    for slot, target in enumerate(everyone):
        kv_copy(me, target, slot).wait_send()
    for n in range(planes):
        sib_copy(n).wait_send()
        for flip in range(FLIPS):
            chip_copy(n, flip).wait_send()


def hand_over(out_ref, key_ref, value_ref, out_to, key_to, value_to):
    out_to[0] = out_ref[...]
    key_to[0] = key_ref[...]
    value_to[0] = value_ref[...]


def fused(
    groups,
    planes,
    hidden_states,
    norm_gain,
    norm_bias,
    query_weight,
    keyvalue_weight,
    out_weight,
    key_cache,
    value_cache,
    cache_length,
):
    own_rows, model = hidden_states.shape[1:]
    page, head_dim = key_cache.shape[1:]
    span = own_rows * groups
    depth, columns = query_weight.shape
    kv_width = keyvalue_weight.shape[1]
    out_rows, width = out_weight.shape
    heads = columns // head_dim
    bf16, f32 = jnp.bfloat16, jnp.float32
    vmem = pl.BlockSpec(memory_space=pltpu.VMEM)
    hbm = pl.BlockSpec(memory_space=pltpu.HBM)
    dma = pltpu.SemaphoreType.DMA
    out, new_key, new_value = pl.pallas_call(
        functools.partial(fused_kernel, planes),
        out_shape=(
            jax.ShapeDtypeStruct((own_rows, model), bf16),
            jax.ShapeDtypeStruct((page, head_dim), bf16),
            jax.ShapeDtypeStruct((page, head_dim), bf16),
        ),
        in_specs=[hbm] * 8 + [pl.BlockSpec(memory_space=pltpu.SMEM)],
        out_specs=(vmem, vmem, vmem),
        scratch_shapes=[
            pltpu.VMEM((own_rows, model), bf16),
            pltpu.VMEM((1, model), f32),
            pltpu.VMEM((1, model), f32),
            pltpu.VMEM((groups, own_rows, model), bf16),
            pltpu.VMEM((heads, planes, depth, head_dim), bf16),
            pltpu.VMEM((planes, kv_width, depth), bf16),
            pltpu.VMEM((out_rows, width), bf16),
            pltpu.VMEM((groups, page, head_dim), bf16),
            pltpu.VMEM((groups, page, head_dim), bf16),
            pltpu.VMEM((groups, kv_width, span), bf16),
            pltpu.VMEM((heads, planes, span, head_dim), bf16),
            pltpu.VMEM((head_dim, groups * page - span), bf16),
            pltpu.VMEM((8, groups * page - span), f32),
            pltpu.VMEM((groups * page // span, span, span), f32),
            pltpu.VMEM((planes, 2 * CHIPS, own_rows, width), f32),
            pltpu.VMEM((planes, CHIPS, own_rows, width), bf16),
            pltpu.VMEM((planes, CHIPS, own_rows, width), bf16),
            pltpu.VMEM((planes, FLIPS, own_rows, width), bf16),
            pltpu.VMEM((planes, FLIPS, own_rows, width), bf16),
            pltpu.VMEM((planes, own_rows, width), f32),
            pltpu.VMEM((planes, own_rows, width), bf16),
            dma((9,)),
            dma((5, planes - 1, 2)),
            dma((5, planes)),
            dma((3, 4 + FLIPS)),
            dma((3, groups)),
            dma((groups - 1,)),
            dma((groups,)),
            dma((planes,)),
            dma((planes,)),
            dma((planes, FLIPS)),
            dma((planes, FLIPS)),
            dma((planes,)),
            dma((planes,)),
        ],
        compiler_params=pltpu.CompilerParams(
            collective_id=0, has_side_effects=True, vmem_limit_bytes=64 * 1024 * 1024
        ),
        cost_estimate=pl.CostEstimate(
            flops=10**9, bytes_accessed=2 * 10**6, transcendentals=10**6
        ),
        name="attention_layer",
    )(
        hidden_states[0],
        norm_gain[None],
        norm_bias[None],
        query_weight,
        keyvalue_weight.T,
        out_weight,
        key_cache[0],
        value_cache[0],
        cache_length,
    )
    results = pl.pallas_call(
        hand_over,
        out_shape=tuple(
            jax.ShapeDtypeStruct((1,) + result.shape, bf16) for result in (out, new_key, new_value)
        ),
        in_specs=[vmem] * 3,
        out_specs=(vmem,) * 3,
        compiler_params=pltpu.CompilerParams(vmem_limit_bytes=64 * 1024 * 1024),
        name="hand_over",
    )(out, new_key, new_value)
    return tuple(results)


def device_program(mesh, *args):
    groups, planes = mesh.shape["gx"], mesh.shape["gy"]
    if groups == 2 * CHIPS and planes == 4:
        return fused(groups, planes, *args)
    return body(*args)


def solution(mesh):
    return jax.shard_map(
        functools.partial(device_program, mesh),
        mesh=mesh,
        in_specs=(
            P("gy", "gx", None),
            P(),
            P(),
            P("gy", "gx"),
            P("gy", "gx"),
            P("gx", "gy"),
            P("gy", "gx", None),
            P("gy", "gx", None),
            P("gy"),
        ),
        out_specs=(P("gy", "gx", None), P("gy", "gx", None), P("gy", "gx", None)),
        check_vma=False,
    )
```

```python
import functools
import math

import jax
import jax.numpy as jnp
from jax import lax
from jax.experimental import pallas as pl
from jax.experimental.pallas import tpu as pltpu
from jax.sharding import PartitionSpec as P

HEADS = 16


NEGATIVE = -1e30


def normalize(hidden_states, norm_gain, norm_bias):
    values = hidden_states.astype(jnp.float32)
    average = jnp.mean(values, axis=-1, keepdims=True)
    centred = values - average
    spread = jnp.mean(centred * centred, axis=-1, keepdims=True)
    return (centred * lax.rsqrt(spread + 1e-05) * norm_gain + norm_bias).astype(jnp.bfloat16)


def page_terms(query_rows, query_pos, key_rows, value_rows, page_size):
    row_count = query_rows.shape[0]
    head_dim = key_rows.shape[1]
    page_count = key_rows.shape[0] // page_size
    scores = lax.dot_general(
        query_rows, key_rows, (((1,), (1,)), ((), ())), preferred_element_type=jnp.float32
    )
    scores = (scores * head_dim ** (-0.5)).reshape(row_count, page_count, page_size)
    key_pos = jnp.arange(page_count * page_size, dtype=jnp.int32).reshape(page_count, page_size)
    allowed = key_pos[None, :, :] <= query_pos[:, None, None]
    maxima = jnp.max(jnp.where(allowed, scores, NEGATIVE), axis=2)
    weights = jnp.where(allowed, jnp.exp(scores - maxima[:, :, None]), 0.0)
    totals = jnp.sum(weights, axis=2)
    weighted = jnp.einsum(
        "rnp,npd->rnd",
        weights.astype(jnp.bfloat16),
        value_rows.reshape(page_count, page_size, head_dim),
        preferred_element_type=jnp.float32,
    )
    return (maxima, totals, weighted)


def reduce_pages(maxima, totals, weighted):
    largest = jnp.max(maxima, axis=1)
    factor = jnp.exp(maxima - largest[:, None])
    return (
        largest,
        jnp.sum(totals * factor, axis=1),
        jnp.sum(weighted * factor[:, :, None], axis=1),
    )


def join_pages(first, second):
    larger = jnp.maximum(first[0], second[0])
    second_factor = jnp.exp(second[0] - larger)
    return (larger, second[1] * second_factor, second[2] * second_factor[:, None])


def body(
    hidden_states,
    norm_gain,
    norm_bias,
    query_weight,
    keyvalue_weight,
    out_weight,
    key_cache,
    value_cache,
    cache_length,
):
    own_tokens = hidden_states.shape[1]
    groups = lax.axis_size("gx")
    column_index = lax.axis_index("gx")
    span_len = own_tokens * groups
    page_size = key_cache.shape[1]
    head_dim = key_cache.shape[2]
    head_count = HEADS
    head_width = head_count * head_dim
    normed = normalize(hidden_states[0], norm_gain, norm_bias)
    full_rows = lax.all_gather(normed, "gx", axis=0, tiled=True)
    pieces = (
        lax.all_gather(query_weight, "gy", axis=0, tiled=True),
        lax.all_gather(keyvalue_weight, "gy", axis=0, tiled=True),
    )
    query_part = jnp.dot(full_rows, pieces[0], preferred_element_type=jnp.float32)
    keyvalue_part = jnp.dot(full_rows, pieces[1], preferred_element_type=jnp.float32)
    query_local = query_part.astype(jnp.bfloat16)
    keyvalue_local = keyvalue_part.astype(jnp.bfloat16)
    queries, new_keyvalue = (
        lax.all_gather(query_local, "gx", axis=1, tiled=True),
        lax.all_gather(keyvalue_local, "gx", axis=1, tiled=True),
    )
    length = cache_length[0]
    page_base = column_index * page_size
    offsets = page_base + jnp.arange(page_size, dtype=jnp.int32) - length
    inside = (offsets >= 0) & (offsets < span_len)
    picked = jnp.take(new_keyvalue, jnp.clip(offsets, 0, span_len - 1), axis=0)
    key_page = jnp.where(inside[:, None], picked[:, :head_dim], key_cache[0])
    value_page = jnp.where(inside[:, None], picked[:, head_dim:], value_cache[0])
    own_rows = lax.dynamic_slice_in_dim(queries, column_index * own_tokens, own_tokens, 0)
    own_rows = own_rows.reshape(own_tokens * head_count, head_dim)
    own_pos = (
        length
        + column_index * own_tokens
        + jnp.arange(own_tokens * head_count, dtype=jnp.int32) // head_count
    )
    own_total = own_tokens * head_count
    empty = (
        jnp.full((own_total,), NEGATIVE, jnp.float32),
        jnp.zeros((own_total,), jnp.float32),
        jnp.zeros((own_total, head_dim), jnp.float32),
    )
    pieces = (
        lax.all_gather(key_page, "gx", axis=0, tiled=True),
        lax.all_gather(value_page, "gx", axis=0, tiled=True),
    )
    maxima, totals, weighted = page_terms(own_rows, own_pos, pieces[0], pieces[1], page_size)
    maxima, totals, weighted = join_pages(empty, reduce_pages(maxima, totals, weighted))
    own_out = (weighted / totals[:, None]).reshape(own_tokens, head_width).astype(jnp.bfloat16)
    attended = lax.all_to_all(own_out, "gx", split_axis=1, concat_axis=0, tiled=True)
    out_full = lax.all_gather(out_weight, "gy", axis=1, tiled=True)
    hidden_part = lax.psum_scatter(
        jnp.dot(attended, out_full, preferred_element_type=jnp.float32),
        "gx",
        scatter_dimension=0,
        tiled=True,
    )
    return (hidden_part.astype(jnp.bfloat16)[None], key_page[None], value_page[None])


MESH = pl.DeviceIdType.MESH
CHIPS = 4
FLIPS = 3


def fused_kernel(
    planes,
    hidden_ref,
    gain_ref,
    bias_ref,
    wq_ref,
    wkv_ref,
    wo_ref,
    key_ref,
    value_ref,
    length_ref,
    out_ref,
    new_key_ref,
    new_value_ref,
    hidden_in,
    gain_in,
    bias_in,
    normed,
    wq_all,
    wkv_all,
    wo_own,
    keys,
    values,
    new_kv,
    attended,
    keys_turned,
    hidden_row,
    scores,
    partial,
    sibling_out,
    sibling_in,
    chip_out,
    chip_in,
    own_sum,
    pieces,
    load_sem,
    z_send,
    z_recv,
    rows_send,
    rows_recv,
    kv_send,
    kv_recv,
    sib_send,
    sib_recv,
    chip_send,
    chip_recv,
    home_send,
    home_recv,
):
    me = lax.axis_index("gx")
    z = lax.axis_index("gy")
    core = me % 2
    chip = me // 2
    cx = chip % 2
    cy = chip // 2
    sibling = chip * 2 + 1 - core
    other_chips = (cy * 2 + 1 - cx, (1 - cy) * 2 + cx, (1 - cy) * 2 + 1 - cx)
    peers = [other * 2 + core for other in other_chips]
    far = [other * 2 + 1 - core for other in other_chips]
    everyone = [sibling] + peers + far
    has_up = z < planes - 1
    has_down = z > 0

    barrier = pltpu.get_barrier_semaphore()
    for peer in everyone:
        pl.semaphore_signal(barrier, inc=1, device_id={"gx": peer}, device_id_type=MESH)

    other_planes = [lax.rem(z + k, planes) for k in range(1, planes)]
    for plane in other_planes:
        pl.semaphore_signal(barrier, inc=1, device_id={"gy": plane}, device_id_type=MESH)

    head_dim = key_ref.shape[1]
    head_columns = [wq_ref.at[:, pl.ds(head * head_dim, head_dim)] for head in range(2)]
    sources = [wkv_ref] + head_columns
    buffers = [wkv_all, wq_all.at[0], wq_all.at[1], attended.at[0], attended.at[1]]
    loads = [
        pltpu.make_async_copy(source, target, load_sem.at[slot])
        for slot, (source, target) in enumerate(
            [
                (hidden_ref, hidden_in),
                (gain_ref, gain_in),
                (bias_ref, bias_in),
                (key_ref, keys.at[me]),
                (value_ref, values.at[me]),
            ]
            + [(source, buffer.at[z]) for source, buffer in zip(sources, buffers)]
            + [(wo_ref, wo_own)]
        )
    ]
    for load in loads:
        load.start()

    pl.semaphore_wait(barrier, len(everyone) + planes - 1)

    def z_copy(kind, step, direction, own=False):
        shard = z - direction * step
        buffer = buffers[kind]
        return pltpu.make_async_remote_copy(
            src_ref=sources[kind] if own and kind < len(sources) else buffer.at[shard],
            dst_ref=buffer.at[shard],
            send_sem=z_send.at[kind, step, (direction + 1) // 2],
            recv_sem=z_recv.at[kind, shard],
            device_id={"gy": z + direction},
            device_id_type=MESH,
        )

    def z_cond(step, direction):
        if direction > 0:
            return has_up & (z - step >= 0)
        return has_down & (z + step < planes)

    def z_arrived(kind, shard):
        buffer = buffers[kind]
        pltpu.make_async_copy(buffer.at[shard], buffer.at[shard], z_recv.at[kind, shard]).wait()

    def z_forward(kind, step):
        for direction in (1, -1):

            @pl.when(z_cond(step, direction))
            def _(direction=direction):
                if step > 0:
                    z_arrived(kind, z - direction * step)
                z_copy(kind, step, direction, step == 0).start()

    def z_wait_send(kind, step):
        for direction in (1, -1):

            @pl.when(z_cond(step, direction))
            def _(direction=direction):
                z_copy(kind, step, direction, step == 0).wait_send()

    def z_last(kind, step):
        @pl.when((z == planes - 1) & (z - 1 - step >= 0))
        def _():
            z_arrived(kind, z - 1 - step)

        @pl.when((z == 0) & (z + 1 + step < planes))
        def _():
            z_arrived(kind, z + 1 + step)

    def second_start(step):
        for direction in (1, -1):
            last = z if direction > 0 else planes - 1 - z

            @pl.when(z_cond(0, direction) & (last == step))
            def _(direction=direction):
                z_copy(2, 0, direction, True).start()

    def z_take(kind, shard):
        z_arrived(kind, shard)

        @pl.when((shard < z) & has_up)
        def _():
            z_copy(kind, z - shard, 1).start()

        @pl.when((shard > z) & has_down)
        def _():
            z_copy(kind, shard - z, -1).start()

    gathered = (normed, keys, values)

    def row_copy(kind, block, target, slot):
        return pltpu.make_async_remote_copy(
            src_ref=gathered[kind].at[block],
            dst_ref=gathered[kind].at[block],
            send_sem=rows_send.at[kind, slot],
            recv_sem=rows_recv.at[kind, block],
            device_id={"gx": target},
            device_id_type=MESH,
        )

    def rows_start(kind):
        for slot, target in enumerate(peers + [sibling]):
            row_copy(kind, me, target, slot).start()

    def rows_wait(kind, block):
        pltpu.make_async_copy(
            gathered[kind].at[block], gathered[kind].at[block], rows_recv.at[kind, block]
        ).wait()

    def rows_forward(kind):
        for flip in range(FLIPS):
            rows_wait(kind, peers[flip])
            row_copy(kind, peers[flip], sibling, 4 + flip).start()

    def rows_finish(kind):
        for block in [sibling] + far:
            rows_wait(kind, block)

    for kind in range(2):
        z_forward(kind, 0)
    second_start(0)

    for slot in range(3):
        loads[slot].wait()
    rows = hidden_in[...].astype(jnp.float32)
    average = jnp.mean(rows, axis=-1, keepdims=True)
    centred = rows - average
    spread = jnp.mean(centred * centred, axis=-1, keepdims=True)
    normed[me] = (
        centred * lax.rsqrt(spread + 1e-05) * gain_in[...] + bias_in[...]
    ).astype(jnp.bfloat16)
    rows_start(0)
    for kind in (1, 2):
        loads[kind + 2].wait()
        rows_start(kind)

    z_forward(0, 1)
    z_forward(0, 2)
    z_forward(1, 1)
    second_start(1)
    rows_forward(0)
    z_forward(1, 2)
    second_start(2)
    rows_finish(0)
    loads[5].wait()
    for step in range(planes - 1):
        z_last(0, step)

    tokens = normed[...].reshape(-1, normed.shape[2])
    token_count = tokens.shape[0]
    depth = wq_all.shape[2]
    kv_width = wkv_all.shape[1]
    kv_part = jnp.zeros((kv_width, token_count), jnp.float32)
    for part in range(planes):
        kv_part += lax.dot_general(
            wkv_all[part],
            tokens[:, part * depth : (part + 1) * depth],
            (((1,), (1,)), ((), ())),
            preferred_element_type=jnp.float32,
        )
    new_kv[me] = kv_part.astype(jnp.bfloat16)

    def kv_copy(block, target, slot):
        return pltpu.make_async_remote_copy(
            src_ref=new_kv.at[block],
            dst_ref=new_kv.at[block],
            send_sem=kv_send.at[slot],
            recv_sem=kv_recv.at[block],
            device_id={"gx": target},
            device_id_type=MESH,
        )

    for slot, target in enumerate(everyone):
        kv_copy(me, target, slot).start()

    rows_forward(1)
    z_forward(2, 1)
    rows_forward(2)
    z_forward(2, 2)

    for block in everyone:
        pltpu.make_async_copy(new_kv.at[block], new_kv.at[block], kv_recv.at[block]).wait()

    length = length_ref[0]
    page = key_ref.shape[0]
    kv_cols = new_kv[...].reshape(2 * head_dim, token_count)
    offsets = (
        lax.broadcasted_iota(jnp.int32, (page, token_count), 0) + me * page - length
    )
    chosen = offsets == lax.broadcasted_iota(jnp.int32, (page, token_count), 1)
    picked = lax.dot_general(
        jnp.where(chosen, 1.0, 0.0).astype(jnp.bfloat16),
        kv_cols,
        (((1,), (1,)), ((), ())),
        preferred_element_type=jnp.float32,
    )
    row_offset = lax.broadcasted_iota(jnp.int32, (page, head_dim), 0) + me * page - length
    inside = (row_offset >= 0) & (row_offset < token_count)
    new_key_ref[...] = jnp.where(
        inside, picked[:, :head_dim], keys[me].astype(jnp.float32)
    ).astype(jnp.bfloat16)
    new_value_ref[...] = jnp.where(
        inside, picked[:, head_dim:], values[me].astype(jnp.float32)
    ).astype(jnp.bfloat16)

    rows_finish(1)
    rows_finish(2)
    def queries(head):
        loads[6 + head].wait()
        for step in range(planes - 1):
            z_last(1 + head, step)
        query = jnp.zeros((token_count, head_dim), jnp.float32)
        for part in range(planes):
            query += jnp.dot(
                normed[:, :, part * depth : (part + 1) * depth].reshape(token_count, depth),
                wq_all[head, part],
                preferred_element_type=jnp.float32,
            )
        return query.astype(jnp.bfloat16)

    cached = keys.shape[0] * page - token_count
    chunk = token_count
    chunks = cached // chunk
    scale = head_dim ** (-0.5) * math.log2(math.e)
    lanes = 128
    keys_turned[...] = (
        keys[...].reshape(-1, head_dim)[:cached].astype(jnp.float32).T.astype(jnp.bfloat16)
    )
    old_pos = lax.broadcasted_iota(jnp.int32, hidden_row.shape, 1)
    hidden_row[...] = jnp.where(old_pos < length, 0.0, NEGATIVE)

    def attend(q):
        running = None
        for c in range(chunks + 1):
            if c < chunks:
                part = jnp.dot(
                    q,
                    keys_turned[:, c * chunk : (c + 1) * chunk],
                    preferred_element_type=jnp.float32,
                )
                part = part * scale + hidden_row[:1, c * chunk : (c + 1) * chunk]
            else:
                part = jnp.dot(
                    q,
                    new_kv[...].reshape(2 * head_dim, token_count)[:head_dim],
                    preferred_element_type=jnp.float32,
                )
                row = lax.broadcasted_iota(jnp.int32, part.shape, 0) % token_count
                col = lax.broadcasted_iota(jnp.int32, part.shape, 1)
                part = jnp.where(col <= row, part * scale, NEGATIVE)
            scores[c] = part
            for first in range(0, chunk, lanes):
                piece = part[:, first : first + lanes]
                running = piece if running is None else jnp.maximum(running, piece)
        top = jnp.max(running, axis=1, keepdims=True)
        total = jnp.zeros((q.shape[0], lanes), jnp.float32)
        summed = jnp.zeros((q.shape[0], head_dim), jnp.float32)
        for c in range(chunks + 1):
            probs = jnp.exp2(scores[c] - top)
            for first in range(0, chunk, lanes):
                total += probs[:, first : first + lanes]
            if c < chunks:
                summed += jnp.dot(
                    probs.astype(jnp.bfloat16),
                    values[...].reshape(-1, head_dim)[c * chunk : (c + 1) * chunk],
                    preferred_element_type=jnp.float32,
                )
            else:
                summed += lax.dot_general(
                    probs.astype(jnp.bfloat16),
                    new_kv[...].reshape(2 * head_dim, token_count)[head_dim:],
                    (((1,), (1,)), ((), ())),
                    preferred_element_type=jnp.float32,
                )
        return (summed / jnp.sum(total, axis=1, keepdims=True)).astype(jnp.bfloat16)

    for head in range(2):
        attended[head, z] = attend(queries(head))
        z_forward(3 + head, 0)
    own_rows = hidden_ref.shape[0]
    width = wo_own.shape[1]

    def sib_copy(n):
        return pltpu.make_async_remote_copy(
            src_ref=sibling_out.at[n],
            dst_ref=sibling_in.at[n],
            send_sem=sib_send.at[n],
            recv_sem=sib_recv.at[n],
            device_id={"gx": sibling},
            device_id_type=MESH,
        )

    def chip_copy(n, flip):
        return pltpu.make_async_remote_copy(
            src_ref=chip_out.at[n, flip],
            dst_ref=chip_in.at[n, flip],
            send_sem=chip_send.at[n, flip],
            recv_sem=chip_recv.at[n, flip],
            device_id={"gx": peers[flip]},
            device_id_type=MESH,
        )

    def head_product(n, head):
        return jnp.dot(
            attended[head, order[n]],
            wo_own[head * head_dim : (head + 1) * head_dim, :],
            preferred_element_type=jnp.float32,
        ).reshape(2 * CHIPS, own_rows, width)

    def project(n):
        partial[n] = head_product(n, 0) + head_product(n, 1)
        for k in range(CHIPS):
            sibling_out[n, k] = partial[n, 2 * k + 1 - core].astype(jnp.bfloat16)
        sib_copy(n).start()

    def spread_sums(n):
        sib_copy(n).wait_recv()
        for flip in range(FLIPS):
            other = other_chips[flip]
            chip_out[n, flip] = (
                partial[n, 2 * other + core] + sibling_in[n, other].astype(jnp.float32)
            ).astype(jnp.bfloat16)
            chip_copy(n, flip).start()
        own_sum[n] = partial[n, me] + sibling_in[n, chip].astype(jnp.float32)

    low = z < planes // 2
    order = [z, jnp.where(low, z + 1, z - 1)]
    order.append(jnp.where(low, (z + planes - 1) % planes, (z + 1) % planes))
    order[2] = jnp.where((z == 0) | (z == planes - 1), jnp.where(low, 2, planes - 3), order[2])
    order.append(jnp.where(low, planes - 1, 0))

    def home_copy(n, plane):
        return pltpu.make_async_remote_copy(
            src_ref=pieces.at[n],
            dst_ref=out_ref.at[:, pl.ds(pl.multiple_of(z * width, width), width)],
            send_sem=home_send.at[n],
            recv_sem=home_recv.at[z],
            device_id={"gy": plane},
            device_id_type=MESH,
        )

    def finish(n):
        total = own_sum[n]
        for flip in range(FLIPS):
            chip_copy(n, flip).wait_recv()
            total += chip_in[n, flip].astype(jnp.float32)
        piece = total.astype(jnp.bfloat16)
        if n == 0:
            out_ref[:, pl.ds(pl.multiple_of(z * width, width), width)] = piece
        else:
            pieces[n] = piece
            home_copy(n, order[n]).start()

    loads[8].wait()
    for n in range(planes):
        if n > 0:
            z_take(3, order[n])
            z_take(4, order[n])
        project(n)
        if n > 0:
            spread_sums(n - 1)
        if n > 1:
            finish(n - 2)
    spread_sums(planes - 1)
    finish(planes - 2)
    finish(planes - 1)
    for plane in other_planes:
        landed = out_ref.at[:, pl.ds(pl.multiple_of(plane * width, width), width)]
        pltpu.make_async_copy(landed, landed, home_recv.at[plane]).wait()

    for n in range(1, planes):
        home_copy(n, order[n]).wait_send()
    for kind in range(5):
        for step in range(planes - 1):
            z_wait_send(kind, step)
    for kind in range(3):
        for slot, target in enumerate(peers + [sibling]):
            row_copy(kind, me, target, slot).wait_send()
        for flip in range(FLIPS):
            row_copy(kind, peers[flip], sibling, 4 + flip).wait_send()
    for slot, target in enumerate(everyone):
        kv_copy(me, target, slot).wait_send()
    for n in range(planes):
        sib_copy(n).wait_send()
        for flip in range(FLIPS):
            chip_copy(n, flip).wait_send()


def hand_over(out_ref, key_ref, value_ref, out_to, key_to, value_to):
    out_to[0] = out_ref[...]
    key_to[0] = key_ref[...]
    value_to[0] = value_ref[...]


def fused(
    groups,
    planes,
    hidden_states,
    norm_gain,
    norm_bias,
    query_weight,
    keyvalue_weight,
    out_weight,
    key_cache,
    value_cache,
    cache_length,
):
    own_rows, model = hidden_states.shape[1:]
    page, head_dim = key_cache.shape[1:]
    span = own_rows * groups
    depth, columns = query_weight.shape
    kv_width = keyvalue_weight.shape[1]
    out_rows, width = out_weight.shape
    heads = columns // head_dim
    bf16, f32 = jnp.bfloat16, jnp.float32
    vmem = pl.BlockSpec(memory_space=pltpu.VMEM)
    hbm = pl.BlockSpec(memory_space=pltpu.HBM)
    dma = pltpu.SemaphoreType.DMA
    out, new_key, new_value = pl.pallas_call(
        functools.partial(fused_kernel, planes),
        out_shape=(
            jax.ShapeDtypeStruct((own_rows, model), bf16),
            jax.ShapeDtypeStruct((page, head_dim), bf16),
            jax.ShapeDtypeStruct((page, head_dim), bf16),
        ),
        in_specs=[hbm] * 8 + [pl.BlockSpec(memory_space=pltpu.SMEM)],
        out_specs=(vmem, vmem, vmem),
        scratch_shapes=[
            pltpu.VMEM((own_rows, model), bf16),
            pltpu.VMEM((1, model), f32),
            pltpu.VMEM((1, model), f32),
            pltpu.VMEM((groups, own_rows, model), bf16),
            pltpu.VMEM((heads, planes, depth, head_dim), bf16),
            pltpu.VMEM((planes, kv_width, depth), bf16),
            pltpu.VMEM((out_rows, width), bf16),
            pltpu.VMEM((groups, page, head_dim), bf16),
            pltpu.VMEM((groups, page, head_dim), bf16),
            pltpu.VMEM((groups, kv_width, span), bf16),
            pltpu.VMEM((heads, planes, span, head_dim), bf16),
            pltpu.VMEM((head_dim, groups * page - span), bf16),
            pltpu.VMEM((8, groups * page - span), f32),
            pltpu.VMEM((groups * page // span, span, span), f32),
            pltpu.VMEM((planes, 2 * CHIPS, own_rows, width), f32),
            pltpu.VMEM((planes, CHIPS, own_rows, width), bf16),
            pltpu.VMEM((planes, CHIPS, own_rows, width), bf16),
            pltpu.VMEM((planes, FLIPS, own_rows, width), bf16),
            pltpu.VMEM((planes, FLIPS, own_rows, width), bf16),
            pltpu.VMEM((planes, own_rows, width), f32),
            pltpu.VMEM((planes, own_rows, width), bf16),
            dma((9,)),
            dma((5, planes - 1, 2)),
            dma((5, planes)),
            dma((3, 4 + FLIPS)),
            dma((3, groups)),
            dma((groups - 1,)),
            dma((groups,)),
            dma((planes,)),
            dma((planes,)),
            dma((planes, FLIPS)),
            dma((planes, FLIPS)),
            dma((planes,)),
            dma((planes,)),
        ],
        compiler_params=pltpu.CompilerParams(
            collective_id=0, has_side_effects=True, vmem_limit_bytes=64 * 1024 * 1024
        ),
        cost_estimate=pl.CostEstimate(
            flops=10**9, bytes_accessed=2 * 10**6, transcendentals=10**6
        ),
        name="attention_layer",
    )(
        hidden_states[0],
        norm_gain[None],
        norm_bias[None],
        query_weight,
        keyvalue_weight.T,
        out_weight,
        key_cache[0],
        value_cache[0],
        cache_length,
    )
    results = pl.pallas_call(
        hand_over,
        out_shape=tuple(
            jax.ShapeDtypeStruct((1,) + result.shape, bf16) for result in (out, new_key, new_value)
        ),
        in_specs=[vmem] * 3,
        out_specs=(vmem,) * 3,
        compiler_params=pltpu.CompilerParams(vmem_limit_bytes=64 * 1024 * 1024),
        name="hand_over",
    )(out, new_key, new_value)
    return tuple(results)


def device_program(mesh, *args):
    groups, planes = mesh.shape["gx"], mesh.shape["gy"]
    if groups == 2 * CHIPS and planes == 4:
        return fused(groups, planes, *args)
    return body(*args)


def solution(mesh):
    return jax.shard_map(
        functools.partial(device_program, mesh),
        mesh=mesh,
        in_specs=(
            P("gy", "gx", None),
            P(),
            P(),
            P("gy", "gx"),
            P("gy", "gx"),
            P("gx", "gy"),
            P("gy", "gx", None),
            P("gy", "gx", None),
            P("gy"),
        ),
        out_specs=(P("gy", "gx", None), P("gy", "gx", None), P("gy", "gx", None)),
        check_vma=False,
    )
```

```python
import functools
import math

import jax
import jax.numpy as jnp
from jax import lax
from jax.experimental import pallas as pl
from jax.experimental.pallas import tpu as pltpu
from jax.sharding import PartitionSpec as P

HEADS = 16


NEGATIVE = -1e30


def normalize(hidden_states, norm_gain, norm_bias):
    values = hidden_states.astype(jnp.float32)
    average = jnp.mean(values, axis=-1, keepdims=True)
    centred = values - average
    spread = jnp.mean(centred * centred, axis=-1, keepdims=True)
    return (centred * lax.rsqrt(spread + 1e-05) * norm_gain + norm_bias).astype(jnp.bfloat16)


def page_terms(query_rows, query_pos, key_rows, value_rows, page_size):
    row_count = query_rows.shape[0]
    head_dim = key_rows.shape[1]
    page_count = key_rows.shape[0] // page_size
    scores = lax.dot_general(
        query_rows, key_rows, (((1,), (1,)), ((), ())), preferred_element_type=jnp.float32
    )
    scores = (scores * head_dim ** (-0.5)).reshape(row_count, page_count, page_size)
    key_pos = jnp.arange(page_count * page_size, dtype=jnp.int32).reshape(page_count, page_size)
    allowed = key_pos[None, :, :] <= query_pos[:, None, None]
    maxima = jnp.max(jnp.where(allowed, scores, NEGATIVE), axis=2)
    weights = jnp.where(allowed, jnp.exp(scores - maxima[:, :, None]), 0.0)
    totals = jnp.sum(weights, axis=2)
    weighted = jnp.einsum(
        "rnp,npd->rnd",
        weights.astype(jnp.bfloat16),
        value_rows.reshape(page_count, page_size, head_dim),
        preferred_element_type=jnp.float32,
    )
    return (maxima, totals, weighted)


def reduce_pages(maxima, totals, weighted):
    largest = jnp.max(maxima, axis=1)
    factor = jnp.exp(maxima - largest[:, None])
    return (
        largest,
        jnp.sum(totals * factor, axis=1),
        jnp.sum(weighted * factor[:, :, None], axis=1),
    )


def join_pages(first, second):
    larger = jnp.maximum(first[0], second[0])
    second_factor = jnp.exp(second[0] - larger)
    return (larger, second[1] * second_factor, second[2] * second_factor[:, None])


def body(
    hidden_states,
    norm_gain,
    norm_bias,
    query_weight,
    keyvalue_weight,
    out_weight,
    key_cache,
    value_cache,
    cache_length,
):
    own_tokens = hidden_states.shape[1]
    groups = lax.axis_size("gx")
    column_index = lax.axis_index("gx")
    span_len = own_tokens * groups
    page_size = key_cache.shape[1]
    head_dim = key_cache.shape[2]
    head_count = HEADS
    head_width = head_count * head_dim
    normed = normalize(hidden_states[0], norm_gain, norm_bias)
    full_rows = lax.all_gather(normed, "gx", axis=0, tiled=True)
    pieces = (
        lax.all_gather(query_weight, "gy", axis=0, tiled=True),
        lax.all_gather(keyvalue_weight, "gy", axis=0, tiled=True),
    )
    query_part = jnp.dot(full_rows, pieces[0], preferred_element_type=jnp.float32)
    keyvalue_part = jnp.dot(full_rows, pieces[1], preferred_element_type=jnp.float32)
    query_local = query_part.astype(jnp.bfloat16)
    keyvalue_local = keyvalue_part.astype(jnp.bfloat16)
    queries, new_keyvalue = (
        lax.all_gather(query_local, "gx", axis=1, tiled=True),
        lax.all_gather(keyvalue_local, "gx", axis=1, tiled=True),
    )
    length = cache_length[0]
    page_base = column_index * page_size
    offsets = page_base + jnp.arange(page_size, dtype=jnp.int32) - length
    inside = (offsets >= 0) & (offsets < span_len)
    picked = jnp.take(new_keyvalue, jnp.clip(offsets, 0, span_len - 1), axis=0)
    key_page = jnp.where(inside[:, None], picked[:, :head_dim], key_cache[0])
    value_page = jnp.where(inside[:, None], picked[:, head_dim:], value_cache[0])
    own_rows = lax.dynamic_slice_in_dim(queries, column_index * own_tokens, own_tokens, 0)
    own_rows = own_rows.reshape(own_tokens * head_count, head_dim)
    own_pos = (
        length
        + column_index * own_tokens
        + jnp.arange(own_tokens * head_count, dtype=jnp.int32) // head_count
    )
    own_total = own_tokens * head_count
    empty = (
        jnp.full((own_total,), NEGATIVE, jnp.float32),
        jnp.zeros((own_total,), jnp.float32),
        jnp.zeros((own_total, head_dim), jnp.float32),
    )
    pieces = (
        lax.all_gather(key_page, "gx", axis=0, tiled=True),
        lax.all_gather(value_page, "gx", axis=0, tiled=True),
    )
    maxima, totals, weighted = page_terms(own_rows, own_pos, pieces[0], pieces[1], page_size)
    maxima, totals, weighted = join_pages(empty, reduce_pages(maxima, totals, weighted))
    own_out = (weighted / totals[:, None]).reshape(own_tokens, head_width).astype(jnp.bfloat16)
    attended = lax.all_to_all(own_out, "gx", split_axis=1, concat_axis=0, tiled=True)
    out_full = lax.all_gather(out_weight, "gy", axis=1, tiled=True)
    hidden_part = lax.psum_scatter(
        jnp.dot(attended, out_full, preferred_element_type=jnp.float32),
        "gx",
        scatter_dimension=0,
        tiled=True,
    )
    return (hidden_part.astype(jnp.bfloat16)[None], key_page[None], value_page[None])


MESH = pl.DeviceIdType.MESH
CHIPS = 4
FLIPS = 3


def fused_kernel(
    planes,
    hidden_ref,
    gain_ref,
    bias_ref,
    wq_ref,
    wkv_ref,
    wo_ref,
    key_ref,
    value_ref,
    length_ref,
    out_ref,
    new_key_ref,
    new_value_ref,
    hidden_in,
    gain_in,
    bias_in,
    normed,
    wq_all,
    wkv_all,
    wo_all,
    keys,
    values,
    new_kv,
    query_rows,
    attended,
    keys_turned,
    hidden_row,
    scores,
    partial,
    sibling_out,
    sibling_in,
    chip_out,
    chip_in,
    own_sum,
    load_sem,
    z_send,
    z_recv,
    rows_send,
    rows_recv,
    kv_send,
    kv_recv,
    sib_send,
    sib_recv,
    chip_send,
    chip_recv,
):
    me = lax.axis_index("gx")
    z = lax.axis_index("gy")
    core = me % 2
    chip = me // 2
    cx = chip % 2
    cy = chip // 2
    sibling = chip * 2 + 1 - core
    other_chips = (cy * 2 + 1 - cx, (1 - cy) * 2 + cx, (1 - cy) * 2 + 1 - cx)
    peers = [other * 2 + core for other in other_chips]
    far = [other * 2 + 1 - core for other in other_chips]
    everyone = [sibling] + peers + far
    has_up = z < planes - 1
    has_down = z > 0

    barrier = pltpu.get_barrier_semaphore()
    for peer in everyone:
        pl.semaphore_signal(barrier, inc=1, device_id={"gx": peer}, device_id_type=MESH)

    @pl.when(has_up)
    def _():
        pl.semaphore_signal(barrier, inc=1, device_id={"gy": z + 1}, device_id_type=MESH)

    @pl.when(has_down)
    def _():
        pl.semaphore_signal(barrier, inc=1, device_id={"gy": z - 1}, device_id_type=MESH)

    half_depth = wq_all.shape[2]
    half_width = wo_all.shape[3]
    half_rows = [wq_ref.at[pl.ds(half * half_depth, half_depth)] for half in range(2)]
    half_cols = [wo_ref.at[:, pl.ds(half * half_width, half_width)] for half in range(2)]
    sources = [wkv_ref] + half_rows + half_cols
    buffers = [wkv_all, wq_all.at[0], wq_all.at[1], wo_all.at[0], wo_all.at[1]]
    loads = [
        pltpu.make_async_copy(source, target, load_sem.at[slot])
        for slot, (source, target) in enumerate(
            [
                (hidden_ref, hidden_in),
                (gain_ref, gain_in),
                (bias_ref, bias_in),
                (key_ref, keys.at[me]),
                (value_ref, values.at[me]),
            ]
            + [(source, buffer.at[z]) for source, buffer in zip(sources, buffers)]
        )
    ]
    for load in loads:
        load.start()

    neighbours = has_up.astype(jnp.int32) + has_down.astype(jnp.int32)
    pl.semaphore_wait(barrier, len(everyone) + neighbours)

    def z_copy(kind, step, direction):
        shard = z - direction * step
        buffer = buffers[kind]
        return pltpu.make_async_remote_copy(
            src_ref=sources[kind] if step == 0 else buffer.at[shard],
            dst_ref=buffer.at[shard],
            send_sem=z_send.at[kind, step, (direction + 1) // 2],
            recv_sem=z_recv.at[kind, shard],
            device_id={"gy": z + direction},
            device_id_type=MESH,
        )

    def z_cond(step, direction):
        if direction > 0:
            return has_up & (z - step >= 0)
        return has_down & (z + step < planes)

    def z_arrived(kind, shard):
        buffer = buffers[kind]
        pltpu.make_async_copy(buffer.at[shard], buffer.at[shard], z_recv.at[kind, shard]).wait()

    def z_forward(kind, step):
        for direction in (1, -1):

            @pl.when(z_cond(step, direction))
            def _(direction=direction):
                if step > 0:
                    z_arrived(kind, z - direction * step)
                z_copy(kind, step, direction).start()

    def z_wait_send(kind, step):
        for direction in (1, -1):

            @pl.when(z_cond(step, direction))
            def _(direction=direction):
                z_copy(kind, step, direction).wait_send()

    def z_last(kind, step):
        @pl.when((z == planes - 1) & (z - 1 - step >= 0))
        def _():
            z_arrived(kind, z - 1 - step)

        @pl.when((z == 0) & (z + 1 + step < planes))
        def _():
            z_arrived(kind, z + 1 + step)

    def out_start(step):
        for direction in (1, -1):
            last = z if direction > 0 else planes - 1 - z

            @pl.when(z_cond(0, direction) & (last == step))
            def _(direction=direction):
                z_copy(3, 0, direction).start()
                z_copy(4, 0, direction).start()

    gathered = (normed, keys, values)

    def row_copy(kind, block, target, slot):
        return pltpu.make_async_remote_copy(
            src_ref=gathered[kind].at[block],
            dst_ref=gathered[kind].at[block],
            send_sem=rows_send.at[kind, slot],
            recv_sem=rows_recv.at[kind, block],
            device_id={"gx": target},
            device_id_type=MESH,
        )

    def rows_start(kind):
        for slot, target in enumerate((peers[0], peers[1], sibling)):
            row_copy(kind, me, target, slot).start()

    def rows_wait(kind, block):
        pltpu.make_async_copy(
            gathered[kind].at[block], gathered[kind].at[block], rows_recv.at[kind, block]
        ).wait()

    def across(kind):
        return (0, 1) if kind == 0 else (1, 0)

    def rows_forward(kind):
        first, second = across(kind)
        rows_wait(kind, peers[first])
        row_copy(kind, peers[first], peers[second], 3).start()
        if kind == 0:
            for cache in (1, 2):
                loads[cache + 2].wait()
                rows_start(cache)
        row_copy(kind, peers[first], sibling, 4).start()
        rows_wait(kind, peers[second])
        row_copy(kind, peers[second], sibling, 5).start()
        rows_wait(kind, peers[2])
        row_copy(kind, peers[2], sibling, 6).start()

    def rows_finish(kind):
        for block in [sibling] + far:
            rows_wait(kind, block)

    for kind in range(3):
        z_forward(kind, 0)
    out_start(0)

    for slot in range(3):
        loads[slot].wait()
    rows = hidden_in[...].astype(jnp.float32)
    average = jnp.mean(rows, axis=-1, keepdims=True)
    centred = rows - average
    spread = jnp.mean(centred * centred, axis=-1, keepdims=True)
    normed[me] = (
        centred * lax.rsqrt(spread + 1e-05) * gain_in[...] + bias_in[...]
    ).astype(jnp.bfloat16)
    rows_start(0)

    z_forward(0, 1)
    z_forward(0, 2)
    z_forward(1, 1)
    rows_forward(0)
    z_forward(2, 1)
    out_start(1)
    rows_finish(0)
    loads[5].wait()
    for step in range(planes - 1):
        z_last(0, step)

    tokens = normed[...].reshape(-1, normed.shape[2])
    token_count = tokens.shape[0]
    depth = 2 * half_depth
    kv_width = wkv_all.shape[1]
    kv_part = jnp.zeros((kv_width, token_count), jnp.float32)
    for part in range(planes):
        kv_part += lax.dot_general(
            wkv_all[part],
            tokens[:, part * depth : (part + 1) * depth],
            (((1,), (1,)), ((), ())),
            preferred_element_type=jnp.float32,
        )
    new_kv[me] = kv_part.astype(jnp.bfloat16)

    def kv_copy(block, target, slot):
        return pltpu.make_async_remote_copy(
            src_ref=new_kv.at[block],
            dst_ref=new_kv.at[block],
            send_sem=kv_send.at[slot],
            recv_sem=kv_recv.at[block],
            device_id={"gx": target},
            device_id_type=MESH,
        )

    for slot, target in enumerate(everyone):
        kv_copy(me, target, slot).start()

    rows_forward(1)
    z_forward(1, 2)
    rows_forward(2)
    z_forward(2, 2)
    out_start(2)

    for block in everyone:
        pltpu.make_async_copy(new_kv.at[block], new_kv.at[block], kv_recv.at[block]).wait()

    length = length_ref[0]
    page = key_ref.shape[0]
    head_dim = key_ref.shape[1]
    kv_cols = new_kv[...].reshape(2 * head_dim, token_count)
    offsets = (
        lax.broadcasted_iota(jnp.int32, (page, token_count), 0) + me * page - length
    )
    chosen = offsets == lax.broadcasted_iota(jnp.int32, (page, token_count), 1)
    picked = lax.dot_general(
        jnp.where(chosen, 1.0, 0.0).astype(jnp.bfloat16),
        kv_cols,
        (((1,), (1,)), ((), ())),
        preferred_element_type=jnp.float32,
    )
    row_offset = lax.broadcasted_iota(jnp.int32, (page, head_dim), 0) + me * page - length
    inside = (row_offset >= 0) & (row_offset < token_count)
    new_key_ref[...] = jnp.where(
        inside, picked[:, :head_dim], keys[me].astype(jnp.float32)
    ).astype(jnp.bfloat16)
    new_value_ref[...] = jnp.where(
        inside, picked[:, head_dim:], values[me].astype(jnp.float32)
    ).astype(jnp.bfloat16)

    rows_finish(1)
    rows_finish(2)
    for half in range(2):
        loads[6 + half].wait()
        for step in range(planes - 1):
            z_last(1 + half, step)

    heads = wq_all.shape[3] // head_dim
    query = jnp.zeros((token_count, heads * head_dim), jnp.float32)
    for part in range(2 * planes):
        query += jnp.dot(
            normed[:, :, part * half_depth : (part + 1) * half_depth].reshape(
                token_count, half_depth
            ),
            wq_all[part % 2, part // 2],
            preferred_element_type=jnp.float32,
        )
    query = query.astype(jnp.bfloat16)
    for head in range(heads):
        query_rows[head * token_count : (head + 1) * token_count, :] = query[
            :, head * head_dim : (head + 1) * head_dim
        ]

    cached = keys.shape[0] * page - token_count
    chunk = token_count
    chunks = cached // chunk
    scale = head_dim ** (-0.5) * math.log2(math.e)
    lanes = 128
    keys_turned[...] = (
        keys[...].reshape(-1, head_dim)[:cached].astype(jnp.float32).T.astype(jnp.bfloat16)
    )
    old_pos = lax.broadcasted_iota(jnp.int32, hidden_row.shape, 1)
    hidden_row[...] = jnp.where(old_pos < length, 0.0, NEGATIVE)

    def attend(q):
        running = None
        for c in range(chunks + 1):
            if c < chunks:
                part = jnp.dot(
                    q,
                    keys_turned[:, c * chunk : (c + 1) * chunk],
                    preferred_element_type=jnp.float32,
                )
                part = part * scale + hidden_row[:1, c * chunk : (c + 1) * chunk]
            else:
                part = jnp.dot(
                    q,
                    new_kv[...].reshape(2 * head_dim, token_count)[:head_dim],
                    preferred_element_type=jnp.float32,
                )
                row = lax.broadcasted_iota(jnp.int32, part.shape, 0) % token_count
                col = lax.broadcasted_iota(jnp.int32, part.shape, 1)
                part = jnp.where(col <= row, part * scale, NEGATIVE)
            scores[c] = part
            for first in range(0, chunk, lanes):
                piece = part[:, first : first + lanes]
                running = piece if running is None else jnp.maximum(running, piece)
        top = jnp.max(running, axis=1, keepdims=True)
        total = jnp.zeros((q.shape[0], lanes), jnp.float32)
        summed = jnp.zeros((q.shape[0], head_dim), jnp.float32)
        for c in range(chunks + 1):
            probs = jnp.exp2(scores[c] - top)
            for first in range(0, chunk, lanes):
                total += probs[:, first : first + lanes]
            if c < chunks:
                summed += jnp.dot(
                    probs.astype(jnp.bfloat16),
                    values[...].reshape(-1, head_dim)[c * chunk : (c + 1) * chunk],
                    preferred_element_type=jnp.float32,
                )
            else:
                summed += lax.dot_general(
                    probs.astype(jnp.bfloat16),
                    new_kv[...].reshape(2 * head_dim, token_count)[head_dim:],
                    (((1,), (1,)), ((), ())),
                    preferred_element_type=jnp.float32,
                )
        return (summed / jnp.sum(total, axis=1, keepdims=True)).astype(jnp.bfloat16)

    for head in range(heads):
        head_rows = slice(head * token_count, (head + 1) * token_count)
        attended[head_rows, :] = attend(query_rows[head_rows, :])
        if head == 0:
            z_forward(3, 1)
            z_forward(4, 1)

    own_rows = hidden_ref.shape[0]
    result_rows = jnp.concatenate(
        [attended[head * token_count : (head + 1) * token_count, :] for head in range(heads)],
        axis=1,
    )

    def sib_copy(n):
        return pltpu.make_async_remote_copy(
            src_ref=sibling_out.at[n],
            dst_ref=sibling_in.at[n],
            send_sem=sib_send.at[n],
            recv_sem=sib_recv.at[n],
            device_id={"gx": sibling},
            device_id_type=MESH,
        )

    def chip_copy(n, flip):
        return pltpu.make_async_remote_copy(
            src_ref=chip_out.at[n, flip],
            dst_ref=chip_in.at[n, flip],
            send_sem=chip_send.at[n, flip],
            recv_sem=chip_recv.at[n, flip],
            device_id={"gx": peers[flip]},
            device_id_type=MESH,
        )

    def project(n):
        partial[n] = jnp.dot(
            result_rows, wo_all[n % 2, order[n // 2]], preferred_element_type=jnp.float32
        ).reshape(2 * CHIPS, own_rows, half_width)
        for k in range(CHIPS):
            sibling_out[n, k] = partial[n, 2 * k + 1 - core].astype(jnp.bfloat16)
        sib_copy(n).start()

    def spread_sums(n):
        sib_copy(n).wait_recv()
        for flip in range(FLIPS):
            other = other_chips[flip]
            chip_out[n, flip] = (
                partial[n, 2 * other + core] + sibling_in[n, other].astype(jnp.float32)
            ).astype(jnp.bfloat16)
            chip_copy(n, flip).start()
        own_sum[n] = partial[n, me] + sibling_in[n, chip].astype(jnp.float32)

    low = z < planes // 2
    order = [z, jnp.where(low, z + 1, z - 1)]
    order.append(jnp.where(low, (z + planes - 1) % planes, (z + 1) % planes))
    order[2] = jnp.where((z == 0) | (z == planes - 1), jnp.where(low, 2, planes - 3), order[2])
    order.append(jnp.where(low, planes - 1, 0))

    slices = 2 * planes
    for n in range(slices):
        step = n // 2 - 1
        if n < 2:
            loads[8 + n].wait()
        else:
            z_last(3 + n % 2, step)
        if n >= 2 and step + 1 == 1:
            z_forward(3 + n % 2, 2)
        project(n)
        if n > 0:
            spread_sums(n - 1)
    spread_sums(slices - 1)
    for n in range(slices):
        total = own_sum[n]
        for flip in range(FLIPS):
            chip_copy(n, flip).wait_recv()
            total += chip_in[n, flip].astype(jnp.float32)
        column = pl.multiple_of(order[n // 2] * 2 * half_width + n % 2 * half_width, half_width)
        out_ref[:, pl.ds(column, half_width)] = total.astype(jnp.bfloat16)

    for kind in range(5):
        for step in range(planes - 1):
            z_wait_send(kind, step)
    for kind in range(3):
        first, second = across(kind)
        for slot, target in enumerate((peers[0], peers[1], sibling)):
            row_copy(kind, me, target, slot).wait_send()
        row_copy(kind, peers[first], peers[second], 3).wait_send()
        for slot, flip in enumerate((first, second, 2)):
            row_copy(kind, peers[flip], sibling, 4 + slot).wait_send()
    for slot, target in enumerate(everyone):
        kv_copy(me, target, slot).wait_send()
    for n in range(slices):
        sib_copy(n).wait_send()
        for flip in range(FLIPS):
            chip_copy(n, flip).wait_send()


def hand_over(out_ref, key_ref, value_ref, out_to, key_to, value_to):
    out_to[0] = out_ref[...]
    key_to[0] = key_ref[...]
    value_to[0] = value_ref[...]


def fused(
    groups,
    planes,
    hidden_states,
    norm_gain,
    norm_bias,
    query_weight,
    keyvalue_weight,
    out_weight,
    key_cache,
    value_cache,
    cache_length,
):
    own_rows, model = hidden_states.shape[1:]
    page, head_dim = key_cache.shape[1:]
    span = own_rows * groups
    depth, columns = query_weight.shape
    kv_width = keyvalue_weight.shape[1]
    out_rows, width = out_weight.shape
    heads = columns // head_dim
    bf16, f32 = jnp.bfloat16, jnp.float32
    vmem = pl.BlockSpec(memory_space=pltpu.VMEM)
    hbm = pl.BlockSpec(memory_space=pltpu.HBM)
    dma = pltpu.SemaphoreType.DMA
    out, new_key, new_value = pl.pallas_call(
        functools.partial(fused_kernel, planes),
        out_shape=(
            jax.ShapeDtypeStruct((own_rows, model), bf16),
            jax.ShapeDtypeStruct((page, head_dim), bf16),
            jax.ShapeDtypeStruct((page, head_dim), bf16),
        ),
        in_specs=[hbm] * 8 + [pl.BlockSpec(memory_space=pltpu.SMEM)],
        out_specs=(vmem, vmem, vmem),
        scratch_shapes=[
            pltpu.VMEM((own_rows, model), bf16),
            pltpu.VMEM((1, model), f32),
            pltpu.VMEM((1, model), f32),
            pltpu.VMEM((groups, own_rows, model), bf16),
            pltpu.VMEM((2, planes, depth // 2, columns), bf16),
            pltpu.VMEM((planes, kv_width, depth), bf16),
            pltpu.VMEM((2, planes, out_rows, width // 2), bf16),
            pltpu.VMEM((groups, page, head_dim), bf16),
            pltpu.VMEM((groups, page, head_dim), bf16),
            pltpu.VMEM((groups, kv_width, span), bf16),
            pltpu.VMEM((heads * span, head_dim), bf16),
            pltpu.VMEM((heads * span, head_dim), bf16),
            pltpu.VMEM((head_dim, groups * page - span), bf16),
            pltpu.VMEM((8, groups * page - span), f32),
            pltpu.VMEM((groups * page // span, span, span), f32),
            pltpu.VMEM((2 * planes, 2 * CHIPS, own_rows, width // 2), f32),
            pltpu.VMEM((2 * planes, CHIPS, own_rows, width // 2), bf16),
            pltpu.VMEM((2 * planes, CHIPS, own_rows, width // 2), bf16),
            pltpu.VMEM((2 * planes, FLIPS, own_rows, width // 2), bf16),
            pltpu.VMEM((2 * planes, FLIPS, own_rows, width // 2), bf16),
            pltpu.VMEM((2 * planes, own_rows, width // 2), f32),
            dma((10,)),
            dma((5, planes - 1, 2)),
            dma((5, planes)),
            dma((3, 4 + FLIPS)),
            dma((3, groups)),
            dma((groups - 1,)),
            dma((groups,)),
            dma((2 * planes,)),
            dma((2 * planes,)),
            dma((2 * planes, FLIPS)),
            dma((2 * planes, FLIPS)),
        ],
        compiler_params=pltpu.CompilerParams(
            collective_id=0, has_side_effects=True, vmem_limit_bytes=64 * 1024 * 1024
        ),
        cost_estimate=pl.CostEstimate(
            flops=10**9, bytes_accessed=2 * 10**6, transcendentals=10**6
        ),
        name="attention_layer",
    )(
        hidden_states[0],
        norm_gain[None],
        norm_bias[None],
        query_weight,
        keyvalue_weight.T,
        out_weight,
        key_cache[0],
        value_cache[0],
        cache_length,
    )
    results = pl.pallas_call(
        hand_over,
        out_shape=tuple(
            jax.ShapeDtypeStruct((1,) + result.shape, bf16) for result in (out, new_key, new_value)
        ),
        in_specs=[vmem] * 3,
        out_specs=(vmem,) * 3,
        compiler_params=pltpu.CompilerParams(vmem_limit_bytes=64 * 1024 * 1024),
        name="hand_over",
    )(out, new_key, new_value)
    return tuple(results)


def device_program(mesh, *args):
    groups, planes = mesh.shape["gx"], mesh.shape["gy"]
    if groups == 2 * CHIPS and planes == 4:
        return fused(groups, planes, *args)
    return body(*args)


def solution(mesh):
    return jax.shard_map(
        functools.partial(device_program, mesh),
        mesh=mesh,
        in_specs=(
            P("gy", "gx", None),
            P(),
            P(),
            P("gy", "gx"),
            P("gy", "gx"),
            P("gx", "gy"),
            P("gy", "gx", None),
            P("gy", "gx", None),
            P("gy"),
        ),
        out_specs=(P("gy", "gx", None), P("gy", "gx", None), P("gy", "gx", None)),
        check_vma=False,
    )
```

```python
import functools
import math

import jax
import jax.numpy as jnp
from jax import lax
from jax.experimental import pallas as pl
from jax.experimental.pallas import tpu as pltpu
from jax.sharding import PartitionSpec as P

HEADS = 16


NEGATIVE = -1e30


def normalize(hidden_states, norm_gain, norm_bias):
    values = hidden_states.astype(jnp.float32)
    average = jnp.mean(values, axis=-1, keepdims=True)
    centred = values - average
    spread = jnp.mean(centred * centred, axis=-1, keepdims=True)
    return (centred * lax.rsqrt(spread + 1e-05) * norm_gain + norm_bias).astype(jnp.bfloat16)


def page_terms(query_rows, query_pos, key_rows, value_rows, page_size):
    row_count = query_rows.shape[0]
    head_dim = key_rows.shape[1]
    page_count = key_rows.shape[0] // page_size
    scores = lax.dot_general(
        query_rows, key_rows, (((1,), (1,)), ((), ())), preferred_element_type=jnp.float32
    )
    scores = (scores * head_dim ** (-0.5)).reshape(row_count, page_count, page_size)
    key_pos = jnp.arange(page_count * page_size, dtype=jnp.int32).reshape(page_count, page_size)
    allowed = key_pos[None, :, :] <= query_pos[:, None, None]
    maxima = jnp.max(jnp.where(allowed, scores, NEGATIVE), axis=2)
    weights = jnp.where(allowed, jnp.exp(scores - maxima[:, :, None]), 0.0)
    totals = jnp.sum(weights, axis=2)
    weighted = jnp.einsum(
        "rnp,npd->rnd",
        weights.astype(jnp.bfloat16),
        value_rows.reshape(page_count, page_size, head_dim),
        preferred_element_type=jnp.float32,
    )
    return (maxima, totals, weighted)


def reduce_pages(maxima, totals, weighted):
    largest = jnp.max(maxima, axis=1)
    factor = jnp.exp(maxima - largest[:, None])
    return (
        largest,
        jnp.sum(totals * factor, axis=1),
        jnp.sum(weighted * factor[:, :, None], axis=1),
    )


def join_pages(first, second):
    larger = jnp.maximum(first[0], second[0])
    second_factor = jnp.exp(second[0] - larger)
    return (larger, second[1] * second_factor, second[2] * second_factor[:, None])


def body(
    hidden_states,
    norm_gain,
    norm_bias,
    query_weight,
    keyvalue_weight,
    out_weight,
    key_cache,
    value_cache,
    cache_length,
):
    own_tokens = hidden_states.shape[1]
    groups = lax.axis_size("gx")
    column_index = lax.axis_index("gx")
    span_len = own_tokens * groups
    page_size = key_cache.shape[1]
    head_dim = key_cache.shape[2]
    head_count = HEADS
    head_width = head_count * head_dim
    normed = normalize(hidden_states[0], norm_gain, norm_bias)
    full_rows = lax.all_gather(normed, "gx", axis=0, tiled=True)
    pieces = (
        lax.all_gather(query_weight, "gy", axis=0, tiled=True),
        lax.all_gather(keyvalue_weight, "gy", axis=0, tiled=True),
    )
    query_part = jnp.dot(full_rows, pieces[0], preferred_element_type=jnp.float32)
    keyvalue_part = jnp.dot(full_rows, pieces[1], preferred_element_type=jnp.float32)
    query_local = query_part.astype(jnp.bfloat16)
    keyvalue_local = keyvalue_part.astype(jnp.bfloat16)
    queries, new_keyvalue = (
        lax.all_gather(query_local, "gx", axis=1, tiled=True),
        lax.all_gather(keyvalue_local, "gx", axis=1, tiled=True),
    )
    length = cache_length[0]
    page_base = column_index * page_size
    offsets = page_base + jnp.arange(page_size, dtype=jnp.int32) - length
    inside = (offsets >= 0) & (offsets < span_len)
    picked = jnp.take(new_keyvalue, jnp.clip(offsets, 0, span_len - 1), axis=0)
    key_page = jnp.where(inside[:, None], picked[:, :head_dim], key_cache[0])
    value_page = jnp.where(inside[:, None], picked[:, head_dim:], value_cache[0])
    own_rows = lax.dynamic_slice_in_dim(queries, column_index * own_tokens, own_tokens, 0)
    own_rows = own_rows.reshape(own_tokens * head_count, head_dim)
    own_pos = (
        length
        + column_index * own_tokens
        + jnp.arange(own_tokens * head_count, dtype=jnp.int32) // head_count
    )
    own_total = own_tokens * head_count
    empty = (
        jnp.full((own_total,), NEGATIVE, jnp.float32),
        jnp.zeros((own_total,), jnp.float32),
        jnp.zeros((own_total, head_dim), jnp.float32),
    )
    pieces = (
        lax.all_gather(key_page, "gx", axis=0, tiled=True),
        lax.all_gather(value_page, "gx", axis=0, tiled=True),
    )
    maxima, totals, weighted = page_terms(own_rows, own_pos, pieces[0], pieces[1], page_size)
    maxima, totals, weighted = join_pages(empty, reduce_pages(maxima, totals, weighted))
    own_out = (weighted / totals[:, None]).reshape(own_tokens, head_width).astype(jnp.bfloat16)
    attended = lax.all_to_all(own_out, "gx", split_axis=1, concat_axis=0, tiled=True)
    out_full = lax.all_gather(out_weight, "gy", axis=1, tiled=True)
    hidden_part = lax.psum_scatter(
        jnp.dot(attended, out_full, preferred_element_type=jnp.float32),
        "gx",
        scatter_dimension=0,
        tiled=True,
    )
    return (hidden_part.astype(jnp.bfloat16)[None], key_page[None], value_page[None])


MESH = pl.DeviceIdType.MESH
CHIPS = 4
FLIPS = 3


def fused_kernel(
    planes,
    hidden_ref,
    gain_ref,
    bias_ref,
    wq_ref,
    wkv_ref,
    wo_ref,
    key_ref,
    value_ref,
    length_ref,
    out_ref,
    new_key_ref,
    new_value_ref,
    hidden_in,
    gain_in,
    bias_in,
    normed,
    wq_all,
    wkv_all,
    wo_all,
    keys,
    values,
    new_kv,
    query_rows,
    attended,
    keys_turned,
    hidden_row,
    scores,
    partial,
    sibling_out,
    sibling_in,
    chip_out,
    chip_in,
    own_sum,
    load_sem,
    z_send,
    z_recv,
    rows_send,
    rows_recv,
    kv_send,
    kv_recv,
    sib_send,
    sib_recv,
    chip_send,
    chip_recv,
):
    me = lax.axis_index("gx")
    z = lax.axis_index("gy")
    core = me % 2
    chip = me // 2
    cx = chip % 2
    cy = chip // 2
    sibling = chip * 2 + 1 - core
    other_chips = (cy * 2 + 1 - cx, (1 - cy) * 2 + cx, (1 - cy) * 2 + 1 - cx)
    peers = [other * 2 + core for other in other_chips]
    far = [other * 2 + 1 - core for other in other_chips]
    everyone = [sibling] + peers + far
    has_up = z < planes - 1
    has_down = z > 0

    barrier = pltpu.get_barrier_semaphore()
    for peer in everyone:
        pl.semaphore_signal(barrier, inc=1, device_id={"gx": peer}, device_id_type=MESH)

    @pl.when(has_up)
    def _():
        pl.semaphore_signal(barrier, inc=1, device_id={"gy": z + 1}, device_id_type=MESH)

    @pl.when(has_down)
    def _():
        pl.semaphore_signal(barrier, inc=1, device_id={"gy": z - 1}, device_id_type=MESH)

    half_depth = wq_all.shape[2]
    half_width = wo_all.shape[3]
    half_rows = [wq_ref.at[pl.ds(half * half_depth, half_depth)] for half in range(2)]
    half_cols = [wo_ref.at[:, pl.ds(half * half_width, half_width)] for half in range(2)]
    sources = [wkv_ref] + half_rows + half_cols
    buffers = [wkv_all, wq_all.at[0], wq_all.at[1], wo_all.at[0], wo_all.at[1]]
    loads = [
        pltpu.make_async_copy(source, target, load_sem.at[slot])
        for slot, (source, target) in enumerate(
            [
                (hidden_ref, hidden_in),
                (gain_ref, gain_in),
                (bias_ref, bias_in),
                (key_ref, keys.at[me]),
                (value_ref, values.at[me]),
            ]
            + [(source, buffer.at[z]) for source, buffer in zip(sources, buffers)]
        )
    ]
    for load in loads:
        load.start()

    neighbours = has_up.astype(jnp.int32) + has_down.astype(jnp.int32)
    pl.semaphore_wait(barrier, len(everyone) + neighbours)

    def z_copy(kind, step, direction):
        shard = z - direction * step
        buffer = buffers[kind]
        return pltpu.make_async_remote_copy(
            src_ref=sources[kind] if step == 0 else buffer.at[shard],
            dst_ref=buffer.at[shard],
            send_sem=z_send.at[kind, step, (direction + 1) // 2],
            recv_sem=z_recv.at[kind, shard],
            device_id={"gy": z + direction},
            device_id_type=MESH,
        )

    def z_cond(step, direction):
        if direction > 0:
            return has_up & (z - step >= 0)
        return has_down & (z + step < planes)

    def z_arrived(kind, shard):
        buffer = buffers[kind]
        pltpu.make_async_copy(buffer.at[shard], buffer.at[shard], z_recv.at[kind, shard]).wait()

    def z_forward(kind, step):
        for direction in (1, -1):

            @pl.when(z_cond(step, direction))
            def _(direction=direction):
                if step > 0:
                    z_arrived(kind, z - direction * step)
                z_copy(kind, step, direction).start()

    def z_wait_send(kind, step):
        for direction in (1, -1):

            @pl.when(z_cond(step, direction))
            def _(direction=direction):
                z_copy(kind, step, direction).wait_send()

    def z_last(kind, step):
        @pl.when((z == planes - 1) & (z - 1 - step >= 0))
        def _():
            z_arrived(kind, z - 1 - step)

        @pl.when((z == 0) & (z + 1 + step < planes))
        def _():
            z_arrived(kind, z + 1 + step)

    def out_start(step):
        for direction in (1, -1):
            last = z if direction > 0 else planes - 1 - z

            @pl.when(z_cond(0, direction) & (last == step))
            def _(direction=direction):
                z_copy(3, 0, direction).start()
                z_copy(4, 0, direction).start()

    gathered = (normed, keys, values)

    def row_copy(kind, block, target, slot):
        return pltpu.make_async_remote_copy(
            src_ref=gathered[kind].at[block],
            dst_ref=gathered[kind].at[block],
            send_sem=rows_send.at[kind, slot],
            recv_sem=rows_recv.at[kind, block],
            device_id={"gx": target},
            device_id_type=MESH,
        )

    def rows_start(kind):
        for slot, target in enumerate(peers + [sibling]):
            row_copy(kind, me, target, slot).start()

    def rows_wait(kind, block):
        pltpu.make_async_copy(
            gathered[kind].at[block], gathered[kind].at[block], rows_recv.at[kind, block]
        ).wait()

    def rows_forward(kind):
        for flip in range(FLIPS):
            rows_wait(kind, peers[flip])
            row_copy(kind, peers[flip], sibling, 4 + flip).start()

    def rows_finish(kind):
        for block in [sibling] + far:
            rows_wait(kind, block)

    for kind in range(3):
        z_forward(kind, 0)
    out_start(0)

    loads[3].wait()
    rows_start(1)
    for slot in range(3):
        loads[slot].wait()
    rows = hidden_in[...].astype(jnp.float32)
    average = jnp.mean(rows, axis=-1, keepdims=True)
    centred = rows - average
    spread = jnp.mean(centred * centred, axis=-1, keepdims=True)
    normed[me] = (
        centred * lax.rsqrt(spread + 1e-05) * gain_in[...] + bias_in[...]
    ).astype(jnp.bfloat16)
    rows_start(0)
    loads[4].wait()
    rows_start(2)

    z_forward(0, 1)
    z_forward(0, 2)
    z_forward(1, 1)
    rows_forward(0)
    z_forward(2, 1)
    out_start(1)
    rows_finish(0)
    loads[5].wait()
    for step in range(planes - 1):
        z_last(0, step)

    tokens = normed[...].reshape(-1, normed.shape[2])
    token_count = tokens.shape[0]
    depth = 2 * half_depth
    kv_width = wkv_all.shape[1]
    kv_part = jnp.zeros((kv_width, token_count), jnp.float32)
    for part in range(planes):
        kv_part += lax.dot_general(
            wkv_all[part],
            tokens[:, part * depth : (part + 1) * depth],
            (((1,), (1,)), ((), ())),
            preferred_element_type=jnp.float32,
        )
    new_kv[me] = kv_part.astype(jnp.bfloat16)

    def kv_copy(block, target, slot):
        return pltpu.make_async_remote_copy(
            src_ref=new_kv.at[block],
            dst_ref=new_kv.at[block],
            send_sem=kv_send.at[slot],
            recv_sem=kv_recv.at[block],
            device_id={"gx": target},
            device_id_type=MESH,
        )

    for slot, target in enumerate(everyone):
        kv_copy(me, target, slot).start()

    z_forward(1, 2)
    z_forward(2, 2)
    out_start(2)
    rows_forward(1)
    rows_forward(2)

    for block in everyone:
        pltpu.make_async_copy(new_kv.at[block], new_kv.at[block], kv_recv.at[block]).wait()

    length = length_ref[0]
    page = key_ref.shape[0]
    head_dim = key_ref.shape[1]
    kv_cols = new_kv[...].reshape(2 * head_dim, token_count)
    offsets = (
        lax.broadcasted_iota(jnp.int32, (page, token_count), 0) + me * page - length
    )
    chosen = offsets == lax.broadcasted_iota(jnp.int32, (page, token_count), 1)
    picked = lax.dot_general(
        jnp.where(chosen, 1.0, 0.0).astype(jnp.bfloat16),
        kv_cols,
        (((1,), (1,)), ((), ())),
        preferred_element_type=jnp.float32,
    )
    row_offset = lax.broadcasted_iota(jnp.int32, (page, head_dim), 0) + me * page - length
    inside = (row_offset >= 0) & (row_offset < token_count)
    new_key_ref[...] = jnp.where(
        inside, picked[:, :head_dim], keys[me].astype(jnp.float32)
    ).astype(jnp.bfloat16)
    new_value_ref[...] = jnp.where(
        inside, picked[:, head_dim:], values[me].astype(jnp.float32)
    ).astype(jnp.bfloat16)

    rows_finish(1)
    rows_finish(2)
    for half in range(2):
        loads[6 + half].wait()
        for step in range(planes - 1):
            z_last(1 + half, step)

    heads = wq_all.shape[3] // head_dim
    query = jnp.zeros((token_count, heads * head_dim), jnp.float32)
    for part in range(2 * planes):
        query += jnp.dot(
            normed[:, :, part * half_depth : (part + 1) * half_depth].reshape(
                token_count, half_depth
            ),
            wq_all[part % 2, part // 2],
            preferred_element_type=jnp.float32,
        )
    query = query.astype(jnp.bfloat16)
    for head in range(heads):
        query_rows[head * token_count : (head + 1) * token_count, :] = query[
            :, head * head_dim : (head + 1) * head_dim
        ]

    cached = keys.shape[0] * page - token_count
    chunk = token_count
    chunks = cached // chunk
    scale = head_dim ** (-0.5) * math.log2(math.e)
    lanes = 128
    keys_turned[...] = (
        keys[...].reshape(-1, head_dim)[:cached].astype(jnp.float32).T.astype(jnp.bfloat16)
    )
    old_pos = lax.broadcasted_iota(jnp.int32, hidden_row.shape, 1)
    hidden_row[...] = jnp.where(old_pos < length, 0.0, NEGATIVE)

    def attend(q):
        running = None
        for c in range(chunks + 1):
            if c < chunks:
                part = jnp.dot(
                    q,
                    keys_turned[:, c * chunk : (c + 1) * chunk],
                    preferred_element_type=jnp.float32,
                )
                part = part * scale + hidden_row[:1, c * chunk : (c + 1) * chunk]
            else:
                part = jnp.dot(
                    q,
                    new_kv[...].reshape(2 * head_dim, token_count)[:head_dim],
                    preferred_element_type=jnp.float32,
                )
                row = lax.broadcasted_iota(jnp.int32, part.shape, 0) % token_count
                col = lax.broadcasted_iota(jnp.int32, part.shape, 1)
                part = jnp.where(col <= row, part * scale, NEGATIVE)
            scores[c] = part
            for first in range(0, chunk, lanes):
                piece = part[:, first : first + lanes]
                running = piece if running is None else jnp.maximum(running, piece)
        top = jnp.max(running, axis=1, keepdims=True)
        total = jnp.zeros((q.shape[0], lanes), jnp.float32)
        summed = jnp.zeros((q.shape[0], head_dim), jnp.float32)
        for c in range(chunks + 1):
            probs = jnp.exp2(scores[c] - top)
            for first in range(0, chunk, lanes):
                total += probs[:, first : first + lanes]
            if c < chunks:
                summed += jnp.dot(
                    probs.astype(jnp.bfloat16),
                    values[...].reshape(-1, head_dim)[c * chunk : (c + 1) * chunk],
                    preferred_element_type=jnp.float32,
                )
            else:
                summed += lax.dot_general(
                    probs.astype(jnp.bfloat16),
                    new_kv[...].reshape(2 * head_dim, token_count)[head_dim:],
                    (((1,), (1,)), ((), ())),
                    preferred_element_type=jnp.float32,
                )
        return (summed / jnp.sum(total, axis=1, keepdims=True)).astype(jnp.bfloat16)

    for head in range(heads):
        head_rows = slice(head * token_count, (head + 1) * token_count)
        attended[head_rows, :] = attend(query_rows[head_rows, :])
        if head == 0:
            z_forward(3, 1)
            z_forward(4, 1)

    own_rows = hidden_ref.shape[0]
    result_rows = jnp.concatenate(
        [attended[head * token_count : (head + 1) * token_count, :] for head in range(heads)],
        axis=1,
    )

    def sib_copy(n):
        return pltpu.make_async_remote_copy(
            src_ref=sibling_out.at[n],
            dst_ref=sibling_in.at[n],
            send_sem=sib_send.at[n],
            recv_sem=sib_recv.at[n],
            device_id={"gx": sibling},
            device_id_type=MESH,
        )

    def chip_copy(n, flip):
        return pltpu.make_async_remote_copy(
            src_ref=chip_out.at[n, flip],
            dst_ref=chip_in.at[n, flip],
            send_sem=chip_send.at[n, flip],
            recv_sem=chip_recv.at[n, flip],
            device_id={"gx": peers[flip]},
            device_id_type=MESH,
        )

    def project(n):
        partial[n] = jnp.dot(
            result_rows, wo_all[n % 2, order[n // 2]], preferred_element_type=jnp.float32
        ).reshape(2 * CHIPS, own_rows, half_width)
        for k in range(CHIPS):
            sibling_out[n, k] = partial[n, 2 * k + 1 - core].astype(jnp.bfloat16)
        sib_copy(n).start()

    def spread_sums(n):
        sib_copy(n).wait_recv()
        for flip in range(FLIPS):
            other = other_chips[flip]
            chip_out[n, flip] = (
                partial[n, 2 * other + core] + sibling_in[n, other].astype(jnp.float32)
            ).astype(jnp.bfloat16)
            chip_copy(n, flip).start()
        own_sum[n] = partial[n, me] + sibling_in[n, chip].astype(jnp.float32)

    low = z < planes // 2
    order = [z, jnp.where(low, z + 1, z - 1)]
    order.append(jnp.where(low, (z + planes - 1) % planes, (z + 1) % planes))
    order[2] = jnp.where((z == 0) | (z == planes - 1), jnp.where(low, 2, planes - 3), order[2])
    order.append(jnp.where(low, planes - 1, 0))

    slices = 2 * planes
    for n in range(slices):
        step = n // 2 - 1
        if n < 2:
            loads[8 + n].wait()
        else:
            z_last(3 + n % 2, step)
        if n >= 2 and step + 1 == 1:
            z_forward(3 + n % 2, 2)
        project(n)
        if n > 0:
            spread_sums(n - 1)
    spread_sums(slices - 1)
    for n in range(slices):
        total = own_sum[n]
        for flip in range(FLIPS):
            chip_copy(n, flip).wait_recv()
            total += chip_in[n, flip].astype(jnp.float32)
        column = pl.multiple_of(order[n // 2] * 2 * half_width + n % 2 * half_width, half_width)
        out_ref[:, pl.ds(column, half_width)] = total.astype(jnp.bfloat16)

    for kind in range(5):
        for step in range(planes - 1):
            z_wait_send(kind, step)
    for kind in range(3):
        for slot, target in enumerate(peers + [sibling]):
            row_copy(kind, me, target, slot).wait_send()
        for flip in range(FLIPS):
            row_copy(kind, peers[flip], sibling, 4 + flip).wait_send()
    for slot, target in enumerate(everyone):
        kv_copy(me, target, slot).wait_send()
    for n in range(slices):
        sib_copy(n).wait_send()
        for flip in range(FLIPS):
            chip_copy(n, flip).wait_send()


def hand_over(out_ref, key_ref, value_ref, out_to, key_to, value_to):
    out_to[0] = out_ref[...]
    key_to[0] = key_ref[...]
    value_to[0] = value_ref[...]


def fused(
    groups,
    planes,
    hidden_states,
    norm_gain,
    norm_bias,
    query_weight,
    keyvalue_weight,
    out_weight,
    key_cache,
    value_cache,
    cache_length,
):
    own_rows, model = hidden_states.shape[1:]
    page, head_dim = key_cache.shape[1:]
    span = own_rows * groups
    depth, columns = query_weight.shape
    kv_width = keyvalue_weight.shape[1]
    out_rows, width = out_weight.shape
    heads = columns // head_dim
    bf16, f32 = jnp.bfloat16, jnp.float32
    vmem = pl.BlockSpec(memory_space=pltpu.VMEM)
    hbm = pl.BlockSpec(memory_space=pltpu.HBM)
    dma = pltpu.SemaphoreType.DMA
    out, new_key, new_value = pl.pallas_call(
        functools.partial(fused_kernel, planes),
        out_shape=(
            jax.ShapeDtypeStruct((own_rows, model), bf16),
            jax.ShapeDtypeStruct((page, head_dim), bf16),
            jax.ShapeDtypeStruct((page, head_dim), bf16),
        ),
        in_specs=[hbm] * 8 + [pl.BlockSpec(memory_space=pltpu.SMEM)],
        out_specs=(vmem, vmem, vmem),
        scratch_shapes=[
            pltpu.VMEM((own_rows, model), bf16),
            pltpu.VMEM((1, model), f32),
            pltpu.VMEM((1, model), f32),
            pltpu.VMEM((groups, own_rows, model), bf16),
            pltpu.VMEM((2, planes, depth // 2, columns), bf16),
            pltpu.VMEM((planes, kv_width, depth), bf16),
            pltpu.VMEM((2, planes, out_rows, width // 2), bf16),
            pltpu.VMEM((groups, page, head_dim), bf16),
            pltpu.VMEM((groups, page, head_dim), bf16),
            pltpu.VMEM((groups, kv_width, span), bf16),
            pltpu.VMEM((heads * span, head_dim), bf16),
            pltpu.VMEM((heads * span, head_dim), bf16),
            pltpu.VMEM((head_dim, groups * page - span), bf16),
            pltpu.VMEM((8, groups * page - span), f32),
            pltpu.VMEM((groups * page // span, span, span), f32),
            pltpu.VMEM((2 * planes, 2 * CHIPS, own_rows, width // 2), f32),
            pltpu.VMEM((2 * planes, CHIPS, own_rows, width // 2), bf16),
            pltpu.VMEM((2 * planes, CHIPS, own_rows, width // 2), bf16),
            pltpu.VMEM((2 * planes, FLIPS, own_rows, width // 2), bf16),
            pltpu.VMEM((2 * planes, FLIPS, own_rows, width // 2), bf16),
            pltpu.VMEM((2 * planes, own_rows, width // 2), f32),
            dma((10,)),
            dma((5, planes - 1, 2)),
            dma((5, planes)),
            dma((3, 4 + FLIPS)),
            dma((3, groups)),
            dma((groups - 1,)),
            dma((groups,)),
            dma((2 * planes,)),
            dma((2 * planes,)),
            dma((2 * planes, FLIPS)),
            dma((2 * planes, FLIPS)),
        ],
        compiler_params=pltpu.CompilerParams(
            collective_id=0, has_side_effects=True, vmem_limit_bytes=64 * 1024 * 1024
        ),
        cost_estimate=pl.CostEstimate(
            flops=10**9, bytes_accessed=2 * 10**6, transcendentals=10**6
        ),
        name="attention_layer",
    )(
        hidden_states[0],
        norm_gain[None],
        norm_bias[None],
        query_weight,
        keyvalue_weight.T,
        out_weight,
        key_cache[0],
        value_cache[0],
        cache_length,
    )
    results = pl.pallas_call(
        hand_over,
        out_shape=tuple(
            jax.ShapeDtypeStruct((1,) + result.shape, bf16) for result in (out, new_key, new_value)
        ),
        in_specs=[vmem] * 3,
        out_specs=(vmem,) * 3,
        compiler_params=pltpu.CompilerParams(vmem_limit_bytes=64 * 1024 * 1024),
        name="hand_over",
    )(out, new_key, new_value)
    return tuple(results)


def device_program(mesh, *args):
    groups, planes = mesh.shape["gx"], mesh.shape["gy"]
    if groups == 2 * CHIPS and planes == 4:
        return fused(groups, planes, *args)
    return body(*args)


def solution(mesh):
    return jax.shard_map(
        functools.partial(device_program, mesh),
        mesh=mesh,
        in_specs=(
            P("gy", "gx", None),
            P(),
            P(),
            P("gy", "gx"),
            P("gy", "gx"),
            P("gx", "gy"),
            P("gy", "gx", None),
            P("gy", "gx", None),
            P("gy"),
        ),
        out_specs=(P("gy", "gx", None), P("gy", "gx", None), P("gy", "gx", None)),
        check_vma=False,
    )
```
